32 devices in a mesh: dp: 8 (over z, y), tensor: 4 (over x, core).
Axes of the slice: x: 2, y: 2, z: 4, core: 2. Of those that a mesh axis runs over, the one named last changes fastest.
Arguments:
- tokens: bfloat16 [16384, 1120], P(('dp', 'tensor')), may hold values from -6 to 6
- cotangent: bfloat16 [16384, 1120], P(('dp', 'tensor')), may hold values from -6 to 6
- ln1_gain: float32 [1120], replicated, may hold values from 0.5 to 1.5
- ln1_bias: float32 [1120], replicated, may hold values from -1.25 to 1.25
- attn_weight: bfloat16 [1120, 3, 1120], P(None, None, 'tensor'), may hold values from -0.1875 to 0.1875
- qv_bias: float32 [2, 1120], P(None, 'tensor'), may hold values from -1.75 to 1.75
- out_weight: bfloat16 [1120, 1120], P('tensor'), may hold values from -0.75 to 0.75
- out_bias: float32 [1120], replicated, may hold values from -1.25 to 1.25
- ln2_gain: float32 [1120], replicated, may hold values from 0.5 to 1.5
- ln2_bias: float32 [1120], replicated, may hold values from -1.25 to 1.25
- up_weight: bfloat16 [1120, 4480], P(None, 'tensor'), may hold values from -0.1875 to 0.1875
- up_bias: float32 [4480], P('tensor'), may hold values from -1.75 to 1.75
- down_weight: bfloat16 [4480, 1120], P('tensor'), may hold values from -0.09375 to 0.09375
- down_bias: float32 [1120], replicated, may hold values from -1.25 to 1.25
- cell_lengths: int32 [8, 11], P('dp'), may hold values from 0 to 1000, as said below
- cell_offsets: int32 [8, 11], P('dp'), may hold values from 0 to 2048, as said below
Outputs:
- layer_out: bfloat16 [16384, 1120], P(('dp', 'tensor'))
- input_grad: bfloat16 [16384, 1120], P(('dp', 'tensor'))
- ln1_gain_grad: float32 [1120], replicated
- ln1_bias_grad: float32 [1120], replicated
- attn_weight_grad: float32 [1120, 3, 1120], P(None, None, 'tensor')
- qv_bias_grad: float32 [2, 1120], P(None, 'tensor')
- out_weight_grad: float32 [1120, 1120], P('tensor')
- out_bias_grad: float32 [1120], replicated
- ln2_gain_grad: float32 [1120], replicated
- ln2_bias_grad: float32 [1120], replicated
- up_weight_grad: float32 [1120, 4480], P(None, 'tensor')
- up_bias_grad: float32 [4480], P('tensor')
- down_weight_grad: float32 [4480, 1120], P('tensor')
- down_bias_grad: float32 [1120], replicated
The draws below stay inside these ranges and needn't reach their ends.
Inputs may be any that keep to these rules, and one draw needn't show every extreme that they name: `cell_lengths`: in each index of dp the cells are laid out slot by slot in increasing order with gaps of padding; a length 0 marks an empty slot, all later slots are empty too, and every index has an empty slot. Lengths of used slots lie between 200 and 1000, with a heavy tail. `cell_offsets`: A used slot's cell covers slots offset to offset + length - 1 of its index, after the previous cell's end; empty slots have offset 2048.
All inputs are finite; a program needn't handle non-finite values.
Results may differ from the reference program's by a relative error of at most 0.015.
Values may be sent and summed in bfloat16 or wider, within the bound.
No kernel may reach another device: no remote copies, remote signals or barrier semaphores. Data moves between devices by JAX's collectives and lax.ppermute only.
A program may use at most 192 MiB of HBM per device.

```python
import jax
import jax.numpy as jnp
from jax import lax

D = 1120
HEAD_DIM = 56
FF = 4480
TOK_DEV = 2048
MOST_LEN = 1000
LEAST_LEN = 200
CELLS = 11
TOKENS = 16384
N_DP = 8


def layout_cells(key):
    key_len = jax.random.fold_in(key, 11)
    key_pick = jax.random.fold_in(key, 12)
    key_gap = jax.random.fold_in(key, 13)
    level = jax.random.randint(key_len, (N_DP, CELLS), 0, 31)
    lengths = LEAST_LEN + level * level * level * (MOST_LEN - LEAST_LEN) // 27000
    chosen = jax.random.randint(key_pick, (), 0, N_DP)
    slots = jnp.arange(CELLS, dtype=jnp.int32)[None, :]
    groups = jnp.arange(N_DP, dtype=jnp.int32)[:, None]
    forced = (groups == chosen) & (slots == 0)
    lengths = jnp.where(forced, MOST_LEN, lengths)
    gaps = jax.random.randint(key_gap, (N_DP, CELLS), 0, 17)
    gaps = jnp.where(forced, 0, gaps)
    ends = jnp.cumsum(gaps + lengths, axis=1)
    starts = ends - lengths
    fits = ends <= TOK_DEV
    fits = jnp.cumprod(fits.astype(jnp.int32), axis=1) > 0
    lengths = jnp.where(fits, lengths, 0).astype(jnp.int32)
    starts = jnp.where(fits, starts, TOK_DEV).astype(jnp.int32)
    return (lengths, starts)


def draw_cell_lengths(key, part):
    lengths, starts = layout_cells(key)
    return lengths


def draw_cell_offsets(key, part):
    lengths, starts = layout_cells(key)
    return starts


def steps_of(rng, extent, pieces, low, high):
    level, own = 1.0, jax.random.fold_in(rng, 6)
    for axis_at, parts in pieces:
        draws = jnp.exp(jax.random.uniform(jax.random.fold_in(own, axis_at), (parts,), jnp.float32, low / len(pieces), high / len(pieces)))
        level = level * jnp.repeat(draws, extent[axis_at] // parts).reshape([-1 if axis == axis_at else 1 for axis in range(len(extent))])
    return level


def normal_values(own_key, dims, width, limit, pieces=(), kind=jnp.bfloat16):
    values = width * jax.random.normal(own_key, dims, jnp.float32)
    if pieces:
        values = values * steps_of(own_key, dims, pieces, -0.22, 0.18)
    return jnp.clip(values, -limit, limit).astype(kind)


def setup_inputs(seed: int = 0) -> dict:
    key_of = jax.random.split(jax.random.key(seed), 17)
    tokens = normal_values(key_of[0], (TOKENS, D), 1.0, 6.0, ((0, 32),))
    cotangent = normal_values(key_of[1], (TOKENS, D), 1.0, 6.0, ((0, 32),))
    ln1_gain = jnp.clip(1.0 + 0.1 * jax.random.normal(key_of[2], (D,), jnp.float32), 0.5, 1.5)
    ln1_bias = normal_values(key_of[3], (D,), 0.2, 1.25, (), jnp.float32)
    attn_weight = normal_values(key_of[4], (D, 3, D), D ** -0.5, 0.1875, ((2, 4),))
    qv_bias = normal_values(key_of[5], (2, D), 0.3, 1.75, ((1, 4),), jnp.float32)
    out_weight = normal_values(key_of[6], (D, D), (D // 16) ** -0.5, 0.75, ((0, 4),))
    out_bias = normal_values(key_of[7], (D,), 0.2, 1.25, (), jnp.float32)
    ln2_gain = jnp.clip(1.0 + 0.1 * jax.random.normal(key_of[8], (D,), jnp.float32), 0.5, 1.5)
    ln2_bias = normal_values(key_of[9], (D,), 0.2, 1.25, (), jnp.float32)
    up_weight = normal_values(key_of[10], (D, FF), D ** -0.5, 0.1875, ((1, 4),))
    up_bias = normal_values(key_of[11], (FF,), 0.3, 1.75, ((0, 4),), jnp.float32)
    down_weight = normal_values(key_of[12], (FF, D), FF ** -0.5, 0.09375, ((0, 4),))
    down_bias = normal_values(key_of[13], (D,), 0.2, 1.25, (), jnp.float32)
    cell_lengths = draw_cell_lengths(jax.random.fold_in(key_of[16], 71), 0)
    cell_offsets = draw_cell_offsets(jax.random.fold_in(key_of[16], 71), 0)
    return dict(tokens=tokens, cotangent=cotangent, ln1_gain=ln1_gain, ln1_bias=ln1_bias, attn_weight=attn_weight, qv_bias=qv_bias, out_weight=out_weight, out_bias=out_bias, ln2_gain=ln2_gain, ln2_bias=ln2_bias, up_weight=up_weight, up_bias=up_bias, down_weight=down_weight, down_bias=down_bias, cell_lengths=cell_lengths, cell_offsets=cell_offsets)


big_negative = -1e+30
eps_norm = 1e-05

@jax.custom_vjp
def low(v):
    return lax.optimization_barrier(v.astype(jnp.bfloat16)).astype(jnp.float32)

@jax.custom_vjp
def low_back(v):
    return v

def low_keep(v):
    return (low(v), None)

def low_pass(kept, grad):
    return (grad,)

def back_keep(v):
    return (v, None)

def back_low(kept, grad):
    return (low(grad),)
low.defvjp(low_keep, low_pass)
low_back.defvjp(back_keep, back_low)

def layer_norm(values, gain, shift):
    center = values - lax.optimization_barrier(jnp.mean(values, axis=-1, keepdims=True))
    spread = lax.optimization_barrier(jnp.mean(center * center, axis=-1, keepdims=True))
    return center * lax.rsqrt(spread + eps_norm) * gain + shift

def group_layer(x_group, group_cells, weights):
    g_one, b_one, w_attn, qv_bias, w_out, b_out, g_two, b_two, w_up, b_up, w_down, b_down = weights
    high = lax.Precision.HIGHEST
    heads = D // HEAD_DIM
    scale = 1.0 / jnp.sqrt(jnp.float32(HEAD_DIM))
    h_one = low(layer_norm(x_group, g_one, b_one))
    mixed = jnp.einsum('td,dke->tke', h_one, w_attn, precision=high)
    query_rows = low(low_back(mixed[:, 0] + qv_bias[0])).reshape(TOK_DEV, heads, HEAD_DIM)
    key_rows = low(low_back(mixed[:, 1])).reshape(TOK_DEV, heads, HEAD_DIM)
    value_rows = low(low_back(mixed[:, 2] + qv_bias[1])).reshape(TOK_DEV, heads, HEAD_DIM)
    places = jnp.arange(TOK_DEV, dtype=jnp.int32)
    same = (group_cells[:, None] == group_cells[None, :]) & (group_cells[:, None] >= 0) & (places[None, :] < places[:, None])
    allowed = same | (places[None, :] == places[:, None])
    scores = jnp.einsum('qhe,khe->hqk', query_rows, key_rows, precision=high) * scale
    scores = low_back(jnp.where(allowed[None], scores, big_negative))
    highest = lax.optimization_barrier(jnp.max(scores, axis=-1, keepdims=True))
    expo = jnp.exp(scores - highest)
    probs = low(expo / lax.optimization_barrier(jnp.sum(expo, axis=-1, keepdims=True)))
    attended = jnp.einsum('hqk,khe->qhe', probs, value_rows, precision=high).reshape(TOK_DEV, D)
    attended = low(low_back(attended))
    branch = low_back(jnp.dot(attended, w_out, precision=high) + b_out)
    y_one = x_group + branch
    h_two = low(layer_norm(y_one, g_two, b_two))
    pre = low_back(jnp.dot(h_two, w_up, precision=high) + b_up)
    act = low(jax.nn.gelu(pre, approximate=True))
    mlp_out = low_back(jnp.dot(act, w_down, precision=high) + b_down)
    return y_one + mlp_out

def reference(tokens, cotangent, ln1_gain, ln1_bias, attn_weight, qv_bias, out_weight, out_bias, ln2_gain, ln2_bias, up_weight, up_bias, down_weight, down_bias, cell_lengths, cell_offsets):
    params = tuple((p.astype(jnp.float32) for p in (ln1_gain, ln1_bias, attn_weight, qv_bias, out_weight, out_bias, ln2_gain, ln2_bias, up_weight, up_bias, down_weight, down_bias)))
    places = jnp.arange(TOK_DEV, dtype=jnp.int32)[None, :, None]
    inside = (places >= cell_offsets[:, None, :]) & (places < cell_offsets[:, None, :] + cell_lengths[:, None, :])
    labels = jnp.arange(CELLS, dtype=jnp.int32)[None, None, :] + 1
    cells = (lax.optimization_barrier(jnp.sum(jnp.where(inside, labels, 0), axis=-1)) - 1).astype(jnp.int32)

    def forward(x_all, weights):

        def one_group(pair):
            return group_layer(pair[0], pair[1], weights)
        result = lax.map(jax.checkpoint(one_group), (x_all.reshape(N_DP, TOK_DEV, D), cells))
        return result.reshape(TOKENS, D)
    result, pullback = jax.vjp(forward, tokens.astype(jnp.float32), params)
    input_grad, grads = pullback(cotangent.astype(jnp.float32))
    return (result.astype(jnp.bfloat16), input_grad.astype(jnp.bfloat16), grads[0], grads[1], grads[2], grads[3], grads[4], grads[5], grads[6], grads[7], grads[8], grads[9], grads[10], grads[11])
```

```python
import functools
import math

import jax
import jax.numpy as jnp
from jax import lax
from jax.experimental import pallas as pl
from jax.experimental.pallas import tpu as pltpu
from jax.sharding import PartitionSpec as P


HEAD_DIM = 56
BLK = 256
SLOTS = 4
NEG = -1e30
EPS = 1e-05
SCALE = 1.0 / math.sqrt(HEAD_DIM)
SCALE2 = SCALE * math.log2(math.e)
GELU_C = math.sqrt(2.0 / math.pi)
GELU_A = 0.044715
F32 = jnp.float32
BF16 = jnp.bfloat16
NT = ((1,), (1,))
VMEM = 48 << 20


def dot(a, b, dims=((1,), (0,))):
    return lax.dot_general(a, b, (dims, ((), ())), preferred_element_type=F32)


def params():
    return pltpu.CompilerParams(vmem_limit_bytes=VMEM)


def cost(flops, nbytes, trans=0):
    return pl.CostEstimate(flops=int(flops), bytes_accessed=int(nbytes), transcendentals=int(trans))


def fold(v):
    total = v[:, :128]
    for at in range(128, v.shape[1], 128):
        total = total + v[:, at : at + 128]
    return total


def normal(x):
    center = x - jnp.mean(x, axis=0, keepdims=True)
    root = lax.rsqrt(jnp.mean(center * center, axis=0, keepdims=True) + EPS)
    return center * root, root


def qkv_kernel(heads, a_ref, b_ref, w_ref, vec_ref, bias_ref, *rest):
    x_out, h_out, q_out, kn_out, vn_out = rest[-5:]
    x = jnp.concatenate([a_ref[...], b_ref[...]], axis=1)
    x_out[...] = x
    n, _ = normal(x.astype(F32))
    h = (n * vec_ref[:, 0:1] + vec_ref[:, 1:2]).astype(BF16)
    h_out[...] = h
    width = heads * HEAD_DIM
    for part in range(3):
        r = dot(w_ref[part], h)
        if part != 1:
            r = r + bias_ref[part]
        r = r.astype(BF16)
        r = r.reshape(heads, HEAD_DIM, r.shape[1])
        q_out[part * heads : (part + 1) * heads] = r
        if part > 0:
            out = kn_out if part == 1 else vn_out
            for h_at in range(heads):
                out[h_at] = r[h_at].T


def qkv_call(pair, a, b, w, vec, bias, carry):
    d, rows = a.shape
    per = rows // BLK
    total = rows * SLOTS
    heads = w.shape[1] // HEAD_DIM
    wide = 2 * BLK
    outs = [
        jax.ShapeDtypeStruct((d, total), BF16),
        jax.ShapeDtypeStruct((d, total), BF16),
        jax.ShapeDtypeStruct((3 * heads, HEAD_DIM, total), BF16),
        jax.ShapeDtypeStruct((heads, total, HEAD_DIM), BF16),
        jax.ShapeDtypeStruct((heads, total, HEAD_DIM), BF16),
    ]
    at = lambda p: p * (SLOTS // 2) + pair
    in_specs = [
        pl.BlockSpec((d, BLK), lambda p: (0, p)),
        pl.BlockSpec((d, BLK), lambda p: (0, p)),
        pl.BlockSpec(w.shape, lambda p: (0, 0, 0)),
        pl.BlockSpec(vec.shape, lambda p: (0, 0)),
        pl.BlockSpec(bias.shape, lambda p: (0, 0, 0)),
    ]
    args = [a, b, w, vec, bias]
    alias = {}
    if carry is not None:
        alias = {len(args) + n: n for n in range(len(outs))}
        in_specs += [pl.BlockSpec(memory_space=pl.ANY)] * len(outs)
        args += list(carry)
    return pl.pallas_call(
        functools.partial(qkv_kernel, heads),
        grid=(per,),
        in_specs=in_specs,
        out_specs=[
            pl.BlockSpec((d, wide), lambda p: (0, at(p))),
            pl.BlockSpec((d, wide), lambda p: (0, at(p))),
            pl.BlockSpec((3 * heads, HEAD_DIM, wide), lambda p: (0, 0, at(p))),
            pl.BlockSpec((heads, wide, HEAD_DIM), lambda p: (0, at(p), 0)),
            pl.BlockSpec((heads, wide, HEAD_DIM), lambda p: (0, at(p), 0)),
        ],
        out_shape=outs,
        input_output_aliases=alias,
        compiler_params=params(),
        cost_estimate=cost(2 * w.size * rows * 2, 2 * (w.size + 8 * d * rows)),
        name="qkv_call",
    )(*args)


def attend_kernel(heads, nb, per, chunk, info, start_ref, q_ref, kn_ref, v_ref, o_ref, lse_ref, acc, m_s, l_s):
    b = pl.program_id(0) * per + chunk

    def visit(kb, diag):
        at = pl.multiple_of(info[nb + kb] * BLK, BLK)
        kpos = lax.broadcasted_iota(jnp.int32, (BLK, BLK), 0)
        ok = kpos >= (start_ref[...] - kb * BLK)
        if diag:
            ok = ok & (kpos <= lax.broadcasted_iota(jnp.int32, (BLK, BLK), 1))
        scores = [dot(kn_ref[h, pl.ds(at, BLK), :], q_ref[h]) for h in range(heads)]
        scores = [jnp.where(ok, s, NEG) for s in scores]
        top = jnp.concatenate([jnp.max(s, axis=0, keepdims=True) for s in scores], 0)
        if not diag:
            old = m_s[0:heads, :]
            top = jnp.maximum(old, top)
            fade = jnp.exp2((old - top) * SCALE2)
        m_s[0:heads, :] = top
        expo = [jnp.exp2((scores[h] - top[h : h + 1]) * SCALE2) for h in range(heads)]
        sums = jnp.concatenate([jnp.sum(e, axis=0, keepdims=True) for e in expo], 0)
        l_s[0:heads, :] = sums if diag else l_s[0:heads, :] * fade + sums
        for h in range(heads):
            new = dot(v_ref[h, :, pl.ds(at, BLK)], expo[h].astype(BF16))
            acc[h] = new if diag else acc[h] * fade[h : h + 1] + new

    visit(b, True)

    def step(kb, _):
        visit(kb, False)
        return 0

    lax.fori_loop(info[b], b, step, 0)
    for h in range(heads):
        total = l_s[h : h + 1, :]
        o_ref[h] = (acc[h] * (1.0 / total)).astype(BF16)
        lse_ref[h : h + 1, :] = m_s[h : h + 1, :] * SCALE2 + jnp.log2(total)


def attend(chunk, info, start, qkv, kn):
    heads, total = qkv.shape[0] // 3, qkv.shape[2]
    nb = total // BLK
    per = nb // SLOTS
    spec = pltpu.PrefetchScalarGridSpec(
        num_scalar_prefetch=1,
        grid=(SLOTS,),
        in_specs=[
            pl.BlockSpec((1, BLK), lambda i, s: (0, i * per + chunk)),
            pl.BlockSpec((heads, HEAD_DIM, BLK), lambda i, s: (0, 0, s[nb + i * per + chunk])),
            pl.BlockSpec((heads, total, HEAD_DIM), lambda i, s: (0, 0, 0)),
            pl.BlockSpec((heads, HEAD_DIM, total), lambda i, s: (2, 0, 0)),
        ],
        out_specs=[
            pl.BlockSpec((heads, HEAD_DIM, BLK), lambda i, s: (0, 0, i)),
            pl.BlockSpec((8, BLK), lambda i, s: (0, i)),
        ],
        scratch_shapes=[
            pltpu.VMEM((heads, HEAD_DIM, BLK), F32),
            pltpu.VMEM((8, BLK), F32),
            pltpu.VMEM((8, BLK), F32),
        ],
    )
    return pl.pallas_call(
        functools.partial(attend_kernel, heads, nb, per, chunk),
        grid_spec=spec,
        out_shape=[
            jax.ShapeDtypeStruct((heads, HEAD_DIM, SLOTS * BLK), BF16),
            jax.ShapeDtypeStruct((8, SLOTS * BLK), F32),
        ],
        compiler_params=params(),
        cost_estimate=cost(6e9, 6e6, 4e6),
        name="attend",
    )(info, start, qkv, kn, qkv)


def attend_back_kernel(heads, nb, per, info, start_ref, q_ref, k_ref, kn_ref, vn_ref, o_ref, do_ref, lse_ref, out_ref, dq_s, dk_s, dv_s, dl):
    j = pl.program_id(0)

    def place(b):
        return pl.multiple_of(info[nb + b] * BLK, BLK)

    def ordered(b):
        return pl.multiple_of(((b % per) * SLOTS + b // per) * BLK, BLK)

    @pl.when(j == 0)
    def _():
        dq_s[...] = jnp.zeros_like(dq_s)
        for b in range(nb):
            cut = slice(b * BLK, (b + 1) * BLK)
            for h in range(heads):
                dl[h : h + 1, cut] = jnp.sum(
                    o_ref[h, :, cut].astype(F32) * do_ref[h, :, cut].astype(F32), axis=0, keepdims=True
                )

    def visit(b, diag):
        at = place(b)
        mine = ordered(b)
        kpos = lax.broadcasted_iota(jnp.int32, (BLK, BLK), 0)
        ok = kpos >= (start_ref[:, pl.ds(pl.multiple_of(b * BLK, BLK), BLK)] - j * BLK)
        if diag:
            ok = ok & (kpos <= lax.broadcasted_iota(jnp.int32, (BLK, BLK), 1))
        every = range(heads)
        query = [q_ref[h, :, pl.ds(at, BLK)] for h in every]
        grad = [do_ref[h, :, pl.ds(mine, BLK)] for h in every]
        scores = [dot(kn_ref[h], query[h]) for h in every]
        prob_grad = [dot(vn_ref[h], grad[h]) for h in every]
        probs = [
            jnp.where(ok, jnp.exp2(scores[h] * SCALE2 - lse_ref[h : h + 1, pl.ds(mine, BLK)]), 0.0) for h in every
        ]
        score_grad = [
            (probs[h] * (prob_grad[h] - dl[h : h + 1, pl.ds(mine, BLK)])).astype(BF16) for h in every
        ]
        dv = [dot(grad[h], probs[h].astype(BF16), NT) for h in every]
        dk = [dot(query[h], score_grad[h], NT) for h in every]
        dq = [dot(k_ref[h], score_grad[h]) for h in every]
        for h in every:
            if diag:
                dv_s[h] = dv[h]
                dk_s[h] = dk[h]
            else:
                dv_s[h] += dv[h]
                dk_s[h] += dk[h]
            dq_s[h, :, pl.ds(at, BLK)] += dq[h]

    visit(j, True)

    def step(b, _):
        visit(b, False)
        return 0

    lax.fori_loop(j + 1, info[2 * nb + j] + 1, step, 0)
    at = place(j)
    for h in range(heads):
        out_ref[h] = (dq_s[h, :, pl.ds(at, BLK)] * SCALE).astype(BF16)
        out_ref[heads + h] = (dk_s[h] * SCALE).astype(BF16)
        out_ref[2 * heads + h] = dv_s[h].astype(BF16)


def attend_back(info, start, qkv, kn, vn, o, do, lse):
    heads, total = qkv.shape[0] // 3, qkv.shape[2]
    nb = total // BLK
    per = nb // SLOTS
    whole = pl.BlockSpec((heads, HEAD_DIM, total), lambda j, s: (0, 0, 0))
    block = lambda a: pl.BlockSpec((heads, HEAD_DIM, BLK), lambda j, s: (a, 0, s[nb + j]))
    tall = pl.BlockSpec((heads, BLK, HEAD_DIM), lambda j, s: (0, s[nb + j], 0))
    spec = pltpu.PrefetchScalarGridSpec(
        num_scalar_prefetch=1,
        grid=(nb,),
        in_specs=[
            pl.BlockSpec((1, total), lambda j, s: (0, 0)),
            whole,
            block(1),
            tall,
            tall,
            whole,
            whole,
            pl.BlockSpec((8, total), lambda j, s: (0, 0)),
        ],
        out_specs=pl.BlockSpec((3 * heads, HEAD_DIM, BLK), lambda j, s: (0, 0, s[nb + j])),
        scratch_shapes=[
            pltpu.VMEM((heads, HEAD_DIM, total), F32),
            pltpu.VMEM((heads, HEAD_DIM, BLK), F32),
            pltpu.VMEM((heads, HEAD_DIM, BLK), F32),
            pltpu.VMEM((8, total), F32),
        ],
    )
    return pl.pallas_call(
        functools.partial(attend_back_kernel, heads, nb, per),
        grid_spec=spec,
        out_shape=jax.ShapeDtypeStruct((3 * heads, HEAD_DIM, total), BF16),
        compiler_params=params(),
        cost_estimate=cost(16e9, 12e6, 8e6),
        name="attend_back",
    )(info, start, qkv, qkv, kn, vn, o, do, lse)


def middle_kernel(info, att_ref, x_ref, g_ref, wot, wo, upt, up, wd, wdt, vec_ref, *outs):
    h_out, act_out, pg_out, layer_out, y1g_out, own_out, sum_out = outs[:7]
    attg_outs = outs[7:]
    s = pl.program_id(0)
    out_bias, gain, shift, up_bias = (vec_ref[:, n : n + 1] for n in range(4))
    g = g_ref[...]
    y1 = x_ref[...].astype(F32) + (dot(wot[...], att_ref[...]) + out_bias)

    @pl.when(s == 0)
    def _():
        own_out[...] = y1

    n, root = normal(y1)
    h = (n * gain + shift).astype(BF16)
    h_out[...] = h
    pre = dot(upt[...], h) + up_bias
    square = pre * pre
    t = jnp.tanh(pre * (GELU_C + (GELU_C * GELU_A) * square))
    half = 0.5 * (1.0 + t)
    act = (pre * half).astype(BF16)
    act_out[...] = act
    slope = half + (0.5 * pre) * (1.0 - t * t) * (GELU_C + (3.0 * GELU_C * GELU_A) * square)
    pg = dot(wd[...], g) * slope
    pgb = pg.astype(BF16)
    pg_out[...] = pgb
    layer_out[0] = dot(wdt[...], act).astype(BF16)
    hg = dot(up[...], pgb)
    e = hg * gain
    y1g = root * (e - jnp.mean(e, axis=0, keepdims=True) - n * jnp.mean(e * n, axis=0, keepdims=True))
    y1g = y1g + jnp.where(s == 0, g.astype(F32), 0.0)
    y1b = y1g.astype(BF16)
    y1g_out[0] = y1b
    attg = dot(wo[...], y1b)
    rows = attg_outs[0].shape[0]
    for k in range(SLOTS):
        attg_outs[k][...] = attg[k * rows : (k + 1) * rows].astype(BF16)
    parts = (fold(hg * n), fold(hg), fold(y1g), fold(pgb.astype(F32)))
    for at, part in enumerate(parts):
        sum_out[at] = jnp.where(s == 0, part, sum_out[at] + part)


def middle(chunk, info, att, x, g, wot, wo, upt, up, wd, wdt, vec):
    d = x.shape[0]
    f = upt.shape[0]
    rows = att.shape[0] // SLOTS
    wide = SLOTS * BLK
    nb = x.shape[1] // BLK
    dev = 3 * nb
    keep = lambda a: pl.BlockSpec(a.shape, lambda s, i: (0,) * a.ndim, pipeline_mode=pl.Buffered(1))
    place = lambda r: pl.BlockSpec((r, BLK), lambda s, i: (0, s ^ i[dev]))
    block = lambda r: pl.BlockSpec((r, BLK), lambda s, i: (0, s))
    full = lambda r: pl.BlockSpec((r, BLK), lambda s, i: (0, chunk * SLOTS + s))
    slot = lambda r: pl.BlockSpec((1, r, BLK), lambda s, i: (s, 0, 0))
    spec = pltpu.PrefetchScalarGridSpec(
        num_scalar_prefetch=1,
        grid=(SLOTS,),
        in_specs=[place(att.shape[0]), full(d), full(d)] + [keep(a) for a in (wot, wo, upt, up, wd, wdt, vec)],
        out_specs=[
            block(d),
            block(f),
            block(f),
            slot(d),
            slot(d),
            pl.BlockSpec((d, BLK), lambda s, i: (0, 0)),
            pl.BlockSpec((4, d, 128), lambda s, i: (0, 0, 0)),
        ]
        + [place(rows)] * SLOTS,
    )
    shape = jax.ShapeDtypeStruct
    return pl.pallas_call(
        middle_kernel,
        grid_spec=spec,
        out_shape=[
            shape((d, wide), BF16),
            shape((f, wide), BF16),
            shape((f, wide), BF16),
            shape((SLOTS, d, BLK), BF16),
            shape((SLOTS, d, BLK), BF16),
            shape((d, BLK), F32),
            shape((4, d, 128), F32),
        ]
        + [shape((rows, wide), BF16)] * SLOTS,
        compiler_params=params(),
        cost_estimate=cost(12 * d * f * wide, 12 * d * f + 20 * d * wide, 2 * f * wide),
        name="middle",
    )(info, att, x, g, wot, wo, upt, up, wd, wdt, vec)


def outer_kernel(count, *refs):
    out = refs[-1]
    total = None
    for n in range(count):
        part = dot(refs[2 * n][...], refs[2 * n + 1][...], NT)
        total = part if total is None else total + part
    out[...] = total.astype(out.dtype)


def outer(pairs, rows):
    m, n = pairs[0][0].shape[0], pairs[0][1].shape[0]
    in_specs, args = [], []
    depth = 0
    for a, b, width, a_at, b_at in pairs:
        in_specs.append(pl.BlockSpec((rows, width), functools.partial(lambda at, i: (i, at), a_at)))
        in_specs.append(
            pl.BlockSpec((n, width), functools.partial(lambda at, i: (0, at), b_at), pipeline_mode=pl.Buffered(1))
        )
        args += [a, b]
        depth += width
    return pl.pallas_call(
        functools.partial(outer_kernel, len(pairs)),
        grid=(m // rows,),
        in_specs=in_specs,
        out_specs=pl.BlockSpec((rows, n), lambda i: (i, 0)),
        out_shape=jax.ShapeDtypeStruct((m, n), BF16),
        compiler_params=params(),
        cost_estimate=cost(2 * m * n * depth, 2 * (m + n) * depth + 2 * m * n),
        name="outer",
    )(*args)


def out_grad_kernel(count, info, *refs):
    outs = refs[2 * count :]
    total = None
    for n in range(count):
        part = dot(refs[2 * n][...], refs[2 * n + 1][...], NT)
        total = part if total is None else total + part
    for k in range(SLOTS):

        @pl.when(pl.program_id(0) == k)
        def _():
            outs[k][...] = total.astype(BF16)


def out_grad_call(info, atts, y1g):
    rows = atts[0].shape[0] // SLOTS
    d = y1g.shape[0]
    count = len(atts)
    dev = info.shape[0] - 1
    in_specs, args = [], []
    for n in range(count):
        in_specs.append(pl.BlockSpec((rows, BLK), lambda k, i: (k, i[dev])))
        in_specs.append(pl.BlockSpec((d, BLK), functools.partial(lambda at, k, i: (0, at), n)))
        args += [atts[n], y1g]
    spec = pltpu.PrefetchScalarGridSpec(
        num_scalar_prefetch=1,
        grid=(SLOTS,),
        in_specs=in_specs,
        out_specs=[pl.BlockSpec((rows, d), lambda k, i: (0, 0))] * SLOTS,
    )
    return pl.pallas_call(
        functools.partial(out_grad_kernel, count),
        grid_spec=spec,
        out_shape=[jax.ShapeDtypeStruct((rows, d), BF16)] * SLOTS,
        compiler_params=params(),
        cost_estimate=cost(2 * SLOTS * rows * d * BLK * count, 4 * SLOTS * rows * d),
        name="out_grad_call",
    )(info, *args)


def attn_grad_kernel(a_ref, b_ref, out_ref, sum_ref):
    a = a_ref[...]
    out_ref[...] = dot(a, b_ref[...], NT).astype(BF16)
    sum_ref[...] = fold(a.astype(F32))


def attn_grad_call(dqkv, h1):
    m, total = dqkv.shape
    d = h1.shape[0]
    rows = m // 3
    return pl.pallas_call(
        attn_grad_kernel,
        grid=(3,),
        in_specs=[
            pl.BlockSpec((rows, total), lambda i: (i, 0)),
            pl.BlockSpec((d, total), lambda i: (0, 0), pipeline_mode=pl.Buffered(1)),
        ],
        out_specs=[pl.BlockSpec((rows, d), lambda i: (i, 0)), pl.BlockSpec((rows, 128), lambda i: (i, 0))],
        out_shape=[jax.ShapeDtypeStruct((m, d), BF16), jax.ShapeDtypeStruct((m, 128), F32)],
        compiler_params=params(),
        cost_estimate=cost(2 * m * d * total, 2 * (m + d) * total + 2 * m * d),
        name="attn_grad_call",
    )(dqkv, h1)


def h1_grad_kernel(w_ref, dqkv_ref, x_ref, out_ref, sum_ref):
    first = (pl.program_id(0) == 0) & (pl.program_id(1) == 0)
    hg = dot(w_ref[...], dqkv_ref[...])
    n, _ = normal(x_ref[...].astype(F32))
    out_ref[0] = hg.astype(BF16)
    for at, part in enumerate((fold(hg * n), fold(hg))):
        sum_ref[at] = jnp.where(first, part, sum_ref[at] + part)


def h1_grad_call(w, dqkv, x):
    d, total = x.shape
    per = total // (BLK * SLOTS)
    m = w.shape[1]
    at = lambda s, p: (0, p * SLOTS + s)
    return pl.pallas_call(
        h1_grad_kernel,
        grid=(SLOTS, per),
        in_specs=[
            pl.BlockSpec((d, m), lambda s, p: (0, 0), pipeline_mode=pl.Buffered(1)),
            pl.BlockSpec((m, BLK), at),
            pl.BlockSpec((d, BLK), at),
        ],
        out_specs=[
            pl.BlockSpec((1, d, BLK), lambda s, p: (s, 0, p)),
            pl.BlockSpec((2, d, 128), lambda s, p: (0, 0, 0)),
        ],
        out_shape=[jax.ShapeDtypeStruct((SLOTS, d, per * BLK), BF16), jax.ShapeDtypeStruct((2, d, 128), F32)],
        compiler_params=params(),
        cost_estimate=cost(2 * d * m * total, 2 * d * m + 6 * d * total),
        name="h1_grad_call",
    )(w, dqkv, x)


def input_grad_kernel(x_ref, a_ref, b_ref, y1g_ref, gain_ref, out_ref):
    n, root = normal(x_ref[...].astype(F32))
    e = (a_ref[...] + b_ref[...].astype(F32)) * gain_ref[...]
    e = root * (e - jnp.mean(e, axis=0, keepdims=True) - n * jnp.mean(e * n, axis=0, keepdims=True))
    out_ref[...] = (y1g_ref[...] + e).astype(BF16)


def input_grad_call(x, a, b, y1g, gain):
    d, rows = x.shape
    block = pl.BlockSpec((d, 128), lambda i: (0, i))
    return pl.pallas_call(
        input_grad_kernel,
        grid=(rows // 128,),
        in_specs=[block] * 4 + [pl.BlockSpec((d, 1), lambda i: (0, 0))],
        out_specs=block,
        out_shape=jax.ShapeDtypeStruct((d, rows), BF16),
        compiler_params=params(),
        cost_estimate=cost(20 * d * rows, 14 * d * rows),
        name="input_grad_call",
    )(x, a, b, y1g, gain)


def swap(v, k):
    return lax.ppermute(v, "tensor", [(i, i ^ k) for i in range(SLOTS)])


def gather(v):
    far = swap(v, 2)
    return v, swap(v, 1), far, swap(far, 1)


def scatter_sum(parts):
    wide = [p.astype(F32) for p in parts]
    far = (wide[2] + swap(parts[3], 1).astype(F32)).astype(BF16)
    near = wide[0] + swap(parts[1], 1).astype(F32)
    return near, swap(far, 2)


def token_starts(lengths, offsets, total, dev):
    pos = jnp.arange(total, dtype=jnp.int32)[:, None]
    inside = (pos >= offsets[None]) & (pos < (offsets + lengths)[None])
    first = jnp.max(jnp.where(inside, offsets[None], -1), axis=1)
    start = jnp.where(first >= 0, first, pos[:, 0])
    nb = total // BLK
    per = nb // SLOTS
    b = jnp.arange(nb, dtype=jnp.int32)
    first_key = start.reshape(nb, BLK)[:, 0] // BLK
    place = (b % per) * SLOTS + ((b // per) ^ dev)
    last_query = jnp.max(jnp.where(first_key[None, :] <= b[:, None], b[None, :], 0), axis=1)
    info = jnp.concatenate([first_key, place, last_query, jnp.full((1,), dev)])
    return start[None], info.astype(jnp.int32)


def body(
    tokens,
    cotangent,
    ln1_gain,
    ln1_bias,
    attn_weight,
    qv_bias,
    out_weight,
    out_bias,
    ln2_gain,
    ln2_bias,
    up_weight,
    up_bias,
    down_weight,
    down_bias,
    cell_lengths,
    cell_offsets,
):
    rows, d = tokens.shape
    width = attn_weight.shape[2]
    heads = width // HEAD_DIM
    total = rows * SLOTS
    per = rows // BLK
    dev = lax.axis_index("tensor")
    start, info = token_starts(cell_lengths[0], cell_offsets[0], total, dev)

    x_own = tokens.T
    g_own = cotangent.T
    x_parts = gather(x_own)
    wo = jnp.concatenate(gather(out_weight), 0)
    g_parts = gather(g_own)

    w_in = attn_weight.transpose(1, 2, 0)
    w_back = w_in.reshape(3 * width, d).T
    vec1 = jnp.stack([ln1_gain, ln1_bias], 1)
    qkv_bias = jnp.stack([qv_bias[0], jnp.zeros_like(qv_bias[0]), qv_bias[1]])[:, :, None]
    carry = qkv_call(0, x_parts[0], x_parts[1], w_in, vec1, qkv_bias, None)
    x_all, h1, qkv, kn, vn = qkv_call(1, x_parts[2], x_parts[3], w_in, vec1, qkv_bias, carry)

    def chunked(parts):
        cut = lambda p, c: p[:, c * BLK : (c + 1) * BLK]
        return jnp.concatenate([cut(p, c) for c in range(per) for p in parts], 1)

    g_all = chunked(g_parts)
    wot, upt, wdt = wo.T, up_weight.T, down_weight.T
    vec2 = jnp.stack([out_bias, ln2_gain, ln2_bias, up_bias], 1)

    fronts = [attend(c, info, start, qkv, kn) for c in range(per)]
    atts = [jnp.concatenate(gather(o.reshape(width, SLOTS * BLK)), 0) for o, _ in fronts]
    mids = [
        middle(c, info, atts[c], x_all, g_all, wot, wo, upt, up_weight, down_weight, wdt, vec2) for c in range(per)
    ]
    h2s, acts, pgs, layers, y1gs, owns, sums = zip(*[m[:7] for m in mids])
    attg = [scatter_sum(m[7:]) for m in mids]
    do = jnp.concatenate([(a + b.astype(F32)).astype(BF16) for a, b in attg], 1).reshape(heads, HEAD_DIM, total)
    o = jnp.concatenate([f[0] for f in fronts], 2)
    lse = jnp.concatenate([f[1] for f in fronts], 1)

    wide = SLOTS * BLK
    down_grad = outer([(acts[c], g_all, wide, 0, c) for c in range(per)], width)
    up_grad = outer([(h2s[c], pgs[c], wide, 0, 0) for c in range(per)], width)
    early = lax.psum((down_grad, up_grad), "dp")

    y1_parts = [scatter_sum([y[k] for k in range(SLOTS)]) for y in y1gs]
    y1_grad = jnp.concatenate([a + b.astype(F32) for a, b in y1_parts], 1)
    layer_parts = [scatter_sum([y[k] for k in range(SLOTS)]) for y in layers]
    layer = jnp.concatenate([a + b.astype(F32) for a, b in layer_parts], 1)
    layer = (jnp.concatenate(owns, 1) + layer + down_bias[:, None]).astype(BF16)

    out_parts = out_grad_call(info, atts, y1_grad.astype(BF16))
    out_near, out_far = scatter_sum(out_parts)
    out_grad = (out_near + out_far.astype(F32)).astype(BF16)

    dqkv = attend_back(info, start, qkv, kn, vn, o, do, lse).reshape(3 * width, total)
    h1_parts, sum1 = h1_grad_call(w_back, dqkv, x_all)
    attn_grad, qkv_sum = attn_grad_call(dqkv, h1)
    near, far = scatter_sum([h1_parts[k] for k in range(SLOTS)])
    input_grad = input_grad_call(x_own, near, far, y1_grad, ln1_gain[:, None])

    sum2 = jnp.sum(sum(sums), axis=2)
    sum1 = jnp.sum(sum1, axis=2)
    qkv_sum = jnp.sum(qkv_sum, axis=1).reshape(3, width)
    down_sum = jnp.sum(g_own.astype(F32), axis=1)
    small = jnp.concatenate([sum1, sum2[:3], down_sum[None]], 0)
    small = lax.psum(small, ("dp", "tensor"))
    late = lax.optimization_barrier((attn_grad, out_grad, early))
    early = late[2]
    late = lax.psum(late[:2], "dp")
    dp_small = lax.psum((sum2[3], qkv_sum), "dp")

    down_grad, up_grad = (v.astype(F32) for v in early)
    attn_grad, out_grad = (v.astype(F32) for v in late)
    up_bias_grad, qkv_sum = dp_small
    return (
        layer.T,
        input_grad.T,
        small[0],
        small[1],
        attn_grad.reshape(3, width, d).transpose(2, 0, 1),
        jnp.stack([qkv_sum[0], qkv_sum[2]]),
        out_grad,
        small[4],
        small[2],
        small[3],
        up_grad,
        up_bias_grad,
        down_grad,
        small[5],
    )


def solution(mesh):
    rows = P(("dp", "tensor"), None)
    in_specs = (
        rows,
        rows,
        P(),
        P(),
        P(None, None, "tensor"),
        P(None, "tensor"),
        P("tensor", None),
        P(),
        P(),
        P(),
        P(None, "tensor"),
        P("tensor"),
        P("tensor", None),
        P(),
        P("dp", None),
        P("dp", None),
    )
    out_specs = (
        rows,
        rows,
        P(),
        P(),
        P(None, None, "tensor"),
        P(None, "tensor"),
        P("tensor", None),
        P(),
        P(),
        P(),
        P(None, "tensor"),
        P("tensor"),
        P("tensor", None),
        P(),
    )
    return jax.shard_map(body, mesh=mesh, in_specs=in_specs, out_specs=out_specs, check_vma=False)
```

```python
import functools
import math

import jax
import jax.numpy as jnp
from jax import lax
from jax.experimental import pallas as pl
from jax.experimental.pallas import tpu as pltpu
from jax.sharding import PartitionSpec as P


HEAD_DIM = 56
BLK = 256
SLOTS = 4
NEG = -1e30
EPS = 1e-05
SCALE = 1.0 / math.sqrt(HEAD_DIM)
SCALE2 = SCALE * math.log2(math.e)
GELU_C = math.sqrt(2.0 / math.pi)
GELU_A = 0.044715
F32 = jnp.float32
BF16 = jnp.bfloat16
NT = ((1,), (1,))
ROWS = 224
GAIN1, SHIFT1, OUT_BIAS, GAIN2, SHIFT2, UP_BIAS, DOWN_BIAS = range(7)
VEC8 = True
ATT_PIECES = True
VMEM = 60 << 20
PACE = 2.3e9


def dot(a, b, dims=((1,), (0,))):
    return lax.dot_general(a, b, (dims, ((), ())), preferred_element_type=F32)


def params():
    return pltpu.CompilerParams(vmem_limit_bytes=VMEM)


def cost(microseconds):
    return pl.CostEstimate(flops=int(microseconds * PACE), bytes_accessed=1, transcendentals=0)


def fold(v):
    total = v[:, :128]
    for at in range(128, v.shape[1], 128):
        total = total + v[:, at : at + 128]
    return total


def normal(x):
    center = x - jnp.mean(x, axis=0, keepdims=True)
    root = lax.rsqrt(jnp.mean(center * center, axis=0, keepdims=True) + EPS)
    return center * root, root


def turn_kernel(count, parts, *refs):
    for n in range(count):
        refs[count + 1 + n][...] = refs[n][...].T
    for n in range(parts):
        refs[2 * count + 1 + n][...] = refs[count][:, n * BLK : (n + 1) * BLK]


def turn(cut, *arrays):
    wide = max(a.shape[1] for a in arrays)
    steps = -(-wide // 256)
    in_specs, out_specs, outs = [], [], []
    for a in arrays:
        rows, columns = a.shape
        if columns == wide:
            in_specs.append(pl.BlockSpec((rows, 256), lambda i: (0, i)))
            out_specs.append(pl.BlockSpec((256, rows), lambda i: (i, 0)))
        else:
            in_specs.append(pl.BlockSpec((rows, columns), lambda i: (0, 0)))
            out_specs.append(pl.BlockSpec((columns, rows), lambda i: (0, 0)))
        outs.append(jax.ShapeDtypeStruct((columns, rows), a.dtype))
    rows, columns = cut.shape
    parts = columns // BLK
    size = -(-rows // (16 * steps)) * 16
    in_specs.append(pl.BlockSpec((size, columns), lambda i: (i, 0)))
    out_specs += [pl.BlockSpec((size, BLK), lambda i: (i, 0))] * parts
    outs += [jax.ShapeDtypeStruct((rows, BLK), cut.dtype)] * parts
    return pl.pallas_call(
        functools.partial(turn_kernel, len(arrays), parts),
        grid=(steps,),
        in_specs=in_specs,
        out_specs=out_specs,
        out_shape=outs,
        compiler_params=params(),
        cost_estimate=cost(8),
        name="turn",
    )(*arrays, cut)


def turn_pieces_kernel(*refs):
    refs[-1][...] = jnp.concatenate([ref[...] for ref in refs[:-1]], 0).T


def turn_pieces(*pieces):
    rows, columns = pieces[0].shape
    return pl.pallas_call(
        turn_pieces_kernel,
        grid=(-(-columns // 256),),
        in_specs=[pl.BlockSpec((rows, 256), lambda i: (0, i))] * len(pieces),
        out_specs=pl.BlockSpec((256, rows * len(pieces)), lambda i: (i, 0)),
        out_shape=jax.ShapeDtypeStruct((columns, rows * len(pieces)), pieces[0].dtype),
        compiler_params=params(),
        cost_estimate=cost(5),
        name="turn_pieces",
    )(*pieces)


def col(ref, at, m):
    return ref[m, at : at + 1]


def cuts(total, size):
    return [slice(at, min(at + size, total)) for at in range(0, total, size)]


def qkv_kernel(heads, a_ref, b_ref, w_ref, vec_ref, bias_ref, *rest):
    x_out, h_out, q_out, kn_out, vn_out = rest[-5:]
    x_out[:, :BLK] = a_ref[...]
    x_out[:, BLK:] = b_ref[...]
    d = x_out.shape[0]
    pieces = cuts(d, ROWS)
    total = 0.0
    for m in pieces:
        total = total + jnp.sum(x_out[m].astype(F32), axis=0, keepdims=True)
    mean = total * (1.0 / d)
    total = 0.0
    for m in pieces:
        center = x_out[m].astype(F32) - mean
        total = total + jnp.sum(center * center, axis=0, keepdims=True)
    root = lax.rsqrt(total * (1.0 / d) + EPS)
    for m in pieces:
        n = (x_out[m].astype(F32) - mean) * root
        h_out[m] = (n * col(vec_ref, GAIN1, m) + col(vec_ref, SHIFT1, m)).astype(BF16)
    h = h_out[...]
    for part in range(3):
        r = (dot(w_ref[part], h) + bias_ref[:, part : part + 1]).astype(BF16)
        r = r.reshape(heads, HEAD_DIM, r.shape[1])
        q_out[part * heads : (part + 1) * heads] = r
        if part > 0:
            out = kn_out if part == 1 else vn_out
            for h_at in range(heads):
                out[h_at] = r[h_at].T


def qkv_call(pair, a, b, w, vec, bias, carry):
    d, rows = a.shape
    per = rows // BLK
    total = rows * SLOTS
    heads = w.shape[1] // HEAD_DIM
    wide = 2 * BLK
    outs = [
        jax.ShapeDtypeStruct((d, total), BF16),
        jax.ShapeDtypeStruct((d, total), BF16),
        jax.ShapeDtypeStruct((3 * heads, HEAD_DIM, total), BF16),
        jax.ShapeDtypeStruct((heads, total, HEAD_DIM), BF16),
        jax.ShapeDtypeStruct((heads, total, HEAD_DIM), BF16),
    ]
    at = lambda p: p * (SLOTS // 2) + pair
    in_specs = [
        pl.BlockSpec((d, BLK), lambda p: (0, p)),
        pl.BlockSpec((d, BLK), lambda p: (0, p)),
        pl.BlockSpec(w.shape, lambda p: (0, 0, 0)),
        pl.BlockSpec(vec.shape, lambda p: (0, 0)),
        pl.BlockSpec(bias.shape, lambda p: (0, 0)),
    ]
    args = [a, b, w, vec, bias]
    alias = {}
    if carry is not None:
        alias = {len(args) + n: n for n in range(len(outs))}
        in_specs += [pl.BlockSpec(memory_space=pl.ANY)] * len(outs)
        args += list(carry)
    return pl.pallas_call(
        functools.partial(qkv_kernel, heads),
        grid=(per,),
        in_specs=in_specs,
        out_specs=[
            pl.BlockSpec((d, wide), lambda p: (0, at(p))),
            pl.BlockSpec((d, wide), lambda p: (0, at(p))),
            pl.BlockSpec((3 * heads, HEAD_DIM, wide), lambda p: (0, 0, at(p))),
            pl.BlockSpec((heads, wide, HEAD_DIM), lambda p: (0, at(p), 0)),
            pl.BlockSpec((heads, wide, HEAD_DIM), lambda p: (0, at(p), 0)),
        ],
        out_shape=outs,
        input_output_aliases=alias,
        compiler_params=params(),
        cost_estimate=cost(8),
        name="qkv_call",
    )(*args)


def attend_kernel(heads, nb, per, chunk, info, start_ref, q_ref, kn_ref, v_ref, o_ref, lse_ref, acc, m_s, l_s):
    b = pl.program_id(0) * per + chunk

    def visit(kb, diag):
        at = pl.multiple_of(info[nb + kb] * BLK, BLK)
        kpos = lax.broadcasted_iota(jnp.int32, (BLK, BLK), 0)
        ok = kpos >= (start_ref[...] - kb * BLK)
        if diag:
            ok = ok & (kpos <= lax.broadcasted_iota(jnp.int32, (BLK, BLK), 1))
        scores = [dot(kn_ref[h, pl.ds(at, BLK), :], q_ref[h]) for h in range(heads)]
        scores = [jnp.where(ok, s, NEG) for s in scores]
        top = jnp.concatenate([jnp.max(s, axis=0, keepdims=True) for s in scores], 0)
        if not diag:
            old = m_s[0:heads, :]
            top = jnp.maximum(old, top)
            fade = jnp.exp2((old - top) * SCALE2)
        m_s[0:heads, :] = top
        expo = [jnp.exp2((scores[h] - top[h : h + 1]) * SCALE2) for h in range(heads)]
        sums = jnp.concatenate([jnp.sum(e, axis=0, keepdims=True) for e in expo], 0)
        l_s[0:heads, :] = sums if diag else l_s[0:heads, :] * fade + sums
        for h in range(heads):
            new = dot(v_ref[h, :, pl.ds(at, BLK)], expo[h].astype(BF16))
            acc[h] = new if diag else acc[h] * fade[h : h + 1] + new

    visit(b, True)

    def step(kb, _):
        visit(kb, False)
        return 0

    lax.fori_loop(info[b], b, step, 0)
    for h in range(heads):
        total = l_s[h : h + 1, :]
        o_ref[h] = (acc[h] * (1.0 / total)).astype(BF16)
        lse_ref[h : h + 1, :] = m_s[h : h + 1, :] * SCALE2 + jnp.log2(total)


def attend(chunk, info, start, qkv, kn):
    heads, total = qkv.shape[0] // 3, qkv.shape[2]
    nb = total // BLK
    per = nb // SLOTS
    spec = pltpu.PrefetchScalarGridSpec(
        num_scalar_prefetch=1,
        grid=(SLOTS,),
        in_specs=[
            pl.BlockSpec((1, BLK), lambda i, s: (0, i * per + chunk)),
            pl.BlockSpec((heads, HEAD_DIM, BLK), lambda i, s: (0, 0, s[nb + i * per + chunk])),
            pl.BlockSpec((heads, total, HEAD_DIM), lambda i, s: (0, 0, 0)),
            pl.BlockSpec((heads, HEAD_DIM, total), lambda i, s: (2, 0, 0)),
        ],
        out_specs=[
            pl.BlockSpec((heads, HEAD_DIM, BLK), lambda i, s: (0, 0, i)),
            pl.BlockSpec((8, BLK), lambda i, s: (0, i)),
        ],
        scratch_shapes=[
            pltpu.VMEM((heads, HEAD_DIM, BLK), F32),
            pltpu.VMEM((8, BLK), F32),
            pltpu.VMEM((8, BLK), F32),
        ],
    )
    return pl.pallas_call(
        functools.partial(attend_kernel, heads, nb, per, chunk),
        grid_spec=spec,
        out_shape=[
            jax.ShapeDtypeStruct((heads, HEAD_DIM, SLOTS * BLK), BF16),
            jax.ShapeDtypeStruct((8, SLOTS * BLK), F32),
        ],
        compiler_params=params(),
        cost_estimate=cost(9.5),
        name="attend",
    )(info, start, qkv, kn, qkv)


def attend_back_kernel(heads, nb, per, info, start_ref, q_ref, k_ref, kn_ref, vn_ref, do_ref, stat_ref, out_ref, dq_s, dk_s, dv_s):
    j = pl.program_id(0)

    def place(b):
        return pl.multiple_of(info[nb + b] * BLK, BLK)

    def ordered(b):
        return pl.multiple_of(((b % per) * SLOTS + b // per) * BLK, BLK)

    @pl.when(j == 0)
    def _():
        dq_s[...] = jnp.zeros_like(dq_s)

    def visit(b, diag):
        at = place(b)
        mine = ordered(b)
        kpos = lax.broadcasted_iota(jnp.int32, (BLK, BLK), 0)
        ok = kpos >= (start_ref[:, pl.ds(pl.multiple_of(b * BLK, BLK), BLK)] - j * BLK)
        if diag:
            ok = ok & (kpos <= lax.broadcasted_iota(jnp.int32, (BLK, BLK), 1))
        every = range(heads)
        query = [q_ref[h, :, pl.ds(at, BLK)] for h in every]
        grad = [do_ref[h, :, pl.ds(mine, BLK)] for h in every]
        scores = [dot(kn_ref[h], query[h]) for h in every]
        prob_grad = [dot(vn_ref[h], grad[h]) for h in every]
        probs = [
            jnp.where(ok, jnp.exp2(scores[h] * SCALE2 - stat_ref[h : h + 1, pl.ds(mine, BLK)]), 0.0) for h in every
        ]
        score_grad = [
            (probs[h] * (prob_grad[h] - stat_ref[8 + h : 9 + h, pl.ds(mine, BLK)])).astype(BF16) for h in every
        ]
        dv = [dot(grad[h], probs[h].astype(BF16), NT) for h in every]
        dk = [dot(query[h], score_grad[h], NT) for h in every]
        dq = [dot(k_ref[h], score_grad[h]) for h in every]
        for h in every:
            if diag:
                dv_s[h] = dv[h]
                dk_s[h] = dk[h]
            else:
                dv_s[h] += dv[h]
                dk_s[h] += dk[h]
            dq_s[h, :, pl.ds(at, BLK)] += dq[h]

    visit(j, True)

    def step(b, _):
        visit(b, False)
        return 0

    lax.fori_loop(j + 1, info[2 * nb + j] + 1, step, 0)
    at = place(j)
    for h in range(heads):
        out_ref[h] = (dq_s[h, :, pl.ds(at, BLK)] * SCALE).astype(BF16)
        out_ref[heads + h] = (dk_s[h] * SCALE).astype(BF16)
        out_ref[2 * heads + h] = dv_s[h].astype(BF16)


def attend_back(info, start, qkv, kn, vn, do, stat):
    heads, total = qkv.shape[0] // 3, qkv.shape[2]
    nb = total // BLK
    per = nb // SLOTS
    whole = pl.BlockSpec((heads, HEAD_DIM, total), lambda j, s: (0, 0, 0))
    block = lambda a: pl.BlockSpec((heads, HEAD_DIM, BLK), lambda j, s: (a, 0, s[nb + j]))
    tall = pl.BlockSpec((heads, BLK, HEAD_DIM), lambda j, s: (0, s[nb + j], 0))
    spec = pltpu.PrefetchScalarGridSpec(
        num_scalar_prefetch=1,
        grid=(nb,),
        in_specs=[
            pl.BlockSpec((1, total), lambda j, s: (0, 0)),
            whole,
            block(1),
            tall,
            tall,
            whole,
            pl.BlockSpec((16, total), lambda j, s: (0, 0)),
        ],
        out_specs=pl.BlockSpec((3 * heads, HEAD_DIM, BLK), lambda j, s: (0, 0, s[nb + j])),
        scratch_shapes=[
            pltpu.VMEM((heads, HEAD_DIM, total), F32),
            pltpu.VMEM((heads, HEAD_DIM, BLK), F32),
            pltpu.VMEM((heads, HEAD_DIM, BLK), F32),
        ],
    )
    return pl.pallas_call(
        functools.partial(attend_back_kernel, heads, nb, per),
        grid_spec=spec,
        out_shape=jax.ShapeDtypeStruct((3 * heads, HEAD_DIM, total), BF16),
        compiler_params=params(),
        cost_estimate=cost(20),
        name="attend_back",
    )(info, start, qkv, qkv, kn, vn, do, stat)


def join_kernel(chunks, *refs):
    do_out, stat_out = refs[-2:]
    h = pl.program_id(0)
    wide = SLOTS * BLK
    for c in range(chunks):
        a, near, far, o, lse = refs[5 * c : 5 * c + 5]
        cut = slice(c * wide, (c + 1) * wide)
        do = (a[0].astype(F32) + near[0, 0].astype(F32) + far[0].astype(F32)).astype(BF16)
        do_out[0, :, cut] = do
        stat_out[pl.ds(h + 8, 1), cut] = jnp.sum(o[0].astype(F32) * do.astype(F32), axis=0, keepdims=True)

        @pl.when(h == 0)
        def _():
            stat_out[0:8, cut] = lse[...]


def join(parts):
    heads, _, wide = parts[0][3].shape
    total = wide * len(parts)
    in_specs, args = [], []
    block = pl.BlockSpec((1, HEAD_DIM, wide), lambda h: (h, 0, 0))
    for a, near, far, o, lse in parts:
        args += [
            a.reshape(heads, HEAD_DIM, wide),
            near.reshape(2, heads, HEAD_DIM, wide),
            far.reshape(heads, HEAD_DIM, wide),
            o,
            lse,
        ]
        in_specs += [
            block,
            pl.BlockSpec((1, 1, HEAD_DIM, wide), lambda h: (0, h, 0, 0)),
            block,
            block,
            pl.BlockSpec((8, wide), lambda h: (0, 0)),
        ]
    return pl.pallas_call(
        functools.partial(join_kernel, len(parts)),
        grid=(heads,),
        in_specs=in_specs,
        out_specs=[pl.BlockSpec((1, HEAD_DIM, total), lambda h: (h, 0, 0)), pl.BlockSpec((16, total), lambda h: (0, 0))],
        out_shape=[jax.ShapeDtypeStruct((heads, HEAD_DIM, total), BF16), jax.ShapeDtypeStruct((16, total), F32)],
        compiler_params=params(),
        cost_estimate=cost(5),
        name="join",
    )(*args)


def to_slot(s, value_ref, outs):
    places = (outs[0], outs[2].at[0], outs[1], outs[2].at[1])
    for k in range(SLOTS):

        @pl.when(s == k)
        def _():
            places[k][...] = value_ref[...]


def add_to(first, ref, at, m, part):
    ref[at, m] = jnp.where(first, part, ref[at, m] + part)


def forward_kernel(info, x_ref, *refs):
    att_refs, refs = refs[:SLOTS], refs[SLOTS:]
    g_refs = refs[:SLOTS]
    wot, upt, wd, wdt, vec_ref = refs[SLOTS : SLOTS + 5]
    h_out, act_out, pg_out, g_out, n_out, root_out, sum_out, own_out = refs[-13:-5]
    layer_outs = refs[-5:-2]
    y1_s, layer_s = refs[-2:]
    s = pl.program_id(0)
    for k in range(SLOTS):

        @pl.when(s == k)
        def _():
            g_out[...] = g_refs[k][...]

    d = x_ref.shape[0]
    pieces = cuts(d, ROWS)
    att = jnp.concatenate([ref[...] for ref in att_refs], 0)
    total = 0.0
    for m in pieces:
        y1 = x_ref[m].astype(F32) + (dot(wot[m], att) + col(vec_ref, OUT_BIAS, m))
        y1_s[m] = y1
        total = total + jnp.sum(y1, axis=0, keepdims=True)
    mean = total * (1.0 / d)
    total = 0.0
    for m in pieces:
        center = y1_s[m] - mean
        total = total + jnp.sum(center * center, axis=0, keepdims=True)
    root = lax.rsqrt(total * (1.0 / d) + EPS)
    root_out[...] = jnp.broadcast_to(root, root_out.shape)
    for m in pieces:
        n = (y1_s[m] - mean) * root
        n_out[m] = n.astype(BF16)
        h_out[m] = (n * col(vec_ref, GAIN2, m) + col(vec_ref, SHIFT2, m)).astype(BF16)
    h = h_out[...]
    g = g_out[...]
    for m in cuts(upt.shape[0], ROWS):
        pre = dot(upt[m], h) + col(vec_ref, UP_BIAS, m)
        act_grad = dot(wd[m], g)
        square = pre * pre
        t = jnp.tanh(pre * (GELU_C + (GELU_C * GELU_A) * square))
        half = 0.5 * (1.0 + t)
        act_out[m] = (pre * half).astype(BF16)
        slope = half + (0.5 * pre) * (1.0 - t * t) * (GELU_C + (3.0 * GELU_C * GELU_A) * square)
        pg = (act_grad * slope).astype(BF16)
        pg_out[m] = pg
        add_to(s == 0, sum_out, 0, m, fold(pg.astype(F32)))
    act = act_out[...]
    for m in pieces:
        layer_s[m] = dot(wdt[m], act).astype(BF16)
    to_slot(s, layer_s, layer_outs)

    @pl.when(s == 0)
    def _():
        own_out[...] = y1_s[...]


def forward(chunk, info, atts, x, gs, wot, upt, wd, wdt, vec, carry):
    d, total = x.shape
    f = upt.shape[0]
    wide = SLOTS * BLK
    dev = 3 * (total // BLK)
    keep = lambda a: pl.BlockSpec(a.shape, lambda s, i: (0,) * a.ndim, pipeline_mode=pl.Buffered(1))
    block = lambda r: pl.BlockSpec((r, BLK), lambda s, i: (0, s))
    mine = pl.BlockSpec((d, BLK), lambda s, i: (0, chunk))
    args = [info, x, *atts, *gs, wot, upt, wd, wdt, vec]
    in_specs = [pl.BlockSpec((d, BLK), lambda s, i: (0, chunk * SLOTS + s))]
    in_specs += [pl.BlockSpec((atts[0].shape[0], BLK), lambda s, i: (0, s ^ i[dev]))] * SLOTS
    in_specs += [pl.BlockSpec((d, BLK), lambda s, i: (0, 0))] * SLOTS + [keep(a) for a in (wot, upt, wd, wdt, vec)]
    alias = {}
    if carry is not None:
        alias = {len(args) + n: 7 + n for n in range(len(carry))}
        in_specs += [pl.BlockSpec(memory_space=pl.ANY)] * len(carry)
        args += list(carry)
    spec = pltpu.PrefetchScalarGridSpec(
        num_scalar_prefetch=1,
        grid=(SLOTS,),
        in_specs=in_specs,
        out_specs=[
            block(d),
            block(f),
            block(f),
            block(d),
            block(d),
            block(8),
            pl.BlockSpec((1, f, 128), lambda s, i: (0, 0, 0)),
            mine,
            mine,
            mine,
            pl.BlockSpec((2, d, BLK), lambda s, i: (0, 0, chunk)),
        ],
        scratch_shapes=[pltpu.VMEM((d, BLK), F32), pltpu.VMEM((d, BLK), BF16)],
    )
    shape = jax.ShapeDtypeStruct
    rows = total // SLOTS
    return pl.pallas_call(
        forward_kernel,
        grid_spec=spec,
        out_shape=[
            shape((d, wide), BF16),
            shape((f, wide), BF16),
            shape((f, wide), BF16),
            shape((d, wide), BF16),
            shape((d, wide), BF16),
            shape((8, wide), F32),
            shape((1, f, 128), F32),
            shape((d, rows), F32),
            shape((d, rows), BF16),
            shape((d, rows), BF16),
            shape((2, d, rows), BF16),
        ],
        input_output_aliases=alias,
        compiler_params=params(),
        cost_estimate=cost(26),
        name="forward",
    )(*args)


def backward_kernel(info, pg_ref, n_ref, root_ref, g_ref, up, *refs):
    wo = refs[:SLOTS]
    vec_ref = refs[SLOTS]
    sum_out, attg0_out, attg2_out, attg_side = refs[-9:-5]
    attg_outs = (attg0_out, attg_side.at[0], attg2_out, attg_side.at[1])
    y1g_outs = refs[-5:-2]
    e_s, y1g_s = refs[-2:]
    s = pl.program_id(0)
    d = n_ref.shape[0]
    pieces = cuts(d, ROWS)
    pg = pg_ref[...]
    mean = 0.0
    tilt = 0.0
    for m in pieces:
        hg = dot(up[m], pg)
        n = n_ref[m].astype(F32)
        hn = hg * n
        gain = col(vec_ref, GAIN2, m)
        e = hg * gain
        e_s[m] = e
        mean = mean + jnp.sum(e, axis=0, keepdims=True)
        tilt = tilt + jnp.sum(hn * gain, axis=0, keepdims=True)
        add_to(s == 0, sum_out, 0, m, fold(hn))
        add_to(s == 0, sum_out, 1, m, fold(hg))
    mean = mean * (1.0 / d)
    tilt = tilt * (1.0 / d)
    root = root_ref[0:1]
    mine = jnp.where(s == 0, 1.0, 0.0)
    for m in pieces:
        y1g = root * (e_s[m] - mean - n_ref[m].astype(F32) * tilt) + g_ref[m].astype(F32) * mine
        y1g_s[m] = y1g.astype(BF16)
        add_to(s == 0, sum_out, 2, m, fold(y1g))
    y1b = y1g_s[...]
    for k in range(SLOTS):
        attg_outs[k][...] = dot(wo[k][...], y1b).astype(BF16)
    to_slot(s, y1g_s, y1g_outs)


def backward(chunk, info, pg, n, root, g, up, wos, vec, carry):
    d, wide = n.shape
    f = up.shape[1]
    rows = wos[0].shape[0]
    dev = info.shape[0] - 1
    keep = lambda a: pl.BlockSpec(a.shape, lambda s, i: (0,) * a.ndim, pipeline_mode=pl.Buffered(1))
    block = lambda r: pl.BlockSpec((r, BLK), lambda s, i: (0, s))
    mine = pl.BlockSpec((d, BLK), lambda s, i: (0, chunk))
    ordered = pl.BlockSpec((rows, BLK), lambda s, i: (0, s ^ i[dev]))
    args = [info, pg, n, root, g, up, *wos, vec]
    in_specs = [block(f), block(d), block(8), mine] + [keep(a) for a in (up, *wos, vec)]
    alias = {}
    if carry is not None:
        alias = {len(args) + n: 4 + n for n in range(len(carry))}
        in_specs += [pl.BlockSpec(memory_space=pl.ANY)] * len(carry)
        args += list(carry)
    spec = pltpu.PrefetchScalarGridSpec(
        num_scalar_prefetch=1,
        grid=(SLOTS,),
        in_specs=in_specs,
        out_specs=[
            pl.BlockSpec((3, d, 128), lambda s, i: (0, 0, 0)),
            ordered,
            ordered,
            pl.BlockSpec((2, rows, BLK), lambda s, i: (0, 0, s ^ i[dev])),
            mine,
            mine,
            pl.BlockSpec((2, d, BLK), lambda s, i: (0, 0, chunk)),
        ],
        scratch_shapes=[pltpu.VMEM((d, BLK), F32), pltpu.VMEM((d, BLK), BF16)],
    )
    shape = jax.ShapeDtypeStruct
    return pl.pallas_call(
        backward_kernel,
        grid_spec=spec,
        out_shape=[
            shape((3, d, 128), F32),
            shape((rows, wide), BF16),
            shape((rows, wide), BF16),
            shape((2, rows, wide), BF16),
            shape((d, g.shape[1]), BF16),
            shape((d, g.shape[1]), BF16),
            shape((2, d, g.shape[1]), BF16),
        ],
        input_output_aliases=alias,
        compiler_params=params(),
        cost_estimate=cost(17),
        name="backward",
    )(*args)


def shard_rows(m):
    return -(-m // (8 * 16)) * 16


def outer_kernel(count, order, with_sum, info, *refs):
    dp = info[0]
    i = pl.program_id(0)
    outs = refs[2 * count :]
    total = None
    for n in range(count):
        part = dot(refs[2 * n][...], refs[2 * n + 1][...], NT)
        total = part if total is None else total + part
    size = total.shape[0] // 2
    for half in range(2):
        slot = (2 * i) ^ (dp & 1) ^ half
        at = jnp.where((slot & order[2]) != 0, 1, 0) + jnp.where((slot & order[1]) != 0, 2, 0)
        rows = pl.ds(pl.multiple_of(at * size, size), size)
        value = total[half * size : (half + 1) * size].astype(BF16)
        goes = (slot & order[0]) != 0

        @pl.when(goes)
        def _():
            outs[1][rows] = value

        @pl.when(jnp.logical_not(goes))
        def _():
            outs[0][rows] = value

    if with_sum:
        outs[2][...] = fold(refs[0][...].astype(F32))


def outer(pairs, info, order, first=0, rows=None, with_sum=False):
    m, depth = pairs[0][0].shape
    n = pairs[0][1].shape[0]
    rows = m if rows is None else rows
    size = shard_rows(rows)
    skip = first // (2 * size)
    in_specs, args = [], []
    for a, b in pairs:
        in_specs.append(pl.BlockSpec((2 * size, depth), lambda i, s: (skip + (i ^ (s[0] >> 1)), 0)))
        in_specs.append(pl.BlockSpec((n, depth), lambda i, s: (0, 0), pipeline_mode=pl.Buffered(1)))
        args += [a, b]
    out_specs = [pl.BlockSpec((4 * size, n), lambda i, s: (0, 0))] * 2
    out_shape = [jax.ShapeDtypeStruct((4 * size, n), BF16)] * 2
    if with_sum:
        out_specs.append(pl.BlockSpec((2 * size, 128), lambda i, s: (i ^ (s[0] >> 1), 0)))
        out_shape.append(jax.ShapeDtypeStruct((8 * size, 128), F32))
    return pl.pallas_call(
        functools.partial(outer_kernel, len(pairs), order, with_sum),
        grid_spec=pltpu.PrefetchScalarGridSpec(num_scalar_prefetch=1, grid=(4,), in_specs=in_specs, out_specs=out_specs),
        out_shape=out_shape,
        compiler_params=params(),
        cost_estimate=cost(11),
        name="outer",
    )(info, *args)


def halve_kernel(keep_ref, recv_ref, keep_out, send_out):
    i = pl.program_id(0)
    total = (keep_ref[...].astype(F32) + recv_ref[...].astype(F32)).astype(BF16)

    @pl.when(i == 0)
    def _():
        keep_out[...] = total

    @pl.when(i == 1)
    def _():
        send_out[...] = total


def halve(keep, recv):
    size, n = keep.shape[0] // 2, keep.shape[1]
    block = pl.BlockSpec((size, n), lambda i: (i, 0))
    return pl.pallas_call(
        halve_kernel,
        grid=(2,),
        in_specs=[block, block],
        out_specs=[pl.BlockSpec((size, n), lambda i: (0, 0))] * 2,
        out_shape=[jax.ShapeDtypeStruct((size, n), BF16)] * 2,
        compiler_params=params(),
        cost_estimate=cost(2.5),
        name="halve",
    )(keep, recv)


def slot_of(i, order):
    return jnp.where(i & 1, order[2], 0) | jnp.where(i & 2, order[1], 0) | jnp.where(i & 4, order[0], 0)


def place_kernel(info, one, two, four, eight, *rest):
    i = pl.program_id(0)
    out = rest[-1]
    for ref, low, high in ((one, 0, 1), (two, 1, 2), (four, 2, 4), (eight, 4, 8)):

        @pl.when((i >= low) & (i < high))
        def _():
            out[...] = ref[...].astype(F32)


def place(parts, info, order, first, rows, carry):
    size, n = parts[0].shape
    start = first // size
    near = lambda at, many: pl.BlockSpec((size, n), lambda i, s: (jnp.clip(i - at, 0, many - 1), 0))
    in_specs = [near(0, 1), near(1, 1), near(2, 2), near(4, 4)]
    args = list(parts)
    alias = {}
    if carry is not None:
        in_specs.append(pl.BlockSpec(memory_space=pl.ANY))
        args.append(carry)
        alias = {5: 0}
    spec = pltpu.PrefetchScalarGridSpec(
        num_scalar_prefetch=1,
        grid=(8,),
        in_specs=in_specs,
        out_specs=pl.BlockSpec((size, n), lambda i, s: (start + (slot_of(i, order) ^ s[0]), 0)),
    )
    return pl.pallas_call(
        place_kernel,
        grid_spec=spec,
        out_shape=jax.ShapeDtypeStruct((rows, n), F32),
        input_output_aliases=alias,
        compiler_params=params(),
        cost_estimate=cost(6.5),
        name="place",
    )(info, *args)


def swap_dp(v, k):
    return lax.ppermute(v, "dp", [(i, i ^ k) for i in range(8)])


class CellSum:
    def __init__(self, line, keep, send, info, order, rows, first=0):
        self.line, self.keep, self.info, self.order = line, keep, info, order
        self.rows, self.first = rows, first
        self.stage = 0
        self.known = lax.axis_size("dp") == 8
        if not self.known:
            both = lax.psum(jnp.stack([keep, send]), "dp")
            size = keep.shape[0] // 4
            self.parts = [both[0, :size], both[0, size : 2 * size], both[0, 2 * size :], both[1]]
            self.got = both[1]
            return
        self.got = swap_dp(send, order[0])

    def step(self):
        if not self.known:
            return
        self.stage += 1
        k1, k2, k3 = self.order
        if self.stage < 3:
            self.keep, send = self.line(halve, self.keep, self.got)
            self.got = swap_dp(send, k2 if self.stage == 1 else k3)
        elif self.stage == 3:
            self.parts = [self.line(lambda a, b: add(BF16, a, b), self.keep, self.got)]
            self.got = swap_dp(self.parts[0], k3)
        else:
            self.parts.append(self.got)
            self.got = swap_dp(self.line(stack, *self.parts), k2 if self.stage == 4 else k1)
            if self.stage == 5:
                self.parts.append(self.got)

    def finish(self, carry=None):
        return self.line(
            lambda p, *c: place(p, self.info, self.order, self.first, self.rows, *(c or (None,))),
            self.parts,
            *([] if carry is None else [carry]),
        )


class Rounds:
    def __init__(self, line, v, over_tensor=False):
        self.line, self.v = line, v
        self.todo = [(swap_dp, 1), (swap_dp, 2), (swap_dp, 4)]
        if lax.axis_size("dp") != 8:
            self.v = lax.psum(v.astype(F32), "dp").astype(v.dtype)
            self.todo = []
        self.cells = self.v
        if over_tensor:
            self.todo += [(swap, 1), (swap, 2)]
        self.send()

    def send(self):
        self.got = None
        if self.todo:
            self.move, k = self.todo.pop(0)
            self.got = self.move(self.v, k)

    def step(self):
        if self.got is None:
            return
        self.v = self.line(lambda a, b: add(a.dtype, a, b), self.v, self.got)
        if self.move is swap_dp:
            self.cells = self.v
        self.send()


def out_grad_kernel(count, info, *refs):
    atts, y1gs, outs = refs[: count * SLOTS], refs[count * SLOTS : count * (SLOTS + 1)], refs[count * (SLOTS + 1) :]
    for k in range(SLOTS):
        total = None
        for n in range(count):
            part = dot(atts[n * SLOTS + k][...], y1gs[n][...], NT)
            total = part if total is None else total + part
        (outs[0], outs[2].at[0], outs[1], outs[2].at[1])[k][...] = total.astype(BF16)


def out_grad_call(info, atts, y1g):
    rows = atts[0][0].shape[0]
    d = y1g.shape[0]
    count = len(atts)
    dev = info.shape[0] - 1
    in_specs = [pl.BlockSpec((rows, BLK), lambda i, s: (0, s[dev]))] * (count * SLOTS)
    in_specs += [pl.BlockSpec((d, BLK), functools.partial(lambda at, i, s: (0, at), n)) for n in range(count)]
    spec = pltpu.PrefetchScalarGridSpec(
        num_scalar_prefetch=1,
        grid=(1,),
        in_specs=in_specs,
        out_specs=[pl.BlockSpec((rows, d), lambda i, s: (0, 0))] * 2 + [pl.BlockSpec((2, rows, d), lambda i, s: (0, 0, 0))],
    )
    return pl.pallas_call(
        functools.partial(out_grad_kernel, count),
        grid_spec=spec,
        out_shape=[jax.ShapeDtypeStruct((rows, d), BF16)] * 2 + [jax.ShapeDtypeStruct((2, rows, d), BF16)],
        compiler_params=params(),
        cost_estimate=cost(5),
        name="out_grad_call",
    )(info, *[a for chunk in atts for a in chunk], *[y1g] * count)


def h1_grad_kernel(w_ref, dqkv_ref, x_ref, sum_ref, *outs):
    s = pl.program_id(1)
    first = (s == 0) & (pl.program_id(0) == 0)
    hg_s = outs[-1]
    d = x_ref.shape[0]
    pieces = cuts(d, ROWS)
    total = 0.0
    for m in pieces:
        total = total + jnp.sum(x_ref[m].astype(F32), axis=0, keepdims=True)
    mean = total * (1.0 / d)
    total = 0.0
    for m in pieces:
        center = x_ref[m].astype(F32) - mean
        total = total + jnp.sum(center * center, axis=0, keepdims=True)
    root = lax.rsqrt(total * (1.0 / d) + EPS)
    dqkv = dqkv_ref[...]
    for m in pieces:
        hg = dot(w_ref[m], dqkv)
        n = (x_ref[m].astype(F32) - mean) * root
        hg_s[m] = hg.astype(BF16)
        add_to(first, sum_ref, 0, m, fold(hg * n))
        add_to(first, sum_ref, 1, m, fold(hg))
    to_slot(s, hg_s, outs[:3])


def h1_grad_call(w, dqkv, x):
    d, total = x.shape
    per = total // (BLK * SLOTS)
    m = w.shape[1]
    at = lambda p, s: (0, p * SLOTS + s)
    mine = pl.BlockSpec((d, BLK), lambda p, s: (0, p))
    side = pl.BlockSpec((2, d, BLK), lambda p, s: (0, 0, p))
    return pl.pallas_call(
        h1_grad_kernel,
        grid=(per, SLOTS),
        in_specs=[
            pl.BlockSpec((d, m), lambda p, s: (0, 0), pipeline_mode=pl.Buffered(1)),
            pl.BlockSpec((m, BLK), at),
            pl.BlockSpec((d, BLK), at),
        ],
        out_specs=[pl.BlockSpec((2, d, 128), lambda p, s: (0, 0, 0)), mine, mine, side],
        out_shape=[jax.ShapeDtypeStruct((2, d, 128), F32)]
        + [jax.ShapeDtypeStruct((d, per * BLK), BF16)] * 2
        + [jax.ShapeDtypeStruct((2, d, per * BLK), BF16)],
        scratch_shapes=[pltpu.VMEM((d, BLK), BF16)],
        compiler_params=params(),
        cost_estimate=cost(13),
        name="h1_grad_call",
    )(w, dqkv, x)


def input_grad_kernel(x_ref, a_ref, b_ref, y1g_ref, gain_ref, out_ref):
    n, root = normal(x_ref[...].astype(F32))
    e = (a_ref[...] + b_ref[...].astype(F32)) * gain_ref[:, GAIN1 : GAIN1 + 1]
    e = root * (e - jnp.mean(e, axis=0, keepdims=True) - n * jnp.mean(e * n, axis=0, keepdims=True))
    out_ref[...] = (y1g_ref[...] + e).astype(BF16)


def input_grad_call(x, a, b, y1g, gain):
    d, rows = x.shape
    block = pl.BlockSpec((d, 128), lambda i: (0, i))
    return pl.pallas_call(
        input_grad_kernel,
        grid=(rows // 128,),
        in_specs=[block] * 4 + [pl.BlockSpec(gain.shape, lambda i: (0, 0))],
        out_specs=block,
        out_shape=jax.ShapeDtypeStruct((d, rows), BF16),
        compiler_params=params(),
        cost_estimate=cost(6),
        name="input_grad_call",
    )(x, a, b, y1g, gain)


def swap(v, k):
    return lax.ppermute(v, "tensor", [(i, i ^ k) for i in range(SLOTS)])


def after(v, *done):
    return lax.optimization_barrier((v, done))[0]


class Line:
    def __init__(self):
        self.last = []

    def __call__(self, step, *args):
        args, _ = lax.optimization_barrier((args, self.last))
        out = step(*args)
        self.last = jax.tree.leaves(out)
        return out

    def wait(self, *values):
        self.last = self.last + jax.tree.leaves(values)

    def pin(self, v, *also):
        return after(v, self.last, also)


class Gather:
    def __init__(self, v):
        self.own, self.side, self.across = v, swap(v, 1), swap(v, 2)

    def finish(self, line):
        self.corner = swap(line.pin(self.across), 1)
        return self

    def all(self):
        return self.own, self.side, self.across, self.corner


def plus(a, b):
    return a.astype(F32) + b.astype(F32)


def plus_low(a, b):
    return plus(a, b).astype(BF16)


def add_kernel(*refs):
    total = None
    for ref in refs[:-1]:
        v = (ref[0] if len(ref.shape) == 3 else ref[...]).astype(F32)
        total = v if total is None else total + v
    refs[-1][...] = total.astype(refs[-1].dtype)


def add(dtype, *terms):
    rows, columns = terms[0].shape
    size = rows // 2 if rows % 32 == 0 and rows * columns > 1 << 18 else rows
    in_specs, args = [], []
    for term in terms:
        if isinstance(term, tuple):
            in_specs.append(pl.BlockSpec((1, size, columns), functools.partial(lambda at, i: (at, i, 0), term[1])))
            args.append(term[0])
        else:
            in_specs.append(pl.BlockSpec((size, columns), lambda i: (i, 0)))
            args.append(term)
    return pl.pallas_call(
        add_kernel,
        grid=(rows // size,),
        in_specs=in_specs,
        out_specs=pl.BlockSpec((size, columns), lambda i: (i, 0)),
        out_shape=jax.ShapeDtypeStruct((rows, columns), dtype),
        compiler_params=params(),
        cost_estimate=cost(2.3),
        name="add",
    )(*args)


def plus_second(a, pair):
    return add(BF16, a, (pair, 1))


def plus_first(a, pair, far, dtype=F32):
    return add(dtype, a, (pair, 0), far)


def stack_kernel(*refs):
    at = 0
    for ref in refs[:-1]:
        refs[-1][at : at + ref.shape[0]] = ref[...]
        at += ref.shape[0]


def stack(*parts):
    return pl.pallas_call(
        stack_kernel,
        out_shape=jax.ShapeDtypeStruct((sum(p.shape[0] for p in parts), parts[0].shape[1]), parts[0].dtype),
        compiler_params=params(),
        cost_estimate=cost(2),
        name="stack",
    )(*parts)


def token_starts(lengths, offsets, total, dev):
    pos = jnp.arange(total, dtype=jnp.int32)[:, None]
    inside = (pos >= offsets[None]) & (pos < (offsets + lengths)[None])
    first = jnp.max(jnp.where(inside, offsets[None], -1), axis=1)
    start = jnp.where(first >= 0, first, pos[:, 0])
    nb = total // BLK
    per = nb // SLOTS
    b = jnp.arange(nb, dtype=jnp.int32)
    first_key = start.reshape(nb, BLK)[:, 0] // BLK
    place = (b % per) * SLOTS + ((b // per) ^ dev)
    last_query = jnp.max(jnp.where(first_key[None, :] <= b[:, None], b[None, :], 0), axis=1)
    info = jnp.concatenate([first_key, place, last_query, jnp.full((1,), dev)])
    return start[None], info.astype(jnp.int32)


def body(
    tokens,
    cotangent,
    ln1_gain,
    ln1_bias,
    attn_weight,
    qv_bias,
    out_weight,
    out_bias,
    ln2_gain,
    ln2_bias,
    up_weight,
    up_bias,
    down_weight,
    down_bias,
    cell_lengths,
    cell_offsets,
):
    rows, d = tokens.shape
    width = attn_weight.shape[2]
    heads = width // HEAD_DIM
    total = rows * SLOTS
    per = rows // BLK
    dev = lax.axis_index("tensor")
    start, info = token_starts(cell_lengths[0], cell_offsets[0], total, dev)

    whole_dp = lax.axis_size("dp") == 8
    dp_info = jnp.full((1,), lax.axis_index("dp") if whole_dp else 0, jnp.int32)

    line = Line()
    x_own = tokens.T
    g_own = cotangent.T
    x_go = Gather(x_own)

    w_in = attn_weight.transpose(1, 2, 0)
    zero = jnp.zeros_like(ln1_gain)
    rows8 = jnp.stack([ln1_gain, ln1_bias, out_bias, ln2_gain, ln2_bias, up_bias, down_bias, zero])
    bias8 = jnp.zeros((8, width), F32).at[0].set(qv_bias[0]).at[2].set(qv_bias[1])
    upt, wdt, w_back, vec, bias, *g_cuts = line(
        turn, g_own, up_weight, down_weight, w_in.reshape(3 * width, d), rows8, bias8
    )
    carry = line(lambda a, b: qkv_call(0, a, b, w_in, vec, bias, None), x_own, x_go.side)
    wo_go = Gather(line.pin(out_weight, x_go.across))
    x_parts = x_go.finish(line).all()
    x_all, h1, qkv, kn, vn = line(lambda a, b, c: qkv_call(1, a, b, w_in, vec, bias, c), x_parts[2], x_parts[3], carry)
    chunks = range(per)
    g_go = [Gather(line.pin(g_cuts[0]))]
    fronts, att_go = [], []
    for c in chunks:
        fronts.append(line(functools.partial(attend, c), info, start, qkv, kn))
        att_go.append(Gather(fronts[c][0].reshape(width, SLOTS * BLK)))
        if c == 0:
            wo_parts = wo_go.finish(line).all()
    wot = line(turn_pieces, *wo_parts)
    g_parts = [g_go[0].finish(line).all()]
    atts, ahead = [], []
    for c in chunks:
        atts.append(att_go[c].finish(line).all())
        if c > 0:
            g_parts.append(g_go[c].finish(line).all())
        if c + 1 < per:
            g_go.append(Gather(line.pin(g_cuts[c + 1], atts[c][2])))
        ahead.append(
            line(
                functools.partial(forward, c),
                info,
                atts[c],
                x_all,
                g_parts[c],
                wot,
                upt,
                down_weight,
                wdt,
                vec,
                ahead[-1][7:] if c else None,
            )
        )
    h2s, acts, pgs, gs, ns, roots, up_sums = zip(*[m[:7] for m in ahead])
    own, layer0, layer2, layer13 = ahead[-1][7:]
    layer_near = swap(layer13, 1)
    flat = lambda a, b: list(zip(a, b))
    y_first, z_first = (1, 2, 4), (2, 1, 4)
    f = down_weight.shape[0]
    down = CellSum(line, *line(lambda a, b: outer(flat(a, b), dp_info, y_first), acts, gs), dp_info, y_first, f)
    layer_far = swap(line(plus_second, layer2, layer_near), 2)
    up = CellSum(line, *line(lambda a, b: outer(flat(a, b), dp_info, z_first), h2s, pgs), dp_info, z_first, d)

    back, attgs = [], []
    for c in chunks:
        carry = back[-1][4:] if c else None
        back.append(
            line(functools.partial(backward, c), info, pgs[c], ns[c], roots[c], g_own, up_weight, wo_parts, vec, carry)
        )
        attg0, attg2, attg13 = back[c][1:4]
        line.wait(attgs[-1][2] if c else layer_far)
        near = swap(line.pin(attg13), 1)
        (up if c else down).step()
        attgs.append((attg0, near, swap(line(plus_second, attg2, near), 2)))
    y1g0, y1g2, y1g13 = back[-1][4:]
    y1_near = swap(line.pin(y1g13), 1)
    down.step()
    y1_far = swap(line(plus_second, y1g2, y1_near), 2)
    do, stat = line(join, [a + tuple(f) for a, f in zip(attgs, fronts)])
    dqkv = line(attend_back, info, start, qkv, kn, vn, do, stat).reshape(3 * width, total)
    down.step()
    up.step()
    line.wait(y1_far)
    attn_parts = line(lambda a, b: outer([(a, b)], dp_info, y_first, with_sum=True), dqkv, h1)
    attn = CellSum(line, *attn_parts[:2], dp_info, y_first, 3 * width)
    down.step()
    up.step()
    sum1, h10, h12, h113 = line(h1_grad_call, w_back, dqkv, x_all)
    h1_near = swap(line.pin(h113), 1)
    down.step()
    up.step()
    h1_far = swap(line(plus_second, h12, h1_near), 2)
    attn.step()
    y1_grad = line(plus_first, y1g0, y1_near, y1_far)
    out0, out2, out13 = line(lambda a, y: out_grad_call(info, a, y.astype(BF16)), atts, y1_grad)

    def smalls(sum1, sums, up_sums, qkv_sum, g):
        sum1 = jnp.sum(sum1, axis=2)
        sum2 = jnp.sum(sum(sums), axis=2)
        up_row = jnp.sum(sum(up_sums), axis=2)
        qkv_sum = jnp.sum(qkv_sum[: 3 * width], axis=1).reshape(3, width)
        down_row = jnp.sum(g.astype(F32), axis=1)
        qv_row = jnp.pad(jnp.concatenate([qkv_sum[0], qkv_sum[2]]), (0, d - 2 * width))
        return jnp.concatenate([sum1, sum2, down_row[None], up_row, qv_row[None]], 0)

    small = line(smalls, sum1, [m[0] for m in back], up_sums, attn_parts[2], g_own)
    up.step()
    attn.step()
    layer = line(
        lambda own, a, near, far: (own + plus_first(a, near, far) + down_bias[:, None]).astype(BF16),
        own,
        layer0,
        layer_near,
        layer_far,
    )
    near = line(lambda a, b: add(F32, a, (b, 0)), h10, h1_near)
    line.wait(h1_far, down.got)
    out_near = swap(line.pin(out13), 1)
    attn.step()
    out_far = swap(line(plus_second, out2, out_near), 2)
    down_grad = down.finish()
    line.wait(out_far)
    small = Rounds(line, line.pin(small), True)
    input_grad = line(input_grad_call, x_own, near, h1_far, y1_grad, vec)
    attn.step()
    small.step()
    line.wait(up.got)
    out_sum = Rounds(line, line(lambda a, b, c: plus_first(a, b, c, BF16), out0, out_near, out_far))
    small.step()
    up_grad = up.finish()
    out_sum.step()
    attn.step()
    small.step()
    out_sum.step()
    small.step()
    out_sum.step()
    small.step()
    out_grad = line(lambda v: v.astype(F32), out_sum.v)
    attn_grad = attn.finish()
    small, own_small = small.v, small.cells[6:]
    return (
        layer.T,
        input_grad.T,
        small[0],
        small[1],
        attn_grad.reshape(3, width, d).transpose(2, 0, 1),
        own_small[1, : 2 * width].reshape(2, width),
        out_grad,
        small[4],
        small[2],
        small[3],
        up_grad,
        own_small[0],
        down_grad,
        small[5],
    )


def solution(mesh):
    rows = P(("dp", "tensor"), None)
    in_specs = (
        rows,
        rows,
        P(),
        P(),
        P(None, None, "tensor"),
        P(None, "tensor"),
        P("tensor", None),
        P(),
        P(),
        P(),
        P(None, "tensor"),
        P("tensor"),
        P("tensor", None),
        P(),
        P("dp", None),
        P("dp", None),
    )
    out_specs = (
        rows,
        rows,
        P(),
        P(),
        P(None, None, "tensor"),
        P(None, "tensor"),
        P("tensor", None),
        P(),
        P(),
        P(),
        P(None, "tensor"),
        P("tensor"),
        P("tensor", None),
        P(),
    )
    return jax.shard_map(body, mesh=mesh, in_specs=in_specs, out_specs=out_specs, check_vma=False)
```

```python
import functools
import math

import jax
import jax.numpy as jnp
from jax import lax
from jax.experimental import pallas as pl
from jax.experimental.pallas import tpu as pltpu
from jax.sharding import PartitionSpec as P


HEAD_DIM = 56
BLK = 256
SLOTS = 4
NEG = -1e30
EPS = 1e-05
SCALE = 1.0 / math.sqrt(HEAD_DIM)
SCALE2 = SCALE * math.log2(math.e)
GELU_C = math.sqrt(2.0 / math.pi)
GELU_A = 0.044715
F32 = jnp.float32
BF16 = jnp.bfloat16
NT = ((1,), (1,))
ROWS = 224
GAIN1, SHIFT1, OUT_BIAS, GAIN2, SHIFT2, UP_BIAS, DOWN_BIAS = range(7)
VEC8 = True
ATT_PIECES = True
VMEM = 60 << 20
PACE = 0.0


def dot(a, b, dims=((1,), (0,))):
    return lax.dot_general(a, b, (dims, ((), ())), preferred_element_type=F32)


def params():
    return pltpu.CompilerParams(vmem_limit_bytes=VMEM)


def cost(microseconds):
    return pl.CostEstimate(flops=max(1, int(microseconds * PACE)), bytes_accessed=1, transcendentals=0)


def fold(v):
    total = v[:, :128]
    for at in range(128, v.shape[1], 128):
        total = total + v[:, at : at + 128]
    return total


def normal(x):
    center = x - jnp.mean(x, axis=0, keepdims=True)
    root = lax.rsqrt(jnp.mean(center * center, axis=0, keepdims=True) + EPS)
    return center * root, root


def turn_kernel(count, parts, *refs):
    for n in range(count):
        refs[count + 1 + n][...] = refs[n][...].T
    for n in range(parts):
        refs[2 * count + 1 + n][...] = refs[count][:, n * BLK : (n + 1) * BLK]


def turn(cut, *arrays):
    wide = max(a.shape[1] for a in arrays)
    steps = -(-wide // 256)
    in_specs, out_specs, outs = [], [], []
    for a in arrays:
        rows, columns = a.shape
        if columns == wide:
            in_specs.append(pl.BlockSpec((rows, 256), lambda i: (0, i)))
            out_specs.append(pl.BlockSpec((256, rows), lambda i: (i, 0)))
        else:
            in_specs.append(pl.BlockSpec((rows, columns), lambda i: (0, 0)))
            out_specs.append(pl.BlockSpec((columns, rows), lambda i: (0, 0)))
        outs.append(jax.ShapeDtypeStruct((columns, rows), a.dtype))
    rows, columns = cut.shape
    parts = columns // BLK
    size = -(-rows // (16 * steps)) * 16
    in_specs.append(pl.BlockSpec((size, columns), lambda i: (i, 0)))
    out_specs += [pl.BlockSpec((size, BLK), lambda i: (i, 0))] * parts
    outs += [jax.ShapeDtypeStruct((rows, BLK), cut.dtype)] * parts
    return pl.pallas_call(
        functools.partial(turn_kernel, len(arrays), parts),
        grid=(steps,),
        in_specs=in_specs,
        out_specs=out_specs,
        out_shape=outs,
        compiler_params=params(),
        cost_estimate=cost(8),
        name="turn",
    )(*arrays, cut)


def turn_pieces_kernel(*refs):
    refs[-1][...] = jnp.concatenate([ref[...] for ref in refs[:-1]], 0).T


def turn_pieces(*pieces):
    rows, columns = pieces[0].shape
    return pl.pallas_call(
        turn_pieces_kernel,
        grid=(-(-columns // 256),),
        in_specs=[pl.BlockSpec((rows, 256), lambda i: (0, i))] * len(pieces),
        out_specs=pl.BlockSpec((256, rows * len(pieces)), lambda i: (i, 0)),
        out_shape=jax.ShapeDtypeStruct((columns, rows * len(pieces)), pieces[0].dtype),
        compiler_params=params(),
        cost_estimate=cost(5),
        name="turn_pieces",
    )(*pieces)


def col(ref, at, m):
    return ref[m, at : at + 1]


def cuts(total, size):
    return [slice(at, min(at + size, total)) for at in range(0, total, size)]


def qkv_kernel(heads, a_ref, b_ref, w_ref, vec_ref, bias_ref, *rest):
    x_out, h_out, q_out, kn_out, vn_out = rest[-5:]
    x_out[:, :BLK] = a_ref[...]
    x_out[:, BLK:] = b_ref[...]
    d = x_out.shape[0]
    pieces = cuts(d, ROWS)
    total = 0.0
    for m in pieces:
        total = total + jnp.sum(x_out[m].astype(F32), axis=0, keepdims=True)
    mean = total * (1.0 / d)
    total = 0.0
    for m in pieces:
        center = x_out[m].astype(F32) - mean
        total = total + jnp.sum(center * center, axis=0, keepdims=True)
    root = lax.rsqrt(total * (1.0 / d) + EPS)
    for m in pieces:
        n = (x_out[m].astype(F32) - mean) * root
        h_out[m] = (n * col(vec_ref, GAIN1, m) + col(vec_ref, SHIFT1, m)).astype(BF16)
    h = h_out[...]
    for part in range(3):
        r = (dot(w_ref[part], h) + bias_ref[:, part : part + 1]).astype(BF16)
        r = r.reshape(heads, HEAD_DIM, r.shape[1])
        q_out[part * heads : (part + 1) * heads] = r
        if part > 0:
            out = kn_out if part == 1 else vn_out
            for h_at in range(heads):
                out[h_at] = r[h_at].T


def qkv_call(pair, a, b, w, vec, bias, carry):
    d, rows = a.shape
    per = rows // BLK
    total = rows * SLOTS
    heads = w.shape[1] // HEAD_DIM
    wide = 2 * BLK
    outs = [
        jax.ShapeDtypeStruct((d, total), BF16),
        jax.ShapeDtypeStruct((d, total), BF16),
        jax.ShapeDtypeStruct((3 * heads, HEAD_DIM, total), BF16),
        jax.ShapeDtypeStruct((heads, total, HEAD_DIM), BF16),
        jax.ShapeDtypeStruct((heads, total, HEAD_DIM), BF16),
    ]
    at = lambda p: p * (SLOTS // 2) + pair
    in_specs = [
        pl.BlockSpec((d, BLK), lambda p: (0, p)),
        pl.BlockSpec((d, BLK), lambda p: (0, p)),
        pl.BlockSpec(w.shape, lambda p: (0, 0, 0)),
        pl.BlockSpec(vec.shape, lambda p: (0, 0)),
        pl.BlockSpec(bias.shape, lambda p: (0, 0)),
    ]
    args = [a, b, w, vec, bias]
    alias = {}
    if carry is not None:
        alias = {len(args) + n: n for n in range(len(outs))}
        in_specs += [pl.BlockSpec(memory_space=pl.ANY)] * len(outs)
        args += list(carry)
    return pl.pallas_call(
        functools.partial(qkv_kernel, heads),
        grid=(per,),
        in_specs=in_specs,
        out_specs=[
            pl.BlockSpec((d, wide), lambda p: (0, at(p))),
            pl.BlockSpec((d, wide), lambda p: (0, at(p))),
            pl.BlockSpec((3 * heads, HEAD_DIM, wide), lambda p: (0, 0, at(p))),
            pl.BlockSpec((heads, wide, HEAD_DIM), lambda p: (0, at(p), 0)),
            pl.BlockSpec((heads, wide, HEAD_DIM), lambda p: (0, at(p), 0)),
        ],
        out_shape=outs,
        input_output_aliases=alias,
        compiler_params=params(),
        cost_estimate=cost(8),
        name="qkv_call",
    )(*args)


def attend_kernel(heads, nb, per, chunk, info, start_ref, q_ref, kn_ref, v_ref, o_ref, lse_ref, acc, m_s, l_s):
    b = pl.program_id(0) * per + chunk

    def visit(kb, diag):
        at = pl.multiple_of(info[nb + kb] * BLK, BLK)
        kpos = lax.broadcasted_iota(jnp.int32, (BLK, BLK), 0)
        ok = kpos >= (start_ref[...] - kb * BLK)
        if diag:
            ok = ok & (kpos <= lax.broadcasted_iota(jnp.int32, (BLK, BLK), 1))
        scores = [dot(kn_ref[h, pl.ds(at, BLK), :], q_ref[h]) for h in range(heads)]
        scores = [jnp.where(ok, s, NEG) for s in scores]
        top = jnp.concatenate([jnp.max(s, axis=0, keepdims=True) for s in scores], 0)
        if not diag:
            old = m_s[0:heads, :]
            top = jnp.maximum(old, top)
            fade = jnp.exp2((old - top) * SCALE2)
        m_s[0:heads, :] = top
        expo = [jnp.exp2((scores[h] - top[h : h + 1]) * SCALE2) for h in range(heads)]
        sums = jnp.concatenate([jnp.sum(e, axis=0, keepdims=True) for e in expo], 0)
        l_s[0:heads, :] = sums if diag else l_s[0:heads, :] * fade + sums
        for h in range(heads):
            new = dot(v_ref[h, :, pl.ds(at, BLK)], expo[h].astype(BF16))
            acc[h] = new if diag else acc[h] * fade[h : h + 1] + new

    visit(b, True)

    def step(kb, _):
        visit(kb, False)
        return 0

    lax.fori_loop(info[b], b, step, 0)
    for h in range(heads):
        total = l_s[h : h + 1, :]
        o_ref[h] = (acc[h] * (1.0 / total)).astype(BF16)
        lse_ref[h : h + 1, :] = m_s[h : h + 1, :] * SCALE2 + jnp.log2(total)


def attend(chunk, info, start, qkv, kn):
    heads, total = qkv.shape[0] // 3, qkv.shape[2]
    nb = total // BLK
    per = nb // SLOTS
    spec = pltpu.PrefetchScalarGridSpec(
        num_scalar_prefetch=1,
        grid=(SLOTS,),
        in_specs=[
            pl.BlockSpec((1, BLK), lambda i, s: (0, i * per + chunk)),
            pl.BlockSpec((heads, HEAD_DIM, BLK), lambda i, s: (0, 0, s[nb + i * per + chunk])),
            pl.BlockSpec((heads, total, HEAD_DIM), lambda i, s: (0, 0, 0)),
            pl.BlockSpec((heads, HEAD_DIM, total), lambda i, s: (2, 0, 0)),
        ],
        out_specs=[
            pl.BlockSpec((heads, HEAD_DIM, BLK), lambda i, s: (0, 0, i)),
            pl.BlockSpec((8, BLK), lambda i, s: (0, i)),
        ],
        scratch_shapes=[
            pltpu.VMEM((heads, HEAD_DIM, BLK), F32),
            pltpu.VMEM((8, BLK), F32),
            pltpu.VMEM((8, BLK), F32),
        ],
    )
    return pl.pallas_call(
        functools.partial(attend_kernel, heads, nb, per, chunk),
        grid_spec=spec,
        out_shape=[
            jax.ShapeDtypeStruct((heads, HEAD_DIM, SLOTS * BLK), BF16),
            jax.ShapeDtypeStruct((8, SLOTS * BLK), F32),
        ],
        compiler_params=params(),
        cost_estimate=cost(9.5),
        name="attend",
    )(info, start, qkv, kn, qkv)


def attend_back_kernel(heads, nb, per, info, start_ref, q_ref, k_ref, kn_ref, vn_ref, do_ref, stat_ref, out_ref, dq_s, dk_s, dv_s):
    j = pl.program_id(0)

    def place(b):
        return pl.multiple_of(info[nb + b] * BLK, BLK)

    def ordered(b):
        return pl.multiple_of(((b % per) * SLOTS + b // per) * BLK, BLK)

    @pl.when(j == 0)
    def _():
        dq_s[...] = jnp.zeros_like(dq_s)

    def visit(b, diag):
        at = place(b)
        mine = ordered(b)
        kpos = lax.broadcasted_iota(jnp.int32, (BLK, BLK), 0)
        ok = kpos >= (start_ref[:, pl.ds(pl.multiple_of(b * BLK, BLK), BLK)] - j * BLK)
        if diag:
            ok = ok & (kpos <= lax.broadcasted_iota(jnp.int32, (BLK, BLK), 1))
        every = range(heads)
        query = [q_ref[h, :, pl.ds(at, BLK)] for h in every]
        grad = [do_ref[h, :, pl.ds(mine, BLK)] for h in every]
        scores = [dot(kn_ref[h], query[h]) for h in every]
        prob_grad = [dot(vn_ref[h], grad[h]) for h in every]
        probs = [
            jnp.where(ok, jnp.exp2(scores[h] * SCALE2 - stat_ref[h : h + 1, pl.ds(mine, BLK)]), 0.0) for h in every
        ]
        score_grad = [
            (probs[h] * (prob_grad[h] - stat_ref[8 + h : 9 + h, pl.ds(mine, BLK)])).astype(BF16) for h in every
        ]
        dv = [dot(grad[h], probs[h].astype(BF16), NT) for h in every]
        dk = [dot(query[h], score_grad[h], NT) for h in every]
        dq = [dot(k_ref[h], score_grad[h]) for h in every]
        for h in every:
            if diag:
                dv_s[h] = dv[h]
                dk_s[h] = dk[h]
            else:
                dv_s[h] += dv[h]
                dk_s[h] += dk[h]
            dq_s[h, :, pl.ds(at, BLK)] += dq[h]

    visit(j, True)

    def step(b, _):
        visit(b, False)
        return 0

    lax.fori_loop(j + 1, info[2 * nb + j] + 1, step, 0)
    at = place(j)
    for h in range(heads):
        out_ref[h] = (dq_s[h, :, pl.ds(at, BLK)] * SCALE).astype(BF16)
        out_ref[heads + h] = (dk_s[h] * SCALE).astype(BF16)
        out_ref[2 * heads + h] = dv_s[h].astype(BF16)


def attend_back(info, start, qkv, kn, vn, do, stat):
    heads, total = qkv.shape[0] // 3, qkv.shape[2]
    nb = total // BLK
    per = nb // SLOTS
    whole = pl.BlockSpec((heads, HEAD_DIM, total), lambda j, s: (0, 0, 0))
    block = lambda a: pl.BlockSpec((heads, HEAD_DIM, BLK), lambda j, s: (a, 0, s[nb + j]))
    tall = pl.BlockSpec((heads, BLK, HEAD_DIM), lambda j, s: (0, s[nb + j], 0))
    spec = pltpu.PrefetchScalarGridSpec(
        num_scalar_prefetch=1,
        grid=(nb,),
        in_specs=[
            pl.BlockSpec((1, total), lambda j, s: (0, 0)),
            whole,
            block(1),
            tall,
            tall,
            whole,
            pl.BlockSpec((16, total), lambda j, s: (0, 0)),
        ],
        out_specs=pl.BlockSpec((3 * heads, HEAD_DIM, BLK), lambda j, s: (0, 0, s[nb + j])),
        scratch_shapes=[
            pltpu.VMEM((heads, HEAD_DIM, total), F32),
            pltpu.VMEM((heads, HEAD_DIM, BLK), F32),
            pltpu.VMEM((heads, HEAD_DIM, BLK), F32),
        ],
    )
    return pl.pallas_call(
        functools.partial(attend_back_kernel, heads, nb, per),
        grid_spec=spec,
        out_shape=jax.ShapeDtypeStruct((3 * heads, HEAD_DIM, total), BF16),
        compiler_params=params(),
        cost_estimate=cost(20),
        name="attend_back",
    )(info, start, qkv, qkv, kn, vn, do, stat)


def join_kernel(chunks, *refs):
    do_out, stat_out = refs[-2:]
    h = pl.program_id(0)
    wide = SLOTS * BLK
    for c in range(chunks):
        a, near, far, o, lse = refs[5 * c : 5 * c + 5]
        cut = slice(c * wide, (c + 1) * wide)
        do = (a[0].astype(F32) + near[0].astype(F32) + far[0].astype(F32)).astype(BF16)
        do_out[0, :, cut] = do
        stat_out[pl.ds(h + 8, 1), cut] = jnp.sum(o[0].astype(F32) * do.astype(F32), axis=0, keepdims=True)

        @pl.when(h == 0)
        def _():
            stat_out[0:8, cut] = lse[...]


def join(parts):
    heads, _, wide = parts[0][3].shape
    total = wide * len(parts)
    in_specs, args = [], []
    block = pl.BlockSpec((1, HEAD_DIM, wide), lambda h: (h, 0, 0))
    for a, near, far, o, lse in parts:
        args += [
            a.reshape(heads, HEAD_DIM, wide),
            near.reshape(heads, HEAD_DIM, wide),
            far.reshape(heads, HEAD_DIM, wide),
            o,
            lse,
        ]
        in_specs += [
            block,
            block,
            block,
            block,
            pl.BlockSpec((8, wide), lambda h: (0, 0)),
        ]
    return pl.pallas_call(
        functools.partial(join_kernel, len(parts)),
        grid=(heads,),
        in_specs=in_specs,
        out_specs=[pl.BlockSpec((1, HEAD_DIM, total), lambda h: (h, 0, 0)), pl.BlockSpec((16, total), lambda h: (0, 0))],
        out_shape=[jax.ShapeDtypeStruct((heads, HEAD_DIM, total), BF16), jax.ShapeDtypeStruct((16, total), F32)],
        compiler_params=params(),
        cost_estimate=cost(5),
        name="join",
    )(*args)


def to_slot(s, value_ref, outs):
    for k in range(SLOTS):

        @pl.when(s == k)
        def _():
            outs[k][...] = value_ref[...]


def add_to(first, ref, at, m, part):
    ref[at, m] = jnp.where(first, part, ref[at, m] + part)


def forward_kernel(info, x_ref, *refs):
    att_refs, refs = refs[:SLOTS], refs[SLOTS:]
    g_refs = refs[:SLOTS]
    wot, upt, wd, wdt, vec_ref = refs[SLOTS : SLOTS + 5]
    h_out, act_out, pg_out, g_out, n_out, root_out, sum_out, own_out = refs[-14:-6]
    layer_outs = refs[-6:-2]
    y1_s, layer_s = refs[-2:]
    s = pl.program_id(0)
    for k in range(SLOTS):

        @pl.when(s == k)
        def _():
            g_out[...] = g_refs[k][...]

    d = x_ref.shape[0]
    pieces = cuts(d, ROWS)
    att = jnp.concatenate([ref[...] for ref in att_refs], 0)
    total = 0.0
    for m in pieces:
        y1 = x_ref[m].astype(F32) + (dot(wot[m], att) + col(vec_ref, OUT_BIAS, m))
        y1_s[m] = y1
        total = total + jnp.sum(y1, axis=0, keepdims=True)
    mean = total * (1.0 / d)
    total = 0.0
    for m in pieces:
        center = y1_s[m] - mean
        total = total + jnp.sum(center * center, axis=0, keepdims=True)
    root = lax.rsqrt(total * (1.0 / d) + EPS)
    root_out[...] = jnp.broadcast_to(root, root_out.shape)
    for m in pieces:
        n = (y1_s[m] - mean) * root
        n_out[m] = n.astype(BF16)
        h_out[m] = (n * col(vec_ref, GAIN2, m) + col(vec_ref, SHIFT2, m)).astype(BF16)
    h = h_out[...]
    g = g_out[...]
    for m in cuts(upt.shape[0], ROWS):
        pre = dot(upt[m], h) + col(vec_ref, UP_BIAS, m)
        act_grad = dot(wd[m], g)
        square = pre * pre
        t = jnp.tanh(pre * (GELU_C + (GELU_C * GELU_A) * square))
        half = 0.5 * (1.0 + t)
        act_out[m] = (pre * half).astype(BF16)
        slope = half + (0.5 * pre) * (1.0 - t * t) * (GELU_C + (3.0 * GELU_C * GELU_A) * square)
        pg = (act_grad * slope).astype(BF16)
        pg_out[m] = pg
        add_to(s == 0, sum_out, 0, m, fold(pg.astype(F32)))
    act = act_out[...]
    for m in pieces:
        layer_s[m] = dot(wdt[m], act).astype(BF16)
    to_slot(s, layer_s, layer_outs)

    @pl.when(s == 0)
    def _():
        own_out[...] = y1_s[...]


def forward(chunk, info, atts, x, gs, wot, upt, wd, wdt, vec, carry):
    d, total = x.shape
    f = upt.shape[0]
    wide = SLOTS * BLK
    dev = 3 * (total // BLK)
    keep = lambda a: pl.BlockSpec(a.shape, lambda s, i: (0,) * a.ndim, pipeline_mode=pl.Buffered(1))
    block = lambda r: pl.BlockSpec((r, BLK), lambda s, i: (0, s))
    mine = pl.BlockSpec((d, BLK), lambda s, i: (0, chunk))
    args = [info, x, *atts, *gs, wot, upt, wd, wdt, vec]
    in_specs = [pl.BlockSpec((d, BLK), lambda s, i: (0, chunk * SLOTS + s))]
    in_specs += [pl.BlockSpec((atts[0].shape[0], BLK), lambda s, i: (0, s ^ i[dev]))] * SLOTS
    in_specs += [pl.BlockSpec((d, BLK), lambda s, i: (0, 0))] * SLOTS + [keep(a) for a in (wot, upt, wd, wdt, vec)]
    alias = {}
    if carry is not None:
        alias = {len(args) + n: 7 + n for n in range(len(carry))}
        in_specs += [pl.BlockSpec(memory_space=pl.ANY)] * len(carry)
        args += list(carry)
    spec = pltpu.PrefetchScalarGridSpec(
        num_scalar_prefetch=1,
        grid=(SLOTS,),
        in_specs=in_specs,
        out_specs=[
            block(d),
            block(f),
            block(f),
            block(d),
            block(d),
            block(8),
            pl.BlockSpec((1, f, 128), lambda s, i: (0, 0, 0)),
        ]
        + [mine] * 5,
        scratch_shapes=[pltpu.VMEM((d, BLK), F32), pltpu.VMEM((d, BLK), BF16)],
    )
    shape = jax.ShapeDtypeStruct
    rows = total // SLOTS
    return pl.pallas_call(
        forward_kernel,
        grid_spec=spec,
        out_shape=[
            shape((d, wide), BF16),
            shape((f, wide), BF16),
            shape((f, wide), BF16),
            shape((d, wide), BF16),
            shape((d, wide), BF16),
            shape((8, wide), F32),
            shape((1, f, 128), F32),
            shape((d, rows), F32),
        ]
        + [shape((d, rows), BF16)] * SLOTS,
        input_output_aliases=alias,
        compiler_params=params(),
        cost_estimate=cost(26),
        name="forward",
    )(*args)


def backward_kernel(info, pg_ref, n_ref, root_ref, g_ref, up, *refs):
    wo = refs[:SLOTS]
    vec_ref = refs[SLOTS]
    sum_out = refs[-11]
    attg_outs = refs[-10:-6]
    y1g_outs = refs[-6:-2]
    e_s, y1g_s = refs[-2:]
    s = pl.program_id(0)
    d = n_ref.shape[0]
    pieces = cuts(d, ROWS)
    pg = pg_ref[...]
    mean = 0.0
    tilt = 0.0
    for m in pieces:
        hg = dot(up[m], pg)
        n = n_ref[m].astype(F32)
        hn = hg * n
        gain = col(vec_ref, GAIN2, m)
        e = hg * gain
        e_s[m] = e
        mean = mean + jnp.sum(e, axis=0, keepdims=True)
        tilt = tilt + jnp.sum(hn * gain, axis=0, keepdims=True)
        add_to(s == 0, sum_out, 0, m, fold(hn))
        add_to(s == 0, sum_out, 1, m, fold(hg))
    mean = mean * (1.0 / d)
    tilt = tilt * (1.0 / d)
    root = root_ref[0:1]
    mine = jnp.where(s == 0, 1.0, 0.0)
    for m in pieces:
        y1g = root * (e_s[m] - mean - n_ref[m].astype(F32) * tilt) + g_ref[m].astype(F32) * mine
        y1g_s[m] = y1g.astype(BF16)
        add_to(s == 0, sum_out, 2, m, fold(y1g))
    y1b = y1g_s[...]
    for k in range(SLOTS):
        attg_outs[k][...] = dot(wo[k][...], y1b).astype(BF16)
    to_slot(s, y1g_s, y1g_outs)


def backward(chunk, info, pg, n, root, g, up, wos, vec, carry):
    d, wide = n.shape
    f = up.shape[1]
    rows = wos[0].shape[0]
    dev = info.shape[0] - 1
    keep = lambda a: pl.BlockSpec(a.shape, lambda s, i: (0,) * a.ndim, pipeline_mode=pl.Buffered(1))
    block = lambda r: pl.BlockSpec((r, BLK), lambda s, i: (0, s))
    mine = pl.BlockSpec((d, BLK), lambda s, i: (0, chunk))
    ordered = pl.BlockSpec((rows, BLK), lambda s, i: (0, s ^ i[dev]))
    args = [info, pg, n, root, g, up, *wos, vec]
    in_specs = [block(f), block(d), block(8), mine] + [keep(a) for a in (up, *wos, vec)]
    alias = {}
    if carry is not None:
        alias = {len(args) + n: 5 + n for n in range(len(carry))}
        in_specs += [pl.BlockSpec(memory_space=pl.ANY)] * len(carry)
        args += list(carry)
    spec = pltpu.PrefetchScalarGridSpec(
        num_scalar_prefetch=1,
        grid=(SLOTS,),
        in_specs=in_specs,
        out_specs=[pl.BlockSpec((3, d, 128), lambda s, i: (0, 0, 0))] + [ordered] * SLOTS + [mine] * SLOTS,
        scratch_shapes=[pltpu.VMEM((d, BLK), F32), pltpu.VMEM((d, BLK), BF16)],
    )
    shape = jax.ShapeDtypeStruct
    return pl.pallas_call(
        backward_kernel,
        grid_spec=spec,
        out_shape=[shape((3, d, 128), F32)] + [shape((rows, wide), BF16)] * SLOTS + [shape(g.shape, BF16)] * SLOTS,
        input_output_aliases=alias,
        compiler_params=params(),
        cost_estimate=cost(17),
        name="backward",
    )(*args)


def shard_rows(m):
    return -(-m // (8 * 16)) * 16


def outer_kernel(count, order, with_sum, with_extra, info, *refs):
    dp = info[0]
    i = pl.program_id(0)
    extra, outs = refs[2 * count : 2 * count + with_extra], refs[2 * count + with_extra :]
    total = None
    for n in range(count):
        part = dot(refs[2 * n][...], refs[2 * n + 1][...], NT)
        total = part if total is None else total + part
    size = total.shape[0] // 2
    shard = size * (1 + with_extra)
    for half in range(2):
        slot = (2 * i) ^ (dp & 1) ^ half
        at = jnp.where((slot & order[2]) != 0, 1, 0) + jnp.where((slot & order[1]) != 0, 2, 0)
        values = [total[half * size : (half + 1) * size].astype(BF16)]
        values += [ref[half * size : (half + 1) * size] for ref in extra]
        goes = (slot & order[0]) != 0
        for k, out in enumerate(outs[:2]):

            @pl.when(goes if k else jnp.logical_not(goes))
            def _():
                for n, value in enumerate(values):
                    out[pl.ds(pl.multiple_of(at * shard + n * size, 16), size)] = value

    if with_sum:
        outs[2][...] = fold(refs[0][...].astype(F32))


def outer(pairs, info, order, first=0, rows=None, with_sum=False, extra=None):
    m, depth = pairs[0][0].shape
    n = pairs[0][1].shape[0]
    rows = m if rows is None else rows
    size = shard_rows(rows)
    skip = first // (2 * size)
    in_specs, args = [], []
    for a, b in pairs:
        in_specs.append(pl.BlockSpec((2 * size, depth), lambda i, s: (skip + (i ^ (s[0] >> 1)), 0)))
        in_specs.append(pl.BlockSpec((n, depth), lambda i, s: (0, 0), pipeline_mode=pl.Buffered(1)))
        args += [a, b]
    both = 0 if extra is None else 1
    if both:
        last = -(-extra.shape[0] // (2 * size)) - 1
        in_specs.append(pl.BlockSpec((2 * size, n), lambda i, s: (jnp.minimum(i ^ (s[0] >> 1), last), 0)))
        args.append(extra)
    out_specs = [pl.BlockSpec((4 * size * (1 + both), n), lambda i, s: (0, 0))] * 2
    out_shape = [jax.ShapeDtypeStruct((4 * size * (1 + both), n), BF16)] * 2
    if with_sum:
        out_specs.append(pl.BlockSpec((2 * size, 128), lambda i, s: (i ^ (s[0] >> 1), 0)))
        out_shape.append(jax.ShapeDtypeStruct((8 * size, 128), F32))
    return pl.pallas_call(
        functools.partial(outer_kernel, len(pairs), order, with_sum, both),
        grid_spec=pltpu.PrefetchScalarGridSpec(num_scalar_prefetch=1, grid=(4,), in_specs=in_specs, out_specs=out_specs),
        out_shape=out_shape,
        compiler_params=params(),
        cost_estimate=cost(11),
        name="outer",
    )(info, *args)


def attn_grad_kernel(a_ref, b_ref, out_ref, sum_ref):
    a = a_ref[...]
    out_ref[...] = dot(a, b_ref[...], NT).astype(BF16)
    sum_ref[...] = fold(a.astype(F32))


def attn_grad_call(dqkv, h1):
    m, total = dqkv.shape
    d = h1.shape[0]
    rows = m // 3
    return pl.pallas_call(
        attn_grad_kernel,
        grid=(3,),
        in_specs=[
            pl.BlockSpec((rows, total), lambda i: (i, 0)),
            pl.BlockSpec((d, total), lambda i: (0, 0), pipeline_mode=pl.Buffered(1)),
        ],
        out_specs=[pl.BlockSpec((rows, d), lambda i: (i, 0)), pl.BlockSpec((rows, 128), lambda i: (i, 0))],
        out_shape=[jax.ShapeDtypeStruct((m, d), BF16), jax.ShapeDtypeStruct((m, 128), F32)],
        compiler_params=params(),
        cost_estimate=cost(9),
        name="attn_grad_call",
    )(dqkv, h1)


def halve_kernel(keep_ref, recv_ref, keep_out, send_out):
    i = pl.program_id(0)
    total = (keep_ref[...].astype(F32) + recv_ref[...].astype(F32)).astype(BF16)

    @pl.when(i == 0)
    def _():
        keep_out[...] = total

    @pl.when(i == 1)
    def _():
        send_out[...] = total


def halve(keep, recv):
    size, n = keep.shape[0] // 2, keep.shape[1]
    block = pl.BlockSpec((size, n), lambda i: (i, 0))
    return pl.pallas_call(
        halve_kernel,
        grid=(2,),
        in_specs=[block, block],
        out_specs=[pl.BlockSpec((size, n), lambda i: (0, 0))] * 2,
        out_shape=[jax.ShapeDtypeStruct((size, n), BF16)] * 2,
        compiler_params=params(),
        cost_estimate=cost(2.5),
        name="halve",
    )(keep, recv)


def slot_of(i, order):
    return jnp.where(i & 1, order[2], 0) | jnp.where(i & 2, order[1], 0) | jnp.where(i & 4, order[0], 0)


def place_kernel(count, info, one, two, four, eight, *rest):
    i = pl.program_id(0)
    outs = rest[-count:]
    for ref, low, high in ((one, 0, 1), (two, 1, 2), (four, 2, 4), (eight, 4, 8)):

        @pl.when((i >= low) & (i < high))
        def _():
            size = ref.shape[0] // count
            for n, out in enumerate(outs):
                out[...] = ref[n * size : (n + 1) * size].astype(F32)


def place(parts, info, order, first, rows, carry, extra_rows):
    size, n = parts[0].shape
    count = 2 if extra_rows else 1
    half = size // count
    start = first // half
    near = lambda at, many: pl.BlockSpec((size, n), lambda i, s: (jnp.clip(i - at, 0, many - 1), 0))
    in_specs = [near(0, 1), near(1, 1), near(2, 2), near(4, 4)]
    args = list(parts)
    alias = {}
    if carry is not None:
        in_specs.append(pl.BlockSpec(memory_space=pl.ANY))
        args.append(carry)
        alias = {5: 0}
    out_specs = [pl.BlockSpec((half, n), lambda i, s: (start + (slot_of(i, order) ^ s[0]), 0))]
    out_shape = [jax.ShapeDtypeStruct((rows, n), F32)]
    if extra_rows:
        out_specs.append(pl.BlockSpec((half, n), lambda i, s: (slot_of(i, order) ^ s[0], 0)))
        out_shape.append(jax.ShapeDtypeStruct((8 * half, n), F32))
    spec = pltpu.PrefetchScalarGridSpec(num_scalar_prefetch=1, grid=(8,), in_specs=in_specs, out_specs=out_specs)
    out = pl.pallas_call(
        functools.partial(place_kernel, count),
        grid_spec=spec,
        out_shape=out_shape,
        input_output_aliases=alias,
        compiler_params=params(),
        cost_estimate=cost(6.5),
        name="place",
    )(info, *args)
    return (out[0], out[1][:extra_rows]) if extra_rows else out[0]


def swap_dp(v, k):
    return lax.ppermute(v, "dp", [(i, i ^ k) for i in range(8)])


class CellSum:
    def __init__(self, line, keep, send, info, order, rows, first=0, extra_rows=0):
        self.line, self.keep, self.info, self.order = line, keep, info, order
        self.rows, self.first, self.extra_rows = rows, first, extra_rows
        self.stage = 0
        self.known = lax.axis_size("dp") == 8
        if not self.known:
            both = lax.psum(jnp.stack([keep, send]), "dp")
            size = keep.shape[0] // 4
            self.parts = [both[0, :size], both[0, size : 2 * size], both[0, 2 * size :], both[1]]
            self.got = both[1]
            return
        self.got = swap_dp(send, order[0])

    def step(self):
        if not self.known:
            return
        self.stage += 1
        k1, k2, k3 = self.order
        if self.stage < 3:
            self.keep, send = self.line(halve, self.keep, self.got)
            self.got = swap_dp(send, k2 if self.stage == 1 else k3)
        elif self.stage == 3:
            self.parts = [self.line(lambda a, b: add(BF16, a, b), self.keep, self.got)]
            self.got = swap_dp(self.parts[0], k3)
        else:
            self.parts.append(self.got)
            self.got = swap_dp(self.line(stack, *self.parts), k2 if self.stage == 4 else k1)
            if self.stage == 5:
                self.parts.append(self.got)

    def finish(self, carry=None):
        return self.line(
            lambda p, *c: place(
                p, self.info, self.order, self.first, self.rows, c[0] if c else None, self.extra_rows
            ),
            self.parts,
            *([] if carry is None else [carry]),
        )


class Rounds:
    def __init__(self, line, v, over_tensor=False):
        self.line, self.v = line, v
        self.todo = [(swap_dp, 1), (swap_dp, 2), (swap_dp, 4)]
        if lax.axis_size("dp") != 8:
            self.v = lax.psum(v.astype(F32), "dp").astype(v.dtype)
            self.todo = []
        self.cells = self.v
        if over_tensor:
            self.todo += [(swap, 1), (swap, 2)]
        self.send()

    def send(self):
        self.got = None
        if self.todo:
            self.move, k = self.todo.pop(0)
            self.got = self.move(self.v, k)

    def step(self):
        if self.got is None:
            return
        self.v = self.line(lambda a, b: add(a.dtype, a, b), self.v, self.got)
        if self.move is swap_dp:
            self.cells = self.v
        self.send()


def out_grad_kernel(chunks, info, *refs):
    k = pl.program_id(0)
    atts, y1gs, outs = refs[: chunks * SLOTS], refs[chunks * SLOTS : -SLOTS], refs[-SLOTS:]
    dev = info[3 * y1gs[0].shape[1] * SLOTS // BLK]
    for n in range(SLOTS):

        @pl.when(k == n)
        def _():
            total = None
            for c in range(chunks):
                for s in range(SLOTS):
                    at = pl.multiple_of((s ^ dev) * BLK, BLK)
                    y1g = y1gs[s][:, c * BLK : (c + 1) * BLK]
                    part = dot(atts[c * SLOTS + n][:, pl.ds(at, BLK)], y1g, NT)
                    total = part if total is None else total + part
            outs[n][...] = total.astype(BF16)


def out_grad_call(info, atts, y1gs):
    rows = atts[0][0].shape[0]
    d = y1gs[0].shape[0]
    arrays = [a for chunk in atts for a in chunk] + list(y1gs)
    spec = pltpu.PrefetchScalarGridSpec(
        num_scalar_prefetch=1,
        grid=(SLOTS,),
        in_specs=[pl.BlockSpec(a.shape, lambda k, s: (0, 0), pipeline_mode=pl.Buffered(1)) for a in arrays],
        out_specs=[pl.BlockSpec((rows, d), lambda k, s: (0, 0))] * SLOTS,
    )
    return pl.pallas_call(
        functools.partial(out_grad_kernel, len(atts)),
        grid_spec=spec,
        out_shape=[jax.ShapeDtypeStruct((rows, d), BF16)] * SLOTS,
        compiler_params=params(),
        cost_estimate=cost(12),
        name="out_grad_call",
    )(info, *arrays)


def h1_grad_kernel(w_ref, dqkv_ref, x_ref, sum_ref, *outs):
    s = pl.program_id(1)
    first = (s == 0) & (pl.program_id(0) == 0)
    hg_s = outs[-1]
    d = x_ref.shape[0]
    pieces = cuts(d, ROWS)
    total = 0.0
    for m in pieces:
        total = total + jnp.sum(x_ref[m].astype(F32), axis=0, keepdims=True)
    mean = total * (1.0 / d)
    total = 0.0
    for m in pieces:
        center = x_ref[m].astype(F32) - mean
        total = total + jnp.sum(center * center, axis=0, keepdims=True)
    root = lax.rsqrt(total * (1.0 / d) + EPS)
    dqkv = dqkv_ref[...]
    for m in pieces:
        hg = dot(w_ref[m], dqkv)
        n = (x_ref[m].astype(F32) - mean) * root
        hg_s[m] = hg.astype(BF16)
        add_to(first, sum_ref, 0, m, fold(hg * n))
        add_to(first, sum_ref, 1, m, fold(hg))
    to_slot(s, hg_s, outs[:SLOTS])


def h1_grad_call(w, dqkv, x):
    d, total = x.shape
    per = total // (BLK * SLOTS)
    m = w.shape[1]
    at = lambda p, s: (0, p * SLOTS + s)
    mine = pl.BlockSpec((d, BLK), lambda p, s: (0, p))
    return pl.pallas_call(
        h1_grad_kernel,
        grid=(per, SLOTS),
        in_specs=[
            pl.BlockSpec((d, m), lambda p, s: (0, 0), pipeline_mode=pl.Buffered(1)),
            pl.BlockSpec((m, BLK), at),
            pl.BlockSpec((d, BLK), at),
        ],
        out_specs=[pl.BlockSpec((2, d, 128), lambda p, s: (0, 0, 0))] + [mine] * SLOTS,
        out_shape=[jax.ShapeDtypeStruct((2, d, 128), F32)]
        + [jax.ShapeDtypeStruct((d, per * BLK), BF16)] * SLOTS,
        scratch_shapes=[pltpu.VMEM((d, BLK), BF16)],
        compiler_params=params(),
        cost_estimate=cost(13),
        name="h1_grad_call",
    )(w, dqkv, x)


def input_grad_kernel(x_ref, a_ref, b_ref, c_ref, d_ref, y1g_ref, gain_ref, out_ref):
    n, root = normal(x_ref[...].astype(F32))
    total = a_ref[...].astype(F32) + b_ref[...].astype(F32) + c_ref[...].astype(F32) + d_ref[...].astype(F32)
    e = total * gain_ref[:, GAIN1 : GAIN1 + 1]
    e = root * (e - jnp.mean(e, axis=0, keepdims=True) - n * jnp.mean(e * n, axis=0, keepdims=True))
    out_ref[...] = (y1g_ref[...] + e).astype(BF16)


def input_grad_call(x, a, b, c, d4, y1g, gain):
    d, rows = x.shape
    block = pl.BlockSpec((d, 128), lambda i: (0, i))
    return pl.pallas_call(
        input_grad_kernel,
        grid=(rows // 128,),
        in_specs=[block] * 6 + [pl.BlockSpec(gain.shape, lambda i: (0, 0))],
        out_specs=block,
        out_shape=jax.ShapeDtypeStruct((d, rows), BF16),
        compiler_params=params(),
        cost_estimate=cost(6),
        name="input_grad_call",
    )(x, a, b, c, d4, y1g, gain)


def layer_kernel(own_ref, a_ref, b_ref, c_ref, vec_ref, out_ref):
    total = a_ref[...].astype(F32) + b_ref[...].astype(F32) + c_ref[...].astype(F32)
    out_ref[...] = (own_ref[...] + total + vec_ref[:, DOWN_BIAS : DOWN_BIAS + 1]).astype(BF16)


def layer_call(own, a, b, c, vec):
    d, rows = own.shape
    block = pl.BlockSpec((d, 128), lambda i: (0, i))
    return pl.pallas_call(
        layer_kernel,
        grid=(rows // 128,),
        in_specs=[block] * 4 + [pl.BlockSpec(vec.shape, lambda i: (0, 0))],
        out_specs=block,
        out_shape=jax.ShapeDtypeStruct((d, rows), BF16),
        compiler_params=params(),
        cost_estimate=cost(3),
        name="layer_call",
    )(own, a, b, c, vec)


def small_kernel(chunks, width, sum1_ref, *refs):
    sums, ups, (qkv_ref, g_ref, out_ref) = refs[:chunks], refs[chunks : 2 * chunks], refs[2 * chunks :]
    across = lambda v: jnp.sum(v, axis=1, keepdims=True)
    columns = [across(sum1_ref[0]), across(sum1_ref[1])]
    columns += [across(sum(ref[n] for ref in sums)) for n in range(3)]
    columns += [across(g_ref[...].astype(F32)), across(sum(ref[0] for ref in ups))]
    d = g_ref.shape[0]
    qv = jnp.concatenate([qkv_ref[0:width], qkv_ref[2 * width : 3 * width]], 0)
    qv = jnp.concatenate([across(qv), jnp.zeros((d - 2 * width, 1), F32)], 0)
    out_ref[...] = jnp.concatenate([v.T for v in columns + [qv]], 0)


def small_sums(sum1, sums, up_sums, qkv_sum, g):
    return pl.pallas_call(
        functools.partial(small_kernel, len(sums), qkv_sum.shape[0] // 3),
        out_shape=jax.ShapeDtypeStruct((8, g.shape[0]), F32),
        compiler_params=params(),
        cost_estimate=cost(5),
        name="small_sums",
    )(sum1, *sums, *up_sums, qkv_sum, g)


def swap(v, k):
    return lax.ppermute(v, "tensor", [(i, i ^ k) for i in range(SLOTS)])


def after(v, *done):
    return lax.optimization_barrier((v, done))[0]


class Line:
    def __init__(self):
        self.last = []

    def __call__(self, step, *args):
        args, _ = lax.optimization_barrier((args, self.last))
        out = step(*args)
        self.last = jax.tree.leaves(out)
        return out

    def wait(self, *values):
        self.last = self.last + jax.tree.leaves(values)

    def pin(self, v, *also):
        return after(v, self.last, also)


class Gather:
    def __init__(self, v):
        self.own, self.side, self.across = v, swap(v, 1), swap(v, 2)

    def finish(self, line):
        self.corner = swap(line.pin(self.across), 1)
        return self

    def all(self):
        return self.own, self.side, self.across, self.corner


def plus(a, b):
    return a.astype(F32) + b.astype(F32)


def plus_low(a, b):
    return plus(a, b).astype(BF16)


def add_kernel(*refs):
    total = None
    for ref in refs[:-1]:
        v = (ref[0] if len(ref.shape) == 3 else ref[...]).astype(F32)
        total = v if total is None else total + v
    refs[-1][...] = total.astype(refs[-1].dtype)


def add(dtype, *terms):
    rows, columns = terms[0].shape
    size = rows // 2 if rows % 32 == 0 and rows * columns > 1 << 18 else rows
    in_specs, args = [], []
    for term in terms:
        if isinstance(term, tuple):
            in_specs.append(pl.BlockSpec((1, size, columns), functools.partial(lambda at, i: (at, i, 0), term[1])))
            args.append(term[0])
        else:
            in_specs.append(pl.BlockSpec((size, columns), lambda i: (i, 0)))
            args.append(term)
    return pl.pallas_call(
        add_kernel,
        grid=(rows // size,),
        in_specs=in_specs,
        out_specs=pl.BlockSpec((size, columns), lambda i: (i, 0)),
        out_shape=jax.ShapeDtypeStruct((rows, columns), dtype),
        compiler_params=params(),
        cost_estimate=cost(2.3),
        name="add",
    )(*args)


class GroupSum:
    def __init__(self, line, parts):
        self.line, self.parts = line, parts
        self.side = swap(line.pin(parts[3]), 1)

    def step(self):
        self.far = swap(self.line(lambda a, b: add(BF16, a, b), self.parts[2], self.side), 2)
        self.near = swap(self.line.pin(self.parts[1]), 1)
        self.line.wait(self.near)

    def terms(self):
        return self.parts[0], self.near, self.far


def stack_kernel(*refs):
    at = 0
    for ref in refs[:-1]:
        refs[-1][at : at + ref.shape[0]] = ref[...]
        at += ref.shape[0]


def stack(*parts):
    return pl.pallas_call(
        stack_kernel,
        out_shape=jax.ShapeDtypeStruct((sum(p.shape[0] for p in parts), parts[0].shape[1]), parts[0].dtype),
        compiler_params=params(),
        cost_estimate=cost(2),
        name="stack",
    )(*parts)


def token_starts(lengths, offsets, total, dev):
    pos = jnp.arange(total, dtype=jnp.int32)[:, None]
    inside = (pos >= offsets[None]) & (pos < (offsets + lengths)[None])
    first = jnp.max(jnp.where(inside, offsets[None], -1), axis=1)
    start = jnp.where(first >= 0, first, pos[:, 0])
    nb = total // BLK
    per = nb // SLOTS
    b = jnp.arange(nb, dtype=jnp.int32)
    first_key = start.reshape(nb, BLK)[:, 0] // BLK
    place = (b % per) * SLOTS + ((b // per) ^ dev)
    last_query = jnp.max(jnp.where(first_key[None, :] <= b[:, None], b[None, :], 0), axis=1)
    info = jnp.concatenate([first_key, place, last_query, jnp.full((1,), dev)])
    return start[None], info.astype(jnp.int32)


def body(
    tokens,
    cotangent,
    ln1_gain,
    ln1_bias,
    attn_weight,
    qv_bias,
    out_weight,
    out_bias,
    ln2_gain,
    ln2_bias,
    up_weight,
    up_bias,
    down_weight,
    down_bias,
    cell_lengths,
    cell_offsets,
):
    rows, d = tokens.shape
    width = attn_weight.shape[2]
    heads = width // HEAD_DIM
    total = rows * SLOTS
    per = rows // BLK
    dev = lax.axis_index("tensor")
    start, info = token_starts(cell_lengths[0], cell_offsets[0], total, dev)

    whole_dp = lax.axis_size("dp") == 8
    dp_info = jnp.full((1,), lax.axis_index("dp") if whole_dp else 0, jnp.int32)

    line = Line()
    x_own = tokens.T
    g_own = cotangent.T
    x_go = Gather(x_own)

    w_in = attn_weight.transpose(1, 2, 0)
    zero = jnp.zeros_like(ln1_gain)
    rows8 = jnp.stack([ln1_gain, ln1_bias, out_bias, ln2_gain, ln2_bias, up_bias, down_bias, zero])
    bias8 = jnp.zeros((8, width), F32).at[0].set(qv_bias[0]).at[2].set(qv_bias[1])
    upt, wdt, w_back, vec, bias, *g_cuts = line(
        turn, g_own, up_weight, down_weight, w_in.reshape(3 * width, d), rows8, bias8
    )
    carry = line(lambda a, b: qkv_call(0, a, b, w_in, vec, bias, None), x_own, x_go.side)
    wo_go = Gather(line.pin(out_weight, x_go.across))
    x_parts = x_go.finish(line).all()
    x_all, h1, qkv, kn, vn = line(lambda a, b, c: qkv_call(1, a, b, w_in, vec, bias, c), x_parts[2], x_parts[3], carry)
    chunks = range(per)
    g_go = [Gather(line.pin(g_cuts[0]))]
    fronts, att_go = [], []
    for c in chunks:
        fronts.append(line(functools.partial(attend, c), info, start, qkv, kn))
        if c == 0:
            line.wait(g_go[0].across, g_go[0].side)
        att_go.append(Gather(line.pin(fronts[c][0]).reshape(width, SLOTS * BLK)))
        if c == 0:
            wo_parts = wo_go.finish(line).all()
    wot = line(turn_pieces, *wo_parts)
    g_parts = [g_go[0].finish(line).all()]
    atts, ahead = [], []
    for c in chunks:
        atts.append(att_go[c].finish(line).all())
        if c > 0:
            g_parts.append(g_go[c].finish(line).all())
        if c + 1 < per:
            g_go.append(Gather(line.pin(g_cuts[c + 1], atts[c][2])))
        ahead.append(
            line(
                functools.partial(forward, c),
                info,
                atts[c],
                x_all,
                g_parts[c],
                wot,
                upt,
                down_weight,
                wdt,
                vec,
                ahead[-1][7:] if c else None,
            )
        )
    h2s, acts, pgs, gs, ns, roots, up_sums = zip(*[m[:7] for m in ahead])
    own, *layer_parts = ahead[-1][7:]
    flat = lambda a, b: list(zip(a, b))
    y_first, z_first = (1, 2, 4), (2, 1, 4)
    f = down_weight.shape[0]
    down = CellSum(line, *line(lambda a, b: outer(flat(a, b), dp_info, y_first), acts, gs), dp_info, y_first, f)
    up = CellSum(line, *line(lambda a, b: outer(flat(a, b), dp_info, z_first), h2s, pgs), dp_info, z_first, d)

    back, attgs = [], []
    for c in chunks:
        carry = back[-1][1 + SLOTS :] if c else None
        back.append(
            line(functools.partial(backward, c), info, pgs[c], ns[c], roots[c], g_own, up_weight, wo_parts, vec, carry)
        )
        if c:
            line.wait(attgs[-1].far, down.got, up.got)
            up.step()
        down.step()
        attgs.append(GroupSum(line, back[c][1 : 1 + SLOTS]))
        attgs[c].step()
    y1g_parts = back[-1][1 + SLOTS :]
    layer_sum = GroupSum(line, layer_parts)
    out_parts = line(out_grad_call, info, atts, y1g_parts)
    line.wait(attgs[-1].far, down.got, up.got, layer_sum.side)
    out = GroupSum(line, out_parts)
    do, stat = line(join, [a.terms() + tuple(f) for a, f in zip(attgs, fronts)])
    out.step()
    layer_sum.step()
    down.step()
    up.step()
    dqkv = line(attend_back, info, start, qkv, kn, vn, do, stat).reshape(3 * width, total)
    line.wait(down.got, up.got, out.far)

    out_grad = line(lambda *v: add(BF16, *v), *out.terms())
    y1g = GroupSum(line, y1g_parts)
    up.step()
    down.step()
    attn_grad, qkv_sum = line(attn_grad_call, dqkv, h1)
    late = lax.psum((attn_grad, out_grad), "dp")
    line.wait(up.got, down.got, layer_sum.far, y1g.side)
    y1g.step()
    up.step()
    down.step()
    sum1, *h1_parts = line(h1_grad_call, w_back, dqkv, x_all)
    line.wait(y1g.far, up.got)
    h1g = [h1_parts[0]] + [swap(line.pin(h1_parts[k]), k) for k in (1, 2, 3)]
    up.step()
    y1_grad = line(lambda *v: add(F32, *v), *y1g.terms())
    small = line(small_sums, sum1, [b[0] for b in back], up_sums, qkv_sum, g_own)
    layer = line(layer_call, own, *layer_sum.terms(), vec)
    line.wait(down.got)
    down_grad = down.finish()
    line.wait(up.got)
    up_grad = up.finish()
    small = Rounds(line, line.pin(small), True)
    small.step()
    line.wait(*h1g[1:])
    input_grad = line(input_grad_call, x_own, *h1g, y1_grad, vec)
    small.step()
    small.step()
    small.step()
    small.step()
    line.wait(late)
    attn_grad, out_grad = (v.astype(F32) for v in line(lambda a, b: (a, b), *late))
    small, own_small = small.v, small.cells[6:]
    return (
        layer.T,
        input_grad.T,
        small[0],
        small[1],
        attn_grad.reshape(3, width, d).transpose(2, 0, 1),
        own_small[1, : 2 * width].reshape(2, width),
        out_grad,
        small[4],
        small[2],
        small[3],
        up_grad,
        own_small[0],
        down_grad,
        small[5],
    )


def solution(mesh):
    rows = P(("dp", "tensor"), None)
    in_specs = (
        rows,
        rows,
        P(),
        P(),
        P(None, None, "tensor"),
        P(None, "tensor"),
        P("tensor", None),
        P(),
        P(),
        P(),
        P(None, "tensor"),
        P("tensor"),
        P("tensor", None),
        P(),
        P("dp", None),
        P("dp", None),
    )
    out_specs = (
        rows,
        rows,
        P(),
        P(),
        P(None, None, "tensor"),
        P(None, "tensor"),
        P("tensor", None),
        P(),
        P(),
        P(),
        P(None, "tensor"),
        P("tensor"),
        P("tensor", None),
        P(),
    )
    return jax.shard_map(body, mesh=mesh, in_specs=in_specs, out_specs=out_specs, check_vma=False)
```

```python
import functools
import math

import jax
import jax.numpy as jnp
from jax import lax
from jax.experimental import pallas as pl
from jax.experimental.pallas import tpu as pltpu
from jax.sharding import PartitionSpec as P


HEAD_DIM = 56
BLK = 256
SLOTS = 4
NEG = -1e30
EPS = 1e-05
SCALE = 1.0 / math.sqrt(HEAD_DIM)
SCALE2 = SCALE * math.log2(math.e)
GELU_C = math.sqrt(2.0 / math.pi)
GELU_A = 0.044715
F32 = jnp.float32
BF16 = jnp.bfloat16
NT = ((1,), (1,))
ROWS = 224
GAIN1, SHIFT1, OUT_BIAS, GAIN2, SHIFT2, UP_BIAS, DOWN_BIAS = range(7)
VEC8 = True
ATT_PIECES = True
VMEM = 60 << 20
PACE = 0.0


def dot(a, b, dims=((1,), (0,))):
    return lax.dot_general(a, b, (dims, ((), ())), preferred_element_type=F32)


def params():
    return pltpu.CompilerParams(vmem_limit_bytes=VMEM)


def cost(microseconds):
    return pl.CostEstimate(flops=max(1, int(microseconds * PACE)), bytes_accessed=1, transcendentals=0)


def fold(v):
    total = v[:, :128]
    for at in range(128, v.shape[1], 128):
        total = total + v[:, at : at + 128]
    return total


def normal(x):
    center = x - jnp.mean(x, axis=0, keepdims=True)
    root = lax.rsqrt(jnp.mean(center * center, axis=0, keepdims=True) + EPS)
    return center * root, root


def turn_kernel(count, parts, *refs):
    for n in range(count):
        refs[count + 1 + n][...] = refs[n][...].T
    for n in range(parts):
        refs[2 * count + 1 + n][...] = refs[count][:, n * BLK : (n + 1) * BLK]


def turn(cut, *arrays):
    wide = max(a.shape[1] for a in arrays)
    steps = -(-wide // 256)
    in_specs, out_specs, outs = [], [], []
    for a in arrays:
        rows, columns = a.shape
        if columns == wide:
            in_specs.append(pl.BlockSpec((rows, 256), lambda i: (0, i)))
            out_specs.append(pl.BlockSpec((256, rows), lambda i: (i, 0)))
        else:
            in_specs.append(pl.BlockSpec((rows, columns), lambda i: (0, 0)))
            out_specs.append(pl.BlockSpec((columns, rows), lambda i: (0, 0)))
        outs.append(jax.ShapeDtypeStruct((columns, rows), a.dtype))
    rows, columns = cut.shape
    parts = columns // BLK
    size = -(-rows // (16 * steps)) * 16
    in_specs.append(pl.BlockSpec((size, columns), lambda i: (i, 0)))
    out_specs += [pl.BlockSpec((size, BLK), lambda i: (i, 0))] * parts
    outs += [jax.ShapeDtypeStruct((rows, BLK), cut.dtype)] * parts
    return pl.pallas_call(
        functools.partial(turn_kernel, len(arrays), parts),
        grid=(steps,),
        in_specs=in_specs,
        out_specs=out_specs,
        out_shape=outs,
        compiler_params=params(),
        cost_estimate=cost(8),
        name="turn",
    )(*arrays, cut)


def turn_pieces_kernel(*refs):
    refs[-1][...] = jnp.concatenate([ref[...] for ref in refs[:-1]], 0).T


def turn_pieces(*pieces):
    rows, columns = pieces[0].shape
    return pl.pallas_call(
        turn_pieces_kernel,
        grid=(-(-columns // 256),),
        in_specs=[pl.BlockSpec((rows, 256), lambda i: (0, i))] * len(pieces),
        out_specs=pl.BlockSpec((256, rows * len(pieces)), lambda i: (i, 0)),
        out_shape=jax.ShapeDtypeStruct((columns, rows * len(pieces)), pieces[0].dtype),
        compiler_params=params(),
        cost_estimate=cost(5),
        name="turn_pieces",
    )(*pieces)


def col(ref, at, m):
    return ref[m, at : at + 1]


def cuts(total, size):
    return [slice(at, min(at + size, total)) for at in range(0, total, size)]


def qkv_kernel(heads, a_ref, b_ref, w_ref, vec_ref, bias_ref, *rest):
    x_out, h_out, q_out, kn_out, vn_out = rest[-5:]
    x_out[:, :BLK] = a_ref[...]
    x_out[:, BLK:] = b_ref[...]
    d = x_out.shape[0]
    pieces = cuts(d, ROWS)
    total = 0.0
    for m in pieces:
        total = total + jnp.sum(x_out[m].astype(F32), axis=0, keepdims=True)
    mean = total * (1.0 / d)
    total = 0.0
    for m in pieces:
        center = x_out[m].astype(F32) - mean
        total = total + jnp.sum(center * center, axis=0, keepdims=True)
    root = lax.rsqrt(total * (1.0 / d) + EPS)
    for m in pieces:
        n = (x_out[m].astype(F32) - mean) * root
        h_out[m] = (n * col(vec_ref, GAIN1, m) + col(vec_ref, SHIFT1, m)).astype(BF16)
    h = h_out[...]
    for part in range(3):
        r = (dot(w_ref[part], h) + bias_ref[:, part : part + 1]).astype(BF16)
        r = r.reshape(heads, HEAD_DIM, r.shape[1])
        q_out[part * heads : (part + 1) * heads] = r
        if part > 0:
            out = kn_out if part == 1 else vn_out
            for h_at in range(heads):
                out[h_at] = r[h_at].T


def qkv_call(pair, a, b, w, vec, bias, carry):
    d, rows = a.shape
    per = rows // BLK
    total = rows * SLOTS
    heads = w.shape[1] // HEAD_DIM
    wide = 2 * BLK
    outs = [
        jax.ShapeDtypeStruct((d, total), BF16),
        jax.ShapeDtypeStruct((d, total), BF16),
        jax.ShapeDtypeStruct((3 * heads, HEAD_DIM, total), BF16),
        jax.ShapeDtypeStruct((heads, total, HEAD_DIM), BF16),
        jax.ShapeDtypeStruct((heads, total, HEAD_DIM), BF16),
    ]
    at = lambda p: p * (SLOTS // 2) + pair
    in_specs = [
        pl.BlockSpec((d, BLK), lambda p: (0, p)),
        pl.BlockSpec((d, BLK), lambda p: (0, p)),
        pl.BlockSpec(w.shape, lambda p: (0, 0, 0)),
        pl.BlockSpec(vec.shape, lambda p: (0, 0)),
        pl.BlockSpec(bias.shape, lambda p: (0, 0)),
    ]
    args = [a, b, w, vec, bias]
    alias = {}
    if carry is not None:
        alias = {len(args) + n: n for n in range(len(outs))}
        in_specs += [pl.BlockSpec(memory_space=pl.ANY)] * len(outs)
        args += list(carry)
    return pl.pallas_call(
        functools.partial(qkv_kernel, heads),
        grid=(per,),
        in_specs=in_specs,
        out_specs=[
            pl.BlockSpec((d, wide), lambda p: (0, at(p))),
            pl.BlockSpec((d, wide), lambda p: (0, at(p))),
            pl.BlockSpec((3 * heads, HEAD_DIM, wide), lambda p: (0, 0, at(p))),
            pl.BlockSpec((heads, wide, HEAD_DIM), lambda p: (0, at(p), 0)),
            pl.BlockSpec((heads, wide, HEAD_DIM), lambda p: (0, at(p), 0)),
        ],
        out_shape=outs,
        input_output_aliases=alias,
        compiler_params=params(),
        cost_estimate=cost(8),
        name="qkv_call",
    )(*args)


def attend_kernel(heads, nb, per, chunk, info, start_ref, q_ref, kn_ref, v_ref, o_ref, lse_ref, acc, m_s, l_s):
    b = pl.program_id(0) * per + chunk

    def visit(kb, diag):
        at = pl.multiple_of(info[nb + kb] * BLK, BLK)
        kpos = lax.broadcasted_iota(jnp.int32, (BLK, BLK), 0)
        ok = kpos >= (start_ref[...] - kb * BLK)
        if diag:
            ok = ok & (kpos <= lax.broadcasted_iota(jnp.int32, (BLK, BLK), 1))
        scores = [dot(kn_ref[h, pl.ds(at, BLK), :], q_ref[h]) for h in range(heads)]
        scores = [jnp.where(ok, s, NEG) for s in scores]
        top = jnp.concatenate([jnp.max(s, axis=0, keepdims=True) for s in scores], 0)
        if not diag:
            old = m_s[0:heads, :]
            top = jnp.maximum(old, top)
            fade = jnp.exp2((old - top) * SCALE2)
        m_s[0:heads, :] = top
        expo = [jnp.exp2((scores[h] - top[h : h + 1]) * SCALE2) for h in range(heads)]
        sums = jnp.concatenate([jnp.sum(e, axis=0, keepdims=True) for e in expo], 0)
        l_s[0:heads, :] = sums if diag else l_s[0:heads, :] * fade + sums
        for h in range(heads):
            new = dot(v_ref[h, :, pl.ds(at, BLK)], expo[h].astype(BF16))
            acc[h] = new if diag else acc[h] * fade[h : h + 1] + new

    visit(b, True)

    def step(kb, _):
        visit(kb, False)
        return 0

    lax.fori_loop(info[b], b, step, 0)
    for h in range(heads):
        total = l_s[h : h + 1, :]
        o_ref[h] = (acc[h] * (1.0 / total)).astype(BF16)
        lse_ref[h : h + 1, :] = m_s[h : h + 1, :] * SCALE2 + jnp.log2(total)


def attend(chunk, info, start, qkv, kn):
    heads, total = qkv.shape[0] // 3, qkv.shape[2]
    nb = total // BLK
    per = nb // SLOTS
    spec = pltpu.PrefetchScalarGridSpec(
        num_scalar_prefetch=1,
        grid=(SLOTS,),
        in_specs=[
            pl.BlockSpec((1, BLK), lambda i, s: (0, i * per + chunk)),
            pl.BlockSpec((heads, HEAD_DIM, BLK), lambda i, s: (0, 0, s[nb + i * per + chunk])),
            pl.BlockSpec((heads, total, HEAD_DIM), lambda i, s: (0, 0, 0)),
            pl.BlockSpec((heads, HEAD_DIM, total), lambda i, s: (2, 0, 0)),
        ],
        out_specs=[
            pl.BlockSpec((heads, HEAD_DIM, BLK), lambda i, s: (0, 0, i)),
            pl.BlockSpec((8, BLK), lambda i, s: (0, i)),
        ],
        scratch_shapes=[
            pltpu.VMEM((heads, HEAD_DIM, BLK), F32),
            pltpu.VMEM((8, BLK), F32),
            pltpu.VMEM((8, BLK), F32),
        ],
    )
    return pl.pallas_call(
        functools.partial(attend_kernel, heads, nb, per, chunk),
        grid_spec=spec,
        out_shape=[
            jax.ShapeDtypeStruct((heads, HEAD_DIM, SLOTS * BLK), BF16),
            jax.ShapeDtypeStruct((8, SLOTS * BLK), F32),
        ],
        compiler_params=params(),
        cost_estimate=cost(9.5),
        name="attend",
    )(info, start, qkv, kn, qkv)


def attend_back_kernel(heads, nb, per, info, start_ref, q_ref, k_ref, kn_ref, vn_ref, do_ref, stat_ref, out_ref, dq_s, dk_s, dv_s):
    j = pl.program_id(0)

    def place(b):
        return pl.multiple_of(info[nb + b] * BLK, BLK)

    def ordered(b):
        return pl.multiple_of(((b % per) * SLOTS + b // per) * BLK, BLK)

    @pl.when(j == 0)
    def _():
        dq_s[...] = jnp.zeros_like(dq_s)

    def visit(b, diag):
        at = place(b)
        mine = ordered(b)
        kpos = lax.broadcasted_iota(jnp.int32, (BLK, BLK), 0)
        ok = kpos >= (start_ref[:, pl.ds(pl.multiple_of(b * BLK, BLK), BLK)] - j * BLK)
        if diag:
            ok = ok & (kpos <= lax.broadcasted_iota(jnp.int32, (BLK, BLK), 1))
        every = range(heads)
        query = [q_ref[h, :, pl.ds(at, BLK)] for h in every]
        grad = [do_ref[h, :, pl.ds(mine, BLK)] for h in every]
        scores = [dot(kn_ref[h], query[h]) for h in every]
        prob_grad = [dot(vn_ref[h], grad[h]) for h in every]
        probs = [
            jnp.where(ok, jnp.exp2(scores[h] * SCALE2 - stat_ref[h : h + 1, pl.ds(mine, BLK)]), 0.0) for h in every
        ]
        score_grad = [
            (probs[h] * (prob_grad[h] - stat_ref[8 + h : 9 + h, pl.ds(mine, BLK)])).astype(BF16) for h in every
        ]
        dv = [dot(grad[h], probs[h].astype(BF16), NT) for h in every]
        dk = [dot(query[h], score_grad[h], NT) for h in every]
        dq = [dot(k_ref[h], score_grad[h]) for h in every]
        for h in every:
            if diag:
                dv_s[h] = dv[h]
                dk_s[h] = dk[h]
            else:
                dv_s[h] += dv[h]
                dk_s[h] += dk[h]
            dq_s[h, :, pl.ds(at, BLK)] += dq[h]

    visit(j, True)

    def step(b, _):
        visit(b, False)
        return 0

    lax.fori_loop(j + 1, info[2 * nb + j] + 1, step, 0)
    at = place(j)
    for h in range(heads):
        out_ref[h] = (dq_s[h, :, pl.ds(at, BLK)] * SCALE).astype(BF16)
        out_ref[heads + h] = (dk_s[h] * SCALE).astype(BF16)
        out_ref[2 * heads + h] = dv_s[h].astype(BF16)


def attend_back(info, start, qkv, kn, vn, do, stat):
    heads, total = qkv.shape[0] // 3, qkv.shape[2]
    nb = total // BLK
    per = nb // SLOTS
    whole = pl.BlockSpec((heads, HEAD_DIM, total), lambda j, s: (0, 0, 0))
    block = lambda a: pl.BlockSpec((heads, HEAD_DIM, BLK), lambda j, s: (a, 0, s[nb + j]))
    tall = pl.BlockSpec((heads, BLK, HEAD_DIM), lambda j, s: (0, s[nb + j], 0))
    spec = pltpu.PrefetchScalarGridSpec(
        num_scalar_prefetch=1,
        grid=(nb,),
        in_specs=[
            pl.BlockSpec((1, total), lambda j, s: (0, 0)),
            whole,
            block(1),
            tall,
            tall,
            whole,
            pl.BlockSpec((16, total), lambda j, s: (0, 0)),
        ],
        out_specs=pl.BlockSpec((3 * heads, HEAD_DIM, BLK), lambda j, s: (0, 0, s[nb + j])),
        scratch_shapes=[
            pltpu.VMEM((heads, HEAD_DIM, total), F32),
            pltpu.VMEM((heads, HEAD_DIM, BLK), F32),
            pltpu.VMEM((heads, HEAD_DIM, BLK), F32),
        ],
    )
    return pl.pallas_call(
        functools.partial(attend_back_kernel, heads, nb, per),
        grid_spec=spec,
        out_shape=jax.ShapeDtypeStruct((3 * heads, HEAD_DIM, total), BF16),
        compiler_params=params(),
        cost_estimate=cost(20),
        name="attend_back",
    )(info, start, qkv, qkv, kn, vn, do, stat)


def join_kernel(chunks, *refs):
    do_out, stat_out = refs[-2:]
    h = pl.program_id(0)
    wide = SLOTS * BLK
    for c in range(chunks):
        a, near, far, o, lse = refs[5 * c : 5 * c + 5]
        cut = slice(c * wide, (c + 1) * wide)
        do = (a[0].astype(F32) + near[0].astype(F32) + far[0].astype(F32)).astype(BF16)
        do_out[0, :, cut] = do
        stat_out[pl.ds(h + 8, 1), cut] = jnp.sum(o[0].astype(F32) * do.astype(F32), axis=0, keepdims=True)

        @pl.when(h == 0)
        def _():
            stat_out[0:8, cut] = lse[...]


def join(parts):
    heads, _, wide = parts[0][3].shape
    total = wide * len(parts)
    in_specs, args = [], []
    block = pl.BlockSpec((1, HEAD_DIM, wide), lambda h: (h, 0, 0))
    for a, near, far, o, lse in parts:
        args += [
            a.reshape(heads, HEAD_DIM, wide),
            near.reshape(heads, HEAD_DIM, wide),
            far.reshape(heads, HEAD_DIM, wide),
            o,
            lse,
        ]
        in_specs += [
            block,
            block,
            block,
            block,
            pl.BlockSpec((8, wide), lambda h: (0, 0)),
        ]
    return pl.pallas_call(
        functools.partial(join_kernel, len(parts)),
        grid=(heads,),
        in_specs=in_specs,
        out_specs=[pl.BlockSpec((1, HEAD_DIM, total), lambda h: (h, 0, 0)), pl.BlockSpec((16, total), lambda h: (0, 0))],
        out_shape=[jax.ShapeDtypeStruct((heads, HEAD_DIM, total), BF16), jax.ShapeDtypeStruct((16, total), F32)],
        compiler_params=params(),
        cost_estimate=cost(5),
        name="join",
    )(*args)


def to_slot(s, value_ref, outs):
    for k in range(SLOTS):

        @pl.when(s == k)
        def _():
            outs[k][...] = value_ref[...]


def add_to(first, ref, at, m, part):
    ref[at, m] = jnp.where(first, part, ref[at, m] + part)


def forward_kernel(info, x_ref, *refs):
    att_refs, refs = refs[:SLOTS], refs[SLOTS:]
    g_refs = refs[:SLOTS]
    wot, vec_ref = refs[SLOTS : SLOTS + 2]
    far_weights = refs[SLOTS + 2 : SLOTS + 5]
    h_out, act_out, pg_out, g_out, n_out, root_out, sum_out, own_out = refs[-18:-10]
    layer_outs = refs[-10:-6]
    y1_s, layer_s, upt, wd, wdt, arrived = refs[-6:]
    s = pl.program_id(0)
    copies = [pltpu.make_async_copy(a, b, arrived.at[n]) for n, (a, b) in enumerate(zip(far_weights, (upt, wd, wdt)))]

    @pl.when(s == 0)
    def _():
        for copy in copies:
            copy.start()

    for k in range(SLOTS):

        @pl.when(s == k)
        def _():
            g_out[...] = g_refs[k][...]

    d = x_ref.shape[0]
    pieces = cuts(d, ROWS)
    att = jnp.concatenate([ref[...] for ref in att_refs], 0)
    total = 0.0
    for m in pieces:
        y1 = x_ref[m].astype(F32) + (dot(wot[m], att) + col(vec_ref, OUT_BIAS, m))
        y1_s[m] = y1
        total = total + jnp.sum(y1, axis=0, keepdims=True)
    mean = total * (1.0 / d)
    total = 0.0
    for m in pieces:
        center = y1_s[m] - mean
        total = total + jnp.sum(center * center, axis=0, keepdims=True)
    root = lax.rsqrt(total * (1.0 / d) + EPS)
    root_out[...] = jnp.broadcast_to(root, root_out.shape)
    for m in pieces:
        n = (y1_s[m] - mean) * root
        n_out[m] = n.astype(BF16)
        h_out[m] = (n * col(vec_ref, GAIN2, m) + col(vec_ref, SHIFT2, m)).astype(BF16)

    @pl.when(s == 0)
    def _():
        for copy in copies:
            copy.wait()

    h = h_out[...]
    g = g_out[...]
    for m in cuts(upt.shape[0], ROWS):
        pre = dot(upt[m], h) + col(vec_ref, UP_BIAS, m)
        act_grad = dot(wd[m], g)
        square = pre * pre
        t = jnp.tanh(pre * (GELU_C + (GELU_C * GELU_A) * square))
        half = 0.5 * (1.0 + t)
        act_out[m] = (pre * half).astype(BF16)
        slope = half + (0.5 * pre) * (1.0 - t * t) * (GELU_C + (3.0 * GELU_C * GELU_A) * square)
        pg = (act_grad * slope).astype(BF16)
        pg_out[m] = pg
        add_to(s == 0, sum_out, 0, m, fold(pg.astype(F32)))
    act = act_out[...]
    for m in pieces:
        layer_s[m] = dot(wdt[m], act).astype(BF16)
    to_slot(s, layer_s, layer_outs)

    @pl.when(s == 0)
    def _():
        own_out[...] = y1_s[...]


def forward(chunk, info, atts, x, gs, wot, upt, wd, wdt, vec, carry):
    d, total = x.shape
    f = upt.shape[0]
    wide = SLOTS * BLK
    dev = 3 * (total // BLK)
    keep = lambda a: pl.BlockSpec(a.shape, lambda s, i: (0,) * a.ndim, pipeline_mode=pl.Buffered(1))
    block = lambda r: pl.BlockSpec((r, BLK), lambda s, i: (0, s))
    mine = pl.BlockSpec((d, BLK), lambda s, i: (0, chunk))
    args = [info, x, *atts, *gs, wot, vec, upt, wd, wdt]
    in_specs = [pl.BlockSpec((d, BLK), lambda s, i: (0, chunk * SLOTS + s))]
    in_specs += [pl.BlockSpec((atts[0].shape[0], BLK), lambda s, i: (0, s ^ i[dev]))] * SLOTS
    in_specs += [pl.BlockSpec((d, BLK), lambda s, i: (0, 0))] * SLOTS + [keep(wot), keep(vec)]
    in_specs += [pl.BlockSpec(memory_space=pl.ANY)] * 3
    alias = {}
    if carry is not None:
        alias = {len(args) + n: 7 + n for n in range(len(carry))}
        in_specs += [pl.BlockSpec(memory_space=pl.ANY)] * len(carry)
        args += list(carry)
    spec = pltpu.PrefetchScalarGridSpec(
        num_scalar_prefetch=1,
        grid=(SLOTS,),
        in_specs=in_specs,
        out_specs=[
            block(d),
            block(f),
            block(f),
            block(d),
            block(d),
            block(8),
            pl.BlockSpec((1, f, 128), lambda s, i: (0, 0, 0)),
        ]
        + [mine] * 5,
        scratch_shapes=[pltpu.VMEM((d, BLK), F32), pltpu.VMEM((d, BLK), BF16)]
        + [pltpu.VMEM(a.shape, BF16) for a in (upt, wd, wdt)]
        + [pltpu.SemaphoreType.DMA((3,))],
    )
    shape = jax.ShapeDtypeStruct
    rows = total // SLOTS
    return pl.pallas_call(
        forward_kernel,
        grid_spec=spec,
        out_shape=[
            shape((d, wide), BF16),
            shape((f, wide), BF16),
            shape((f, wide), BF16),
            shape((d, wide), BF16),
            shape((d, wide), BF16),
            shape((8, wide), F32),
            shape((1, f, 128), F32),
            shape((d, rows), F32),
        ]
        + [shape((d, rows), BF16)] * SLOTS,
        input_output_aliases=alias,
        compiler_params=params(),
        cost_estimate=cost(26),
        name="forward",
    )(*args)


def backward_kernel(info, pg_ref, n_ref, root_ref, g_ref, up, *refs):
    vec_ref = refs[0]
    sum_out = refs[-16]
    attg_outs = refs[-15:-11]
    y1g_outs = refs[-11:-7]
    e_s, y1g_s = refs[-7:-5]
    wo, arrived = refs[-5:-1], refs[-1]
    s = pl.program_id(0)
    copies = [pltpu.make_async_copy(refs[1 + k], wo[k], arrived.at[k]) for k in range(SLOTS)]

    @pl.when(s == 0)
    def _():
        for copy in copies:
            copy.start()

    d = n_ref.shape[0]
    pieces = cuts(d, ROWS)
    pg = pg_ref[...]
    mean = 0.0
    tilt = 0.0
    for m in pieces:
        hg = dot(up[m], pg)
        n = n_ref[m].astype(F32)
        hn = hg * n
        gain = col(vec_ref, GAIN2, m)
        e = hg * gain
        e_s[m] = e
        mean = mean + jnp.sum(e, axis=0, keepdims=True)
        tilt = tilt + jnp.sum(hn * gain, axis=0, keepdims=True)
        add_to(s == 0, sum_out, 0, m, fold(hn))
        add_to(s == 0, sum_out, 1, m, fold(hg))
    mean = mean * (1.0 / d)
    tilt = tilt * (1.0 / d)
    root = root_ref[0:1]
    mine = jnp.where(s == 0, 1.0, 0.0)
    for m in pieces:
        y1g = root * (e_s[m] - mean - n_ref[m].astype(F32) * tilt) + g_ref[m].astype(F32) * mine
        y1g_s[m] = y1g.astype(BF16)
        add_to(s == 0, sum_out, 2, m, fold(y1g))

    @pl.when(s == 0)
    def _():
        for copy in copies:
            copy.wait()

    y1b = y1g_s[...]
    for k in range(SLOTS):
        attg_outs[k][...] = dot(wo[k][...], y1b).astype(BF16)
    to_slot(s, y1g_s, y1g_outs)


def backward(chunk, info, pg, n, root, g, up, wos, vec, carry):
    d, wide = n.shape
    f = up.shape[1]
    rows = wos[0].shape[0]
    dev = info.shape[0] - 1
    keep = lambda a: pl.BlockSpec(a.shape, lambda s, i: (0,) * a.ndim, pipeline_mode=pl.Buffered(1))
    block = lambda r: pl.BlockSpec((r, BLK), lambda s, i: (0, s))
    mine = pl.BlockSpec((d, BLK), lambda s, i: (0, chunk))
    ordered = pl.BlockSpec((rows, BLK), lambda s, i: (0, s ^ i[dev]))
    args = [info, pg, n, root, g, up, vec, *wos]
    in_specs = [block(f), block(d), block(8), mine, keep(up), keep(vec)] + [pl.BlockSpec(memory_space=pl.ANY)] * SLOTS
    alias = {}
    if carry is not None:
        alias = {len(args) + n: 5 + n for n in range(len(carry))}
        in_specs += [pl.BlockSpec(memory_space=pl.ANY)] * len(carry)
        args += list(carry)
    spec = pltpu.PrefetchScalarGridSpec(
        num_scalar_prefetch=1,
        grid=(SLOTS,),
        in_specs=in_specs,
        out_specs=[pl.BlockSpec((3, d, 128), lambda s, i: (0, 0, 0))] + [ordered] * SLOTS + [mine] * SLOTS,
        scratch_shapes=[pltpu.VMEM((d, BLK), F32), pltpu.VMEM((d, BLK), BF16)]
        + [pltpu.VMEM(a.shape, BF16) for a in wos]
        + [pltpu.SemaphoreType.DMA((SLOTS,))],
    )
    shape = jax.ShapeDtypeStruct
    return pl.pallas_call(
        backward_kernel,
        grid_spec=spec,
        out_shape=[shape((3, d, 128), F32)] + [shape((rows, wide), BF16)] * SLOTS + [shape(g.shape, BF16)] * SLOTS,
        input_output_aliases=alias,
        compiler_params=params(),
        cost_estimate=cost(17),
        name="backward",
    )(*args)


def shard_rows(m):
    return -(-m // (8 * 16)) * 16


COLUMNS = 256


def outer_kernel(count, order, info, *refs):
    dp = info[0]
    outs = refs[2 * count :]
    total = None
    for n in range(count):
        part = dot(refs[2 * n][...], refs[2 * n + 1][...], NT)
        total = part if total is None else total + part
    m = total.shape[0]
    size = shard_rows(m)
    for shard in range(8):
        low, high = min(shard * size, m), min((shard + 1) * size, m)
        if low == high:
            continue
        slot = shard ^ dp
        at = jnp.where((slot & order[2]) != 0, 1, 0) + jnp.where((slot & order[1]) != 0, 2, 0)
        value = total[low:high].astype(BF16)
        if high - low < size:
            value = jnp.concatenate([value, jnp.zeros((size - (high - low), value.shape[1]), BF16)], 0)
        goes = (slot & order[0]) != 0
        for k, out in enumerate(outs):

            @pl.when(goes if k else jnp.logical_not(goes))
            def _():
                out[pl.ds(pl.multiple_of(at * size, 16), size)] = value


def outer(pairs, info, order):
    m, depth = pairs[0][0].shape
    n = pairs[0][1].shape[0]
    size = shard_rows(m)
    in_specs, args = [], []
    for a, b in pairs:
        in_specs.append(pl.BlockSpec((m, depth), lambda i, s: (0, 0), pipeline_mode=pl.Buffered(1)))
        in_specs.append(pl.BlockSpec((COLUMNS, depth), lambda i, s: (i, 0)))
        args += [a, b]
    spec = pltpu.PrefetchScalarGridSpec(
        num_scalar_prefetch=1,
        grid=(-(-n // COLUMNS),),
        in_specs=in_specs,
        out_specs=[pl.BlockSpec((4 * size, COLUMNS), lambda i, s: (0, i))] * 2,
    )
    return pl.pallas_call(
        functools.partial(outer_kernel, len(pairs), order),
        grid_spec=spec,
        out_shape=[jax.ShapeDtypeStruct((4 * size, n), BF16)] * 2,
        compiler_params=params(),
        cost_estimate=cost(8),
        name="outer",
    )(info, *args)


def attn_grad_kernel(a_ref, b_ref, out_ref, sum_ref):
    a = a_ref[...]
    out_ref[...] = dot(a, b_ref[...], NT).astype(BF16)

    @pl.when(pl.program_id(0) == 0)
    def _():
        sum_ref[...] = fold(a.astype(F32))


def attn_grad_call(dqkv, h1):
    m, total = dqkv.shape
    d = h1.shape[0]
    return pl.pallas_call(
        attn_grad_kernel,
        grid=(-(-d // COLUMNS),),
        in_specs=[
            pl.BlockSpec((m, total), lambda i: (0, 0), pipeline_mode=pl.Buffered(1)),
            pl.BlockSpec((COLUMNS, total), lambda i: (i, 0)),
        ],
        out_specs=[pl.BlockSpec((m, COLUMNS), lambda i: (0, i)), pl.BlockSpec((m, 128), lambda i: (0, 0))],
        out_shape=[jax.ShapeDtypeStruct((m, d), BF16), jax.ShapeDtypeStruct((m, 128), F32)],
        compiler_params=params(),
        cost_estimate=cost(7),
        name="attn_grad_call",
    )(dqkv, h1)


def halve_kernel(keep_ref, recv_ref, keep_out, send_out):
    i = pl.program_id(0)
    total = (keep_ref[...].astype(F32) + recv_ref[...].astype(F32)).astype(BF16)

    @pl.when(i == 0)
    def _():
        keep_out[...] = total

    @pl.when(i == 1)
    def _():
        send_out[...] = total


def halve(keep, recv):
    size, n = keep.shape[0] // 2, keep.shape[1]
    block = pl.BlockSpec((size, n), lambda i: (i, 0))
    return pl.pallas_call(
        halve_kernel,
        grid=(2,),
        in_specs=[block, block],
        out_specs=[pl.BlockSpec((size, n), lambda i: (0, 0))] * 2,
        out_shape=[jax.ShapeDtypeStruct((size, n), BF16)] * 2,
        compiler_params=params(),
        cost_estimate=cost(2.5),
        name="halve",
    )(keep, recv)


def slot_of(i, order):
    return jnp.where(i & 1, order[2], 0) | jnp.where(i & 2, order[1], 0) | jnp.where(i & 4, order[0], 0)


def place_kernel(count, info, one, two, four, eight, *rest):
    i = pl.program_id(0)
    outs = rest[-count:]
    for ref, low, high in ((one, 0, 1), (two, 1, 2), (four, 2, 4), (eight, 4, 8)):

        @pl.when((i >= low) & (i < high))
        def _():
            size = ref.shape[0] // count
            for n, out in enumerate(outs):
                out[...] = ref[n * size : (n + 1) * size].astype(F32)


def place(parts, info, order, first, rows, carry, extra_rows):
    size, n = parts[0].shape
    count = 2 if extra_rows else 1
    half = size // count
    start = first // half
    near = lambda at, many: pl.BlockSpec((size, n), lambda i, s: (jnp.clip(i - at, 0, many - 1), 0))
    in_specs = [near(0, 1), near(1, 1), near(2, 2), near(4, 4)]
    args = list(parts)
    alias = {}
    if carry is not None:
        in_specs.append(pl.BlockSpec(memory_space=pl.ANY))
        args.append(carry)
        alias = {5: 0}
    out_specs = [pl.BlockSpec((half, n), lambda i, s: (start + (slot_of(i, order) ^ s[0]), 0))]
    out_shape = [jax.ShapeDtypeStruct((rows, n), F32)]
    if extra_rows:
        out_specs.append(pl.BlockSpec((half, n), lambda i, s: (slot_of(i, order) ^ s[0], 0)))
        out_shape.append(jax.ShapeDtypeStruct((8 * half, n), F32))
    spec = pltpu.PrefetchScalarGridSpec(num_scalar_prefetch=1, grid=(8,), in_specs=in_specs, out_specs=out_specs)
    out = pl.pallas_call(
        functools.partial(place_kernel, count),
        grid_spec=spec,
        out_shape=out_shape,
        input_output_aliases=alias,
        compiler_params=params(),
        cost_estimate=cost(6.5),
        name="place",
    )(info, *args)
    return (out[0], out[1][:extra_rows]) if extra_rows else out[0]


def swap_dp(v, k):
    return lax.ppermute(v, "dp", [(i, i ^ k) for i in range(8)])


class CellSum:
    def __init__(self, line, keep, send, info, order, rows, first=0, extra_rows=0):
        self.line, self.keep, self.info, self.order = line, keep, info, order
        self.rows, self.first, self.extra_rows = rows, first, extra_rows
        self.stage = 0
        self.known = lax.axis_size("dp") == 8
        if not self.known:
            both = lax.psum(jnp.stack([keep, send]), "dp")
            size = keep.shape[0] // 4
            self.parts = [both[0, :size], both[0, size : 2 * size], both[0, 2 * size :], both[1]]
            self.got = both[1]
            return
        self.got = swap_dp(send, order[0])

    def step(self):
        if not self.known:
            return
        self.stage += 1
        k1, k2, k3 = self.order
        if self.stage < 3:
            self.keep, send = self.line(halve, self.keep, self.got)
            self.got = swap_dp(send, k2 if self.stage == 1 else k3)
        elif self.stage == 3:
            self.parts = [self.line(lambda a, b: add(BF16, a, b), self.keep, self.got)]
            self.got = swap_dp(self.parts[0], k3)
        else:
            self.parts.append(self.got)
            self.got = swap_dp(self.line(stack, *self.parts), k2 if self.stage == 4 else k1)
            if self.stage == 5:
                self.parts.append(self.got)

    def finish(self, carry=None):
        return self.line(
            lambda p, *c: place(
                p, self.info, self.order, self.first, self.rows, c[0] if c else None, self.extra_rows
            ),
            self.parts,
            *([] if carry is None else [carry]),
        )


class Rounds:
    def __init__(self, line, v, over_tensor=False):
        self.line, self.v = line, v
        self.todo = [(swap_dp, 1), (swap_dp, 2), (swap_dp, 4)]
        if lax.axis_size("dp") != 8:
            self.v = lax.psum(v.astype(F32), "dp").astype(v.dtype)
            self.todo = []
        self.cells = self.v
        if over_tensor:
            self.todo += [(swap, 1), (swap, 2)]
        self.send()

    def send(self):
        self.got = None
        if self.todo:
            self.move, k = self.todo.pop(0)
            self.got = self.move(self.v, k)

    def step(self):
        if self.got is None:
            return
        self.v = self.line(lambda a, b: add(a.dtype, a, b), self.v, self.got)
        if self.move is swap_dp:
            self.cells = self.v
        self.send()


def out_grad_kernel(chunks, dev_at, info, *refs):
    atts, y1gs, outs = refs[: chunks * SLOTS], refs[chunks * SLOTS : -SLOTS], refs[-SLOTS:]
    dev = info[dev_at]
    totals = [None] * SLOTS
    for c in range(chunks):
        for s in range(SLOTS):
            at = pl.multiple_of((s ^ dev) * BLK, BLK)
            y1g = y1gs[s][:, c * BLK : (c + 1) * BLK]
            for n in range(SLOTS):
                part = dot(atts[c * SLOTS + n][:, pl.ds(at, BLK)], y1g, NT)
                totals[n] = part if totals[n] is None else totals[n] + part
    for n in range(SLOTS):
        outs[n][...] = totals[n].astype(BF16)


def out_grad_call(info, atts, y1gs):
    rows = atts[0][0].shape[0]
    d, wide = y1gs[0].shape
    heads = [a for chunk in atts for a in chunk]
    spec = pltpu.PrefetchScalarGridSpec(
        num_scalar_prefetch=1,
        grid=(-(-d // COLUMNS),),
        in_specs=[pl.BlockSpec(a.shape, lambda i, s: (0, 0), pipeline_mode=pl.Buffered(1)) for a in heads]
        + [pl.BlockSpec((COLUMNS, wide), lambda i, s: (i, 0))] * SLOTS,
        out_specs=[pl.BlockSpec((rows, COLUMNS), lambda i, s: (0, i))] * SLOTS,
    )
    return pl.pallas_call(
        functools.partial(out_grad_kernel, len(atts), 3 * wide * SLOTS // BLK),
        grid_spec=spec,
        out_shape=[jax.ShapeDtypeStruct((rows, d), BF16)] * SLOTS,
        compiler_params=params(),
        cost_estimate=cost(9),
        name="out_grad_call",
    )(info, *heads, *y1gs)


def h1_grad_kernel(w_ref, dqkv_ref, x_ref, sum_ref, *outs):
    s = pl.program_id(1)
    first = (s == 0) & (pl.program_id(0) == 0)
    hg_s = outs[-1]
    d = x_ref.shape[0]
    pieces = cuts(d, ROWS)
    total = 0.0
    for m in pieces:
        total = total + jnp.sum(x_ref[m].astype(F32), axis=0, keepdims=True)
    mean = total * (1.0 / d)
    total = 0.0
    for m in pieces:
        center = x_ref[m].astype(F32) - mean
        total = total + jnp.sum(center * center, axis=0, keepdims=True)
    root = lax.rsqrt(total * (1.0 / d) + EPS)
    dqkv = dqkv_ref[...]
    for m in pieces:
        hg = dot(w_ref[m], dqkv)
        n = (x_ref[m].astype(F32) - mean) * root
        hg_s[m] = hg.astype(BF16)
        add_to(first, sum_ref, 0, m, fold(hg * n))
        add_to(first, sum_ref, 1, m, fold(hg))
    to_slot(s, hg_s, outs[:SLOTS])


def h1_grad_call(w, dqkv, x):
    d, total = x.shape
    per = total // (BLK * SLOTS)
    m = w.shape[1]
    at = lambda p, s: (0, p * SLOTS + s)
    mine = pl.BlockSpec((d, BLK), lambda p, s: (0, p))
    return pl.pallas_call(
        h1_grad_kernel,
        grid=(per, SLOTS),
        in_specs=[
            pl.BlockSpec((d, m), lambda p, s: (0, 0), pipeline_mode=pl.Buffered(1)),
            pl.BlockSpec((m, BLK), at),
            pl.BlockSpec((d, BLK), at),
        ],
        out_specs=[pl.BlockSpec((2, d, 128), lambda p, s: (0, 0, 0))] + [mine] * SLOTS,
        out_shape=[jax.ShapeDtypeStruct((2, d, 128), F32)]
        + [jax.ShapeDtypeStruct((d, per * BLK), BF16)] * SLOTS,
        scratch_shapes=[pltpu.VMEM((d, BLK), BF16)],
        compiler_params=params(),
        cost_estimate=cost(13),
        name="h1_grad_call",
    )(w, dqkv, x)


def input_grad_kernel(x_ref, a_ref, b_ref, c_ref, d_ref, y1g_ref, gain_ref, out_ref):
    n, root = normal(x_ref[...].astype(F32))
    total = a_ref[...].astype(F32) + b_ref[...].astype(F32) + c_ref[...].astype(F32) + d_ref[...].astype(F32)
    e = total * gain_ref[:, GAIN1 : GAIN1 + 1]
    e = root * (e - jnp.mean(e, axis=0, keepdims=True) - n * jnp.mean(e * n, axis=0, keepdims=True))
    out_ref[...] = (y1g_ref[...] + e).astype(BF16)


def input_grad_call(x, a, b, c, d4, y1g, gain):
    d, rows = x.shape
    block = pl.BlockSpec((d, 128), lambda i: (0, i))
    return pl.pallas_call(
        input_grad_kernel,
        grid=(rows // 128,),
        in_specs=[block] * 6 + [pl.BlockSpec(gain.shape, lambda i: (0, 0))],
        out_specs=block,
        out_shape=jax.ShapeDtypeStruct((d, rows), BF16),
        compiler_params=params(),
        cost_estimate=cost(6),
        name="input_grad_call",
    )(x, a, b, c, d4, y1g, gain)


def layer_kernel(own_ref, a_ref, b_ref, c_ref, vec_ref, out_ref):
    total = a_ref[...].astype(F32) + b_ref[...].astype(F32) + c_ref[...].astype(F32)
    out_ref[...] = (own_ref[...] + total + vec_ref[:, DOWN_BIAS : DOWN_BIAS + 1]).astype(BF16)


def layer_call(own, a, b, c, vec):
    d, rows = own.shape
    block = pl.BlockSpec((d, 128), lambda i: (0, i))
    return pl.pallas_call(
        layer_kernel,
        grid=(rows // 128,),
        in_specs=[block] * 4 + [pl.BlockSpec(vec.shape, lambda i: (0, 0))],
        out_specs=block,
        out_shape=jax.ShapeDtypeStruct((d, rows), BF16),
        compiler_params=params(),
        cost_estimate=cost(3),
        name="layer_call",
    )(own, a, b, c, vec)


def small_kernel(chunks, width, sum1_ref, *refs):
    sums, ups, (qkv_ref, g_ref, out_ref) = refs[:chunks], refs[chunks : 2 * chunks], refs[2 * chunks :]
    across = lambda v: jnp.sum(v, axis=1, keepdims=True)
    columns = [across(sum1_ref[0]), across(sum1_ref[1])]
    columns += [across(sum(ref[n] for ref in sums)) for n in range(3)]
    columns += [across(g_ref[...].astype(F32)), across(sum(ref[0] for ref in ups))]
    d = g_ref.shape[0]
    qv = jnp.concatenate([qkv_ref[0:width], qkv_ref[2 * width : 3 * width]], 0)
    qv = jnp.concatenate([across(qv), jnp.zeros((d - 2 * width, 1), F32)], 0)
    out_ref[...] = jnp.concatenate([v.T for v in columns + [qv]], 0)


def small_sums(sum1, sums, up_sums, qkv_sum, g):
    return pl.pallas_call(
        functools.partial(small_kernel, len(sums), qkv_sum.shape[0] // 3),
        out_shape=jax.ShapeDtypeStruct((8, g.shape[0]), F32),
        compiler_params=params(),
        cost_estimate=cost(5),
        name="small_sums",
    )(sum1, *sums, *up_sums, qkv_sum, g)


def swap(v, k):
    return lax.ppermute(v, "tensor", [(i, i ^ k) for i in range(SLOTS)])


def after(v, *done):
    return lax.optimization_barrier((v, done))[0]


class Line:
    def __init__(self):
        self.last = []

    def __call__(self, step, *args):
        args, _ = lax.optimization_barrier((args, self.last))
        out = step(*args)
        self.last = jax.tree.leaves(out)
        return out

    def wait(self, *values):
        self.last = self.last + jax.tree.leaves(values)

    def pin(self, v, *also):
        return after(v, self.last, also)


class Gather:
    def __init__(self, v):
        self.own, self.side, self.across = v, swap(v, 1), swap(v, 2)

    def finish(self, line):
        self.corner = swap(line.pin(self.across), 1)
        return self

    def all(self):
        return self.own, self.side, self.across, self.corner


def plus(a, b):
    return a.astype(F32) + b.astype(F32)


def plus_low(a, b):
    return plus(a, b).astype(BF16)


def add_kernel(*refs):
    total = None
    for ref in refs[:-1]:
        v = (ref[0] if len(ref.shape) == 3 else ref[...]).astype(F32)
        total = v if total is None else total + v
    refs[-1][...] = total.astype(refs[-1].dtype)


def add(dtype, *terms):
    rows, columns = terms[0].shape
    size = rows // 2 if rows % 32 == 0 and rows * columns > 1 << 18 else rows
    in_specs, args = [], []
    for term in terms:
        if isinstance(term, tuple):
            in_specs.append(pl.BlockSpec((1, size, columns), functools.partial(lambda at, i: (at, i, 0), term[1])))
            args.append(term[0])
        else:
            in_specs.append(pl.BlockSpec((size, columns), lambda i: (i, 0)))
            args.append(term)
    return pl.pallas_call(
        add_kernel,
        grid=(rows // size,),
        in_specs=in_specs,
        out_specs=pl.BlockSpec((size, columns), lambda i: (i, 0)),
        out_shape=jax.ShapeDtypeStruct((rows, columns), dtype),
        compiler_params=params(),
        cost_estimate=cost(2.3),
        name="add",
    )(*args)


class GroupSum:
    def __init__(self, line, parts):
        self.line, self.parts = line, parts
        self.side = swap(line.pin(parts[3]), 1)

    def step(self, wait=True):
        self.far = swap(self.line(lambda a, b: add(BF16, a, b), self.parts[2], self.side), 2)
        self.near = swap(self.line.pin(self.parts[1]), 1)
        if wait:
            self.line.wait(self.near)

    def terms(self):
        return self.parts[0], self.near, self.far


def stack_kernel(*refs):
    at = 0
    for ref in refs[:-1]:
        refs[-1][at : at + ref.shape[0]] = ref[...]
        at += ref.shape[0]


def stack(*parts):
    return pl.pallas_call(
        stack_kernel,
        out_shape=jax.ShapeDtypeStruct((sum(p.shape[0] for p in parts), parts[0].shape[1]), parts[0].dtype),
        compiler_params=params(),
        cost_estimate=cost(2),
        name="stack",
    )(*parts)


def token_starts(lengths, offsets, total, dev):
    pos = jnp.arange(total, dtype=jnp.int32)[:, None]
    inside = (pos >= offsets[None]) & (pos < (offsets + lengths)[None])
    first = jnp.max(jnp.where(inside, offsets[None], -1), axis=1)
    start = jnp.where(first >= 0, first, pos[:, 0])
    nb = total // BLK
    per = nb // SLOTS
    b = jnp.arange(nb, dtype=jnp.int32)
    first_key = start.reshape(nb, BLK)[:, 0] // BLK
    place = (b % per) * SLOTS + ((b // per) ^ dev)
    last_query = jnp.max(jnp.where(first_key[None, :] <= b[:, None], b[None, :], 0), axis=1)
    info = jnp.concatenate([first_key, place, last_query, jnp.full((1,), dev)])
    return start[None], info.astype(jnp.int32)


def body(
    tokens,
    cotangent,
    ln1_gain,
    ln1_bias,
    attn_weight,
    qv_bias,
    out_weight,
    out_bias,
    ln2_gain,
    ln2_bias,
    up_weight,
    up_bias,
    down_weight,
    down_bias,
    cell_lengths,
    cell_offsets,
):
    rows, d = tokens.shape
    width = attn_weight.shape[2]
    heads = width // HEAD_DIM
    total = rows * SLOTS
    per = rows // BLK
    dev = lax.axis_index("tensor")
    start, info = token_starts(cell_lengths[0], cell_offsets[0], total, dev)

    whole_dp = lax.axis_size("dp") == 8
    dp_info = jnp.full((1,), lax.axis_index("dp") if whole_dp else 0, jnp.int32)

    line = Line()
    x_own = tokens.T
    g_own = cotangent.T
    x_go = Gather(x_own)

    w_in = attn_weight.transpose(1, 2, 0)
    zero = jnp.zeros_like(ln1_gain)
    rows8 = jnp.stack([ln1_gain, ln1_bias, out_bias, ln2_gain, ln2_bias, up_bias, down_bias, zero])
    bias8 = jnp.zeros((8, width), F32).at[0].set(qv_bias[0]).at[2].set(qv_bias[1])
    upt, wdt, w_back, vec, bias, *g_cuts = line(
        turn, g_own, up_weight, down_weight, w_in.reshape(3 * width, d), rows8, bias8
    )
    carry = line(lambda a, b: qkv_call(0, a, b, w_in, vec, bias, None), x_own, x_go.side)
    wo_go = Gather(line.pin(out_weight, x_go.across))
    g_go = [Gather(line.pin(g_cuts[0], x_go.across))]
    x_parts = x_go.finish(line).all()
    x_all, h1, qkv, kn, vn = line(lambda a, b, c: qkv_call(1, a, b, w_in, vec, bias, c), x_parts[2], x_parts[3], carry)
    chunks = range(per)
    fronts, att_go = [], []
    for c in chunks:
        fronts.append(line(functools.partial(attend, c), info, start, qkv, kn))
        if c == 0:
            line.wait(wo_go.across, g_go[0].across)
        att_go.append(Gather(line.pin(fronts[c][0]).reshape(width, SLOTS * BLK)))
        if c == 0:
            wo_parts = wo_go.finish(line).all()
    wot = line(turn_pieces, *wo_parts)
    g_parts = [g_go[0].finish(line).all()]
    atts, ahead = [], []
    for c in chunks:
        atts.append(att_go[c].finish(line).all())
        if c > 0:
            g_parts.append(g_go[c].finish(line).all())
        if c + 1 < per:
            g_go.append(Gather(line.pin(g_cuts[c + 1], atts[c][2])))
        ahead.append(
            line(
                functools.partial(forward, c),
                info,
                atts[c],
                x_all,
                g_parts[c],
                wot,
                upt,
                down_weight,
                wdt,
                vec,
                ahead[-1][7:] if c else None,
            )
        )
    h2s, acts, pgs, gs, ns, roots, up_sums = zip(*[m[:7] for m in ahead])
    own, *layer_parts = ahead[-1][7:]
    flat = lambda a, b: list(zip(a, b))
    down_order, up_order = (2, 1, 4), (2, 1, 4)
    f = down_weight.shape[0]
    layer_sum = GroupSum(line, layer_parts)
    down = CellSum(line, *line(lambda a, b: outer(flat(a, b), dp_info, down_order), acts, gs), dp_info, down_order, f)
    layer_sum.step(False)
    up = CellSum(line, *line(lambda a, b: outer(flat(a, b), dp_info, up_order), h2s, pgs), dp_info, up_order, d)

    back, attgs = [], []
    for c in chunks:
        carry = back[-1][1 + SLOTS :] if c else None
        back.append(
            line(functools.partial(backward, c), info, pgs[c], ns[c], roots[c], g_own, up_weight, wo_parts, vec, carry)
        )
        if c:
            line.wait(attgs[-1].far, down.got, up.got)
            up.step()
        else:
            line.wait(layer_sum.far, layer_sum.near, down.got)
        down.step()
        attgs.append(GroupSum(line, back[c][1 : 1 + SLOTS]))
        attgs[c].step()
    y1g_parts = back[-1][1 + SLOTS :]
    y1g = GroupSum(line, y1g_parts)
    out_parts = line(out_grad_call, info, atts, y1g_parts)
    line.wait(attgs[-1].far, down.got, up.got, y1g.side)
    out_terms = [out_parts[0]] + [swap(line.pin(out_parts[k]), k) for k in (1, 2, 3)]
    down.step()
    up.step()
    do, stat = line(join, [a.terms() + tuple(f) for a, f in zip(attgs, fronts)])
    dqkv = line(attend_back, info, start, qkv, kn, vn, do, stat).reshape(3 * width, total)
    line.wait(down.got, up.got, out_terms)
    down.step()
    up.step()
    attn_grad, qkv_sum = line(attn_grad_call, dqkv, h1)
    line.wait(down.got, up.got)
    out_grad = line(lambda *v: add(BF16, *v), *out_terms)
    late = lax.psum((attn_grad, out_grad), "dp")
    y1g.step(False)
    sum1, *h1_parts = line(h1_grad_call, w_back, dqkv, x_all)
    line.wait(y1g.near)
    up.step()
    down.step()
    small = line(small_sums, sum1, [b[0] for b in back], up_sums, qkv_sum, g_own)
    layer = line(layer_call, own, *layer_sum.terms(), vec)
    line.wait(up.got, y1g.far)
    h1g = [h1_parts[0]] + [swap(line.pin(h1_parts[k]), k) for k in (1, 2, 3)]
    up.step()
    y1_grad = line(lambda *v: add(F32, *v), *y1g.terms())
    line.wait(down.got)
    down_grad = down.finish()
    small = Rounds(line, line.pin(small), True)
    line.wait(h1g)
    input_grad = line(input_grad_call, x_own, *h1g, y1_grad, vec)
    small.step()
    small.step()
    line.wait(up.got)
    up_grad = up.finish()
    small.step()
    small.step()
    small.step()
    line.wait(late)
    attn_grad, out_grad = (v.astype(F32) for v in line(lambda a, b: (a, b), *late))
    small, own_small = small.v, small.cells[6:]
    return (
        layer.T,
        input_grad.T,
        small[0],
        small[1],
        attn_grad.reshape(3, width, d).transpose(2, 0, 1),
        own_small[1, : 2 * width].reshape(2, width),
        out_grad,
        small[4],
        small[2],
        small[3],
        up_grad,
        own_small[0],
        down_grad,
        small[5],
    )


def solution(mesh):
    rows = P(("dp", "tensor"), None)
    in_specs = (
        rows,
        rows,
        P(),
        P(),
        P(None, None, "tensor"),
        P(None, "tensor"),
        P("tensor", None),
        P(),
        P(),
        P(),
        P(None, "tensor"),
        P("tensor"),
        P("tensor", None),
        P(),
        P("dp", None),
        P("dp", None),
    )
    out_specs = (
        rows,
        rows,
        P(),
        P(),
        P(None, None, "tensor"),
        P(None, "tensor"),
        P("tensor", None),
        P(),
        P(),
        P(),
        P(None, "tensor"),
        P("tensor"),
        P("tensor", None),
        P(),
    )
    return jax.shard_map(body, mesh=mesh, in_specs=in_specs, out_specs=out_specs, check_vma=False)
```

```python
import functools
import math

import jax
import jax.numpy as jnp
from jax import lax
from jax.experimental import pallas as pl
from jax.experimental.pallas import tpu as pltpu
from jax.sharding import PartitionSpec as P


HEAD_DIM = 56
BLK = 256
SLOTS = 4
NEG = -1e30
EPS = 1e-05
SCALE = 1.0 / math.sqrt(HEAD_DIM)
SCALE2 = SCALE * math.log2(math.e)
GELU_C = math.sqrt(2.0 / math.pi)
GELU_A = 0.044715
F32 = jnp.float32
BF16 = jnp.bfloat16
NT = ((1,), (1,))
ROWS = 224
GAIN1, SHIFT1, OUT_BIAS, GAIN2, SHIFT2, UP_BIAS, DOWN_BIAS = range(7)
VEC8 = True
ATT_PIECES = True
VMEM = 60 << 20
PACE = 0.0


def dot(a, b, dims=((1,), (0,))):
    return lax.dot_general(a, b, (dims, ((), ())), preferred_element_type=F32)


def params():
    return pltpu.CompilerParams(vmem_limit_bytes=VMEM)


def cost(microseconds):
    return pl.CostEstimate(flops=max(1, int(microseconds * PACE)), bytes_accessed=1, transcendentals=0)


def fold(v):
    total = v[:, :128]
    for at in range(128, v.shape[1], 128):
        total = total + v[:, at : at + 128]
    return total


def normal(x):
    center = x - jnp.mean(x, axis=0, keepdims=True)
    root = lax.rsqrt(jnp.mean(center * center, axis=0, keepdims=True) + EPS)
    return center * root, root


def turn_kernel(count, parts, *refs):
    for n in range(count):
        refs[count + 1 + n][...] = refs[n][...].T
    for n in range(parts):
        refs[2 * count + 1 + n][...] = refs[count][:, n * BLK : (n + 1) * BLK]


def turn(cut, *arrays):
    wide = max(a.shape[1] for a in arrays)
    steps = -(-wide // 256)
    in_specs, out_specs, outs = [], [], []
    for a in arrays:
        rows, columns = a.shape
        if columns == wide:
            in_specs.append(pl.BlockSpec((rows, 256), lambda i: (0, i)))
            out_specs.append(pl.BlockSpec((256, rows), lambda i: (i, 0)))
        else:
            in_specs.append(pl.BlockSpec((rows, columns), lambda i: (0, 0)))
            out_specs.append(pl.BlockSpec((columns, rows), lambda i: (0, 0)))
        outs.append(jax.ShapeDtypeStruct((columns, rows), a.dtype))
    rows, columns = cut.shape
    parts = columns // BLK
    size = -(-rows // (16 * steps)) * 16
    in_specs.append(pl.BlockSpec((size, columns), lambda i: (i, 0)))
    out_specs += [pl.BlockSpec((size, BLK), lambda i: (i, 0))] * parts
    outs += [jax.ShapeDtypeStruct((rows, BLK), cut.dtype)] * parts
    return pl.pallas_call(
        functools.partial(turn_kernel, len(arrays), parts),
        grid=(steps,),
        in_specs=in_specs,
        out_specs=out_specs,
        out_shape=outs,
        compiler_params=params(),
        cost_estimate=cost(8),
        name="turn",
    )(*arrays, cut)


def turn_pieces_kernel(*refs):
    refs[-1][...] = jnp.concatenate([ref[...] for ref in refs[:-1]], 0).T


def turn_pieces(*pieces):
    rows, columns = pieces[0].shape
    return pl.pallas_call(
        turn_pieces_kernel,
        grid=(-(-columns // 256),),
        in_specs=[pl.BlockSpec((rows, 256), lambda i: (0, i))] * len(pieces),
        out_specs=pl.BlockSpec((256, rows * len(pieces)), lambda i: (i, 0)),
        out_shape=jax.ShapeDtypeStruct((columns, rows * len(pieces)), pieces[0].dtype),
        compiler_params=params(),
        cost_estimate=cost(5),
        name="turn_pieces",
    )(*pieces)


def col(ref, at, m):
    return ref[m, at : at + 1]


def cuts(total, size):
    return [slice(at, min(at + size, total)) for at in range(0, total, size)]


def qkv_kernel(heads, a_ref, b_ref, w_ref, vec_ref, bias_ref, *rest):
    x_out, h_out, q_out, kn_out, vn_out = rest[-5:]
    x_out[:, :BLK] = a_ref[...]
    x_out[:, BLK:] = b_ref[...]
    d = x_out.shape[0]
    pieces = cuts(d, ROWS)
    total = 0.0
    for m in pieces:
        total = total + jnp.sum(x_out[m].astype(F32), axis=0, keepdims=True)
    mean = total * (1.0 / d)
    total = 0.0
    for m in pieces:
        center = x_out[m].astype(F32) - mean
        total = total + jnp.sum(center * center, axis=0, keepdims=True)
    root = lax.rsqrt(total * (1.0 / d) + EPS)
    for m in pieces:
        n = (x_out[m].astype(F32) - mean) * root
        h_out[m] = (n * col(vec_ref, GAIN1, m) + col(vec_ref, SHIFT1, m)).astype(BF16)
    h = h_out[...]
    for part in range(3):
        r = (dot(w_ref[part], h) + bias_ref[:, part : part + 1]).astype(BF16)
        r = r.reshape(heads, HEAD_DIM, r.shape[1])
        q_out[part * heads : (part + 1) * heads] = r
        if part > 0:
            out = kn_out if part == 1 else vn_out
            for h_at in range(heads):
                out[h_at] = r[h_at].T


def qkv_call(pair, a, b, w, vec, bias, carry):
    d, rows = a.shape
    per = rows // BLK
    total = rows * SLOTS
    heads = w.shape[1] // HEAD_DIM
    wide = 2 * BLK
    outs = [
        jax.ShapeDtypeStruct((d, total), BF16),
        jax.ShapeDtypeStruct((d, total), BF16),
        jax.ShapeDtypeStruct((3 * heads, HEAD_DIM, total), BF16),
        jax.ShapeDtypeStruct((heads, total, HEAD_DIM), BF16),
        jax.ShapeDtypeStruct((heads, total, HEAD_DIM), BF16),
    ]
    at = lambda p: p * (SLOTS // 2) + pair
    in_specs = [
        pl.BlockSpec((d, BLK), lambda p: (0, p)),
        pl.BlockSpec((d, BLK), lambda p: (0, p)),
        pl.BlockSpec(w.shape, lambda p: (0, 0, 0)),
        pl.BlockSpec(vec.shape, lambda p: (0, 0)),
        pl.BlockSpec(bias.shape, lambda p: (0, 0)),
    ]
    args = [a, b, w, vec, bias]
    alias = {}
    if carry is not None:
        alias = {len(args) + n: n for n in range(len(outs))}
        in_specs += [pl.BlockSpec(memory_space=pl.ANY)] * len(outs)
        args += list(carry)
    return pl.pallas_call(
        functools.partial(qkv_kernel, heads),
        grid=(per,),
        in_specs=in_specs,
        out_specs=[
            pl.BlockSpec((d, wide), lambda p: (0, at(p))),
            pl.BlockSpec((d, wide), lambda p: (0, at(p))),
            pl.BlockSpec((3 * heads, HEAD_DIM, wide), lambda p: (0, 0, at(p))),
            pl.BlockSpec((heads, wide, HEAD_DIM), lambda p: (0, at(p), 0)),
            pl.BlockSpec((heads, wide, HEAD_DIM), lambda p: (0, at(p), 0)),
        ],
        out_shape=outs,
        input_output_aliases=alias,
        compiler_params=params(),
        cost_estimate=cost(8),
        name="qkv_call",
    )(*args)


def attend_kernel(heads, nb, per, chunk, info, start_ref, q_ref, kn_ref, v_ref, o_ref, lse_ref, acc, m_s, l_s):
    b = pl.program_id(0) * per + chunk

    def visit(kb, diag):
        at = pl.multiple_of(info[nb + kb] * BLK, BLK)
        kpos = lax.broadcasted_iota(jnp.int32, (BLK, BLK), 0)
        ok = kpos >= (start_ref[...] - kb * BLK)
        if diag:
            ok = ok & (kpos <= lax.broadcasted_iota(jnp.int32, (BLK, BLK), 1))
        scores = [dot(kn_ref[h, pl.ds(at, BLK), :], q_ref[h]) for h in range(heads)]
        scores = [jnp.where(ok, s, NEG) for s in scores]
        top = jnp.concatenate([jnp.max(s, axis=0, keepdims=True) for s in scores], 0)
        if not diag:
            old = m_s[0:heads, :]
            top = jnp.maximum(old, top)
            fade = jnp.exp2((old - top) * SCALE2)
        m_s[0:heads, :] = top
        expo = [jnp.exp2((scores[h] - top[h : h + 1]) * SCALE2) for h in range(heads)]
        sums = jnp.concatenate([jnp.sum(e, axis=0, keepdims=True) for e in expo], 0)
        l_s[0:heads, :] = sums if diag else l_s[0:heads, :] * fade + sums
        for h in range(heads):
            new = dot(v_ref[h, :, pl.ds(at, BLK)], expo[h].astype(BF16))
            acc[h] = new if diag else acc[h] * fade[h : h + 1] + new

    visit(b, True)

    def step(kb, _):
        visit(kb, False)
        return 0

    lax.fori_loop(info[b], b, step, 0)
    for h in range(heads):
        total = l_s[h : h + 1, :]
        o_ref[h] = (acc[h] * (1.0 / total)).astype(BF16)
        lse_ref[h : h + 1, :] = m_s[h : h + 1, :] * SCALE2 + jnp.log2(total)


def attend(chunk, info, start, qkv, kn):
    heads, total = qkv.shape[0] // 3, qkv.shape[2]
    nb = total // BLK
    per = nb // SLOTS
    spec = pltpu.PrefetchScalarGridSpec(
        num_scalar_prefetch=1,
        grid=(SLOTS,),
        in_specs=[
            pl.BlockSpec((1, BLK), lambda i, s: (0, i * per + chunk)),
            pl.BlockSpec((heads, HEAD_DIM, BLK), lambda i, s: (0, 0, s[nb + i * per + chunk])),
            pl.BlockSpec((heads, total, HEAD_DIM), lambda i, s: (0, 0, 0)),
            pl.BlockSpec((heads, HEAD_DIM, total), lambda i, s: (2, 0, 0)),
        ],
        out_specs=[
            pl.BlockSpec((heads, HEAD_DIM, BLK), lambda i, s: (0, 0, i)),
            pl.BlockSpec((8, BLK), lambda i, s: (0, i)),
        ],
        scratch_shapes=[
            pltpu.VMEM((heads, HEAD_DIM, BLK), F32),
            pltpu.VMEM((8, BLK), F32),
            pltpu.VMEM((8, BLK), F32),
        ],
    )
    return pl.pallas_call(
        functools.partial(attend_kernel, heads, nb, per, chunk),
        grid_spec=spec,
        out_shape=[
            jax.ShapeDtypeStruct((heads, HEAD_DIM, SLOTS * BLK), BF16),
            jax.ShapeDtypeStruct((8, SLOTS * BLK), F32),
        ],
        compiler_params=params(),
        cost_estimate=cost(9.5),
        name="attend",
    )(info, start, qkv, kn, qkv)


def attend_back_kernel(heads, nb, per, info, start_ref, q_ref, k_ref, kn_ref, vn_ref, do_ref, stat_ref, out_ref, dq_s, dk_s, dv_s):
    j = pl.program_id(0)

    def place(b):
        return pl.multiple_of(info[nb + b] * BLK, BLK)

    def ordered(b):
        return pl.multiple_of(((b % per) * SLOTS + b // per) * BLK, BLK)

    @pl.when(j == 0)
    def _():
        dq_s[...] = jnp.zeros_like(dq_s)

    def visit(b, diag):
        at = place(b)
        mine = ordered(b)
        kpos = lax.broadcasted_iota(jnp.int32, (BLK, BLK), 0)
        ok = kpos >= (start_ref[:, pl.ds(pl.multiple_of(b * BLK, BLK), BLK)] - j * BLK)
        if diag:
            ok = ok & (kpos <= lax.broadcasted_iota(jnp.int32, (BLK, BLK), 1))
        every = range(heads)
        query = [q_ref[h, :, pl.ds(at, BLK)] for h in every]
        grad = [do_ref[h, :, pl.ds(mine, BLK)] for h in every]
        scores = [dot(kn_ref[h], query[h]) for h in every]
        prob_grad = [dot(vn_ref[h], grad[h]) for h in every]
        probs = [
            jnp.where(ok, jnp.exp2(scores[h] * SCALE2 - stat_ref[h : h + 1, pl.ds(mine, BLK)]), 0.0) for h in every
        ]
        score_grad = [
            (probs[h] * (prob_grad[h] - stat_ref[8 + h : 9 + h, pl.ds(mine, BLK)])).astype(BF16) for h in every
        ]
        dv = [dot(grad[h], probs[h].astype(BF16), NT) for h in every]
        dk = [dot(query[h], score_grad[h], NT) for h in every]
        dq = [dot(k_ref[h], score_grad[h]) for h in every]
        for h in every:
            if diag:
                dv_s[h] = dv[h]
                dk_s[h] = dk[h]
            else:
                dv_s[h] += dv[h]
                dk_s[h] += dk[h]
            dq_s[h, :, pl.ds(at, BLK)] += dq[h]

    visit(j, True)

    def step(b, _):
        visit(b, False)
        return 0

    lax.fori_loop(j + 1, info[2 * nb + j] + 1, step, 0)
    at = place(j)
    for h in range(heads):
        out_ref[h] = (dq_s[h, :, pl.ds(at, BLK)] * SCALE).astype(BF16)
        out_ref[heads + h] = (dk_s[h] * SCALE).astype(BF16)
        out_ref[2 * heads + h] = dv_s[h].astype(BF16)


def attend_back(info, start, qkv, kn, vn, do, stat):
    heads, total = qkv.shape[0] // 3, qkv.shape[2]
    nb = total // BLK
    per = nb // SLOTS
    whole = pl.BlockSpec((heads, HEAD_DIM, total), lambda j, s: (0, 0, 0))
    block = lambda a: pl.BlockSpec((heads, HEAD_DIM, BLK), lambda j, s: (a, 0, s[nb + j]))
    tall = pl.BlockSpec((heads, BLK, HEAD_DIM), lambda j, s: (0, s[nb + j], 0))
    spec = pltpu.PrefetchScalarGridSpec(
        num_scalar_prefetch=1,
        grid=(nb,),
        in_specs=[
            pl.BlockSpec((1, total), lambda j, s: (0, 0)),
            whole,
            block(1),
            tall,
            tall,
            whole,
            pl.BlockSpec((16, total), lambda j, s: (0, 0)),
        ],
        out_specs=pl.BlockSpec((3 * heads, HEAD_DIM, BLK), lambda j, s: (0, 0, s[nb + j])),
        scratch_shapes=[
            pltpu.VMEM((heads, HEAD_DIM, total), F32),
            pltpu.VMEM((heads, HEAD_DIM, BLK), F32),
            pltpu.VMEM((heads, HEAD_DIM, BLK), F32),
        ],
    )
    return pl.pallas_call(
        functools.partial(attend_back_kernel, heads, nb, per),
        grid_spec=spec,
        out_shape=jax.ShapeDtypeStruct((3 * heads, HEAD_DIM, total), BF16),
        compiler_params=params(),
        cost_estimate=cost(20),
        name="attend_back",
    )(info, start, qkv, qkv, kn, vn, do, stat)


def join_kernel(chunks, *refs):
    do_out, stat_out = refs[-2:]
    h = pl.program_id(0)
    wide = SLOTS * BLK
    for c in range(chunks):
        a, near, far, o, lse = refs[5 * c : 5 * c + 5]
        cut = slice(c * wide, (c + 1) * wide)
        do = (a[0].astype(F32) + near[0].astype(F32) + far[0].astype(F32)).astype(BF16)
        do_out[0, :, cut] = do
        stat_out[pl.ds(h + 8, 1), cut] = jnp.sum(o[0].astype(F32) * do.astype(F32), axis=0, keepdims=True)

        @pl.when(h == 0)
        def _():
            stat_out[0:8, cut] = lse[...]


def join(parts):
    heads, _, wide = parts[0][3].shape
    total = wide * len(parts)
    in_specs, args = [], []
    block = pl.BlockSpec((1, HEAD_DIM, wide), lambda h: (h, 0, 0))
    for a, near, far, o, lse in parts:
        args += [
            a.reshape(heads, HEAD_DIM, wide),
            near.reshape(heads, HEAD_DIM, wide),
            far.reshape(heads, HEAD_DIM, wide),
            o,
            lse,
        ]
        in_specs += [
            block,
            block,
            block,
            block,
            pl.BlockSpec((8, wide), lambda h: (0, 0)),
        ]
    return pl.pallas_call(
        functools.partial(join_kernel, len(parts)),
        grid=(heads,),
        in_specs=in_specs,
        out_specs=[pl.BlockSpec((1, HEAD_DIM, total), lambda h: (h, 0, 0)), pl.BlockSpec((16, total), lambda h: (0, 0))],
        out_shape=[jax.ShapeDtypeStruct((heads, HEAD_DIM, total), BF16), jax.ShapeDtypeStruct((16, total), F32)],
        compiler_params=params(),
        cost_estimate=cost(5),
        name="join",
    )(*args)


def to_slot(s, value_ref, outs):
    for k in range(SLOTS):

        @pl.when(s == k)
        def _():
            outs[k][...] = value_ref[...]


def add_to(first, ref, at, m, part):
    ref[at, m] = jnp.where(first, part, ref[at, m] + part)


def forward_kernel(info, x_ref, *refs):
    att_refs, refs = refs[:SLOTS], refs[SLOTS:]
    g_refs = refs[:SLOTS]
    wot, vec_ref = refs[SLOTS : SLOTS + 2]
    far_weights = refs[SLOTS + 2 : SLOTS + 5]
    h_out, act_out, pg_out, g_out, n_out, root_out, sum_out, own_out = refs[-18:-10]
    layer_outs = refs[-10:-6]
    y1_s, layer_s, upt, wd, wdt, arrived = refs[-6:]
    s = pl.program_id(0)
    copies = [pltpu.make_async_copy(a, b, arrived.at[n]) for n, (a, b) in enumerate(zip(far_weights, (upt, wd, wdt)))]

    @pl.when(s == 0)
    def _():
        for copy in copies:
            copy.start()

    for k in range(SLOTS):

        @pl.when(s == k)
        def _():
            g_out[...] = g_refs[k][...]

    d = x_ref.shape[0]
    pieces = cuts(d, ROWS)
    att = jnp.concatenate([ref[...] for ref in att_refs], 0)
    total = 0.0
    for m in pieces:
        y1 = x_ref[m].astype(F32) + (dot(wot[m], att) + col(vec_ref, OUT_BIAS, m))
        y1_s[m] = y1
        total = total + jnp.sum(y1, axis=0, keepdims=True)
    mean = total * (1.0 / d)
    total = 0.0
    for m in pieces:
        center = y1_s[m] - mean
        total = total + jnp.sum(center * center, axis=0, keepdims=True)
    root = lax.rsqrt(total * (1.0 / d) + EPS)
    root_out[...] = jnp.broadcast_to(root, root_out.shape)
    for m in pieces:
        n = (y1_s[m] - mean) * root
        n_out[m] = n.astype(BF16)
        h_out[m] = (n * col(vec_ref, GAIN2, m) + col(vec_ref, SHIFT2, m)).astype(BF16)

    @pl.when(s == 0)
    def _():
        for copy in copies:
            copy.wait()

    h = h_out[...]
    g = g_out[...]
    for m in cuts(upt.shape[0], ROWS):
        pre = dot(upt[m], h) + col(vec_ref, UP_BIAS, m)
        act_grad = dot(wd[m], g)
        square = pre * pre
        t = jnp.tanh(pre * (GELU_C + (GELU_C * GELU_A) * square))
        half = 0.5 * (1.0 + t)
        act_out[m] = (pre * half).astype(BF16)
        slope = half + (0.5 * pre) * (1.0 - t * t) * (GELU_C + (3.0 * GELU_C * GELU_A) * square)
        pg = (act_grad * slope).astype(BF16)
        pg_out[m] = pg
        add_to(s == 0, sum_out, 0, m, fold(pg.astype(F32)))
    act = act_out[...]
    for m in pieces:
        layer_s[m] = dot(wdt[m], act).astype(BF16)
    to_slot(s, layer_s, layer_outs)

    @pl.when(s == 0)
    def _():
        own_out[...] = y1_s[...]


def forward(chunk, info, atts, x, gs, wot, upt, wd, wdt, vec, carry):
    d, total = x.shape
    f = upt.shape[0]
    wide = SLOTS * BLK
    dev = 3 * (total // BLK)
    keep = lambda a: pl.BlockSpec(a.shape, lambda s, i: (0,) * a.ndim, pipeline_mode=pl.Buffered(1))
    block = lambda r: pl.BlockSpec((r, BLK), lambda s, i: (0, s))
    mine = pl.BlockSpec((d, BLK), lambda s, i: (0, chunk))
    args = [info, x, *atts, *gs, wot, vec, upt, wd, wdt]
    in_specs = [pl.BlockSpec((d, BLK), lambda s, i: (0, chunk * SLOTS + s))]
    in_specs += [pl.BlockSpec((atts[0].shape[0], BLK), lambda s, i: (0, s ^ i[dev]))] * SLOTS
    in_specs += [pl.BlockSpec((d, BLK), lambda s, i: (0, 0))] * SLOTS + [keep(wot), keep(vec)]
    in_specs += [pl.BlockSpec(memory_space=pl.ANY)] * 3
    alias = {}
    if carry is not None:
        alias = {len(args) + n: 7 + n for n in range(len(carry))}
        in_specs += [pl.BlockSpec(memory_space=pl.ANY)] * len(carry)
        args += list(carry)
    spec = pltpu.PrefetchScalarGridSpec(
        num_scalar_prefetch=1,
        grid=(SLOTS,),
        in_specs=in_specs,
        out_specs=[
            block(d),
            block(f),
            block(f),
            block(d),
            block(d),
            block(8),
            pl.BlockSpec((1, f, 128), lambda s, i: (0, 0, 0)),
        ]
        + [mine] * 5,
        scratch_shapes=[pltpu.VMEM((d, BLK), F32), pltpu.VMEM((d, BLK), BF16)]
        + [pltpu.VMEM(a.shape, BF16) for a in (upt, wd, wdt)]
        + [pltpu.SemaphoreType.DMA((3,))],
    )
    shape = jax.ShapeDtypeStruct
    rows = total // SLOTS
    return pl.pallas_call(
        forward_kernel,
        grid_spec=spec,
        out_shape=[
            shape((d, wide), BF16),
            shape((f, wide), BF16),
            shape((f, wide), BF16),
            shape((d, wide), BF16),
            shape((d, wide), BF16),
            shape((8, wide), F32),
            shape((1, f, 128), F32),
            shape((d, rows), F32),
        ]
        + [shape((d, rows), BF16)] * SLOTS,
        input_output_aliases=alias,
        compiler_params=params(),
        cost_estimate=cost(26),
        name="forward",
    )(*args)


def backward_kernel(info, pg_ref, n_ref, root_ref, g_ref, up, *refs):
    vec_ref = refs[0]
    sum_out = refs[-16]
    attg_outs = refs[-15:-11]
    y1g_outs = refs[-11:-7]
    e_s, y1g_s = refs[-7:-5]
    wo, arrived = refs[-5:-1], refs[-1]
    s = pl.program_id(0)
    copies = [pltpu.make_async_copy(refs[1 + k], wo[k], arrived.at[k]) for k in range(SLOTS)]

    @pl.when(s == 0)
    def _():
        for copy in copies:
            copy.start()

    d = n_ref.shape[0]
    pieces = cuts(d, ROWS)
    pg = pg_ref[...]
    mean = 0.0
    tilt = 0.0
    for m in pieces:
        hg = dot(up[m], pg)
        n = n_ref[m].astype(F32)
        hn = hg * n
        gain = col(vec_ref, GAIN2, m)
        e = hg * gain
        e_s[m] = e
        mean = mean + jnp.sum(e, axis=0, keepdims=True)
        tilt = tilt + jnp.sum(hn * gain, axis=0, keepdims=True)
        add_to(s == 0, sum_out, 0, m, fold(hn))
        add_to(s == 0, sum_out, 1, m, fold(hg))
    mean = mean * (1.0 / d)
    tilt = tilt * (1.0 / d)
    root = root_ref[0:1]
    mine = jnp.where(s == 0, 1.0, 0.0)
    for m in pieces:
        y1g = root * (e_s[m] - mean - n_ref[m].astype(F32) * tilt) + g_ref[m].astype(F32) * mine
        y1g_s[m] = y1g.astype(BF16)
        add_to(s == 0, sum_out, 2, m, fold(y1g))

    @pl.when(s == 0)
    def _():
        for copy in copies:
            copy.wait()

    y1b = y1g_s[...]
    for k in range(SLOTS):
        attg_outs[k][...] = dot(wo[k][...], y1b).astype(BF16)
    to_slot(s, y1g_s, y1g_outs)


def backward(chunk, info, pg, n, root, g, up, wos, vec, carry):
    d, wide = n.shape
    f = up.shape[1]
    rows = wos[0].shape[0]
    dev = info.shape[0] - 1
    keep = lambda a: pl.BlockSpec(a.shape, lambda s, i: (0,) * a.ndim, pipeline_mode=pl.Buffered(1))
    block = lambda r: pl.BlockSpec((r, BLK), lambda s, i: (0, s))
    mine = pl.BlockSpec((d, BLK), lambda s, i: (0, chunk))
    ordered = pl.BlockSpec((rows, BLK), lambda s, i: (0, s ^ i[dev]))
    args = [info, pg, n, root, g, up, vec, *wos]
    in_specs = [block(f), block(d), block(8), mine, keep(up), keep(vec)] + [pl.BlockSpec(memory_space=pl.ANY)] * SLOTS
    alias = {}
    if carry is not None:
        alias = {len(args) + n: 5 + n for n in range(len(carry))}
        in_specs += [pl.BlockSpec(memory_space=pl.ANY)] * len(carry)
        args += list(carry)
    spec = pltpu.PrefetchScalarGridSpec(
        num_scalar_prefetch=1,
        grid=(SLOTS,),
        in_specs=in_specs,
        out_specs=[pl.BlockSpec((3, d, 128), lambda s, i: (0, 0, 0))] + [ordered] * SLOTS + [mine] * SLOTS,
        scratch_shapes=[pltpu.VMEM((d, BLK), F32), pltpu.VMEM((d, BLK), BF16)]
        + [pltpu.VMEM(a.shape, BF16) for a in wos]
        + [pltpu.SemaphoreType.DMA((SLOTS,))],
    )
    shape = jax.ShapeDtypeStruct
    return pl.pallas_call(
        backward_kernel,
        grid_spec=spec,
        out_shape=[shape((3, d, 128), F32)] + [shape((rows, wide), BF16)] * SLOTS + [shape(g.shape, BF16)] * SLOTS,
        input_output_aliases=alias,
        compiler_params=params(),
        cost_estimate=cost(17),
        name="backward",
    )(*args)


def shard_rows(m):
    return -(-m // (8 * 16)) * 16


COLUMNS = 256


def outer_kernel(count, order, info, *refs):
    dp = info[0]
    outs = refs[2 * count :]
    total = None
    for n in range(count):
        part = dot(refs[2 * n][...], refs[2 * n + 1][...], NT)
        total = part if total is None else total + part
    m = total.shape[0]
    size = shard_rows(m)
    for shard in range(8):
        low, high = min(shard * size, m), min((shard + 1) * size, m)
        if low == high:
            continue
        slot = shard ^ dp
        at = jnp.where((slot & order[2]) != 0, 1, 0) + jnp.where((slot & order[1]) != 0, 2, 0)
        value = total[low:high].astype(BF16)
        if high - low < size:
            value = jnp.concatenate([value, jnp.zeros((size - (high - low), value.shape[1]), BF16)], 0)
        goes = (slot & order[0]) != 0
        for k, out in enumerate(outs):

            @pl.when(goes if k else jnp.logical_not(goes))
            def _():
                out[pl.ds(pl.multiple_of(at * size, 16), size)] = value


def outer(pairs, info, order):
    m, depth = pairs[0][0].shape
    n = pairs[0][1].shape[0]
    size = shard_rows(m)
    in_specs, args = [], []
    for a, b in pairs:
        in_specs.append(pl.BlockSpec((m, depth), lambda i, s: (0, 0), pipeline_mode=pl.Buffered(1)))
        in_specs.append(pl.BlockSpec((COLUMNS, depth), lambda i, s: (i, 0)))
        args += [a, b]
    spec = pltpu.PrefetchScalarGridSpec(
        num_scalar_prefetch=1,
        grid=(-(-n // COLUMNS),),
        in_specs=in_specs,
        out_specs=[pl.BlockSpec((4 * size, COLUMNS), lambda i, s: (0, i))] * 2,
    )
    return pl.pallas_call(
        functools.partial(outer_kernel, len(pairs), order),
        grid_spec=spec,
        out_shape=[jax.ShapeDtypeStruct((4 * size, n), BF16)] * 2,
        compiler_params=params(),
        cost_estimate=cost(8),
        name="outer",
    )(info, *args)


def attn_grad_kernel(a_ref, b_ref, out_ref, sum_ref):
    a = a_ref[...]
    out_ref[...] = dot(a, b_ref[...], NT).astype(BF16)

    @pl.when(pl.program_id(0) == 0)
    def _():
        sum_ref[...] = fold(a.astype(F32))


def attn_grad_call(dqkv, h1):
    m, total = dqkv.shape
    d = h1.shape[0]
    return pl.pallas_call(
        attn_grad_kernel,
        grid=(-(-d // COLUMNS),),
        in_specs=[
            pl.BlockSpec((m, total), lambda i: (0, 0), pipeline_mode=pl.Buffered(1)),
            pl.BlockSpec((COLUMNS, total), lambda i: (i, 0)),
        ],
        out_specs=[pl.BlockSpec((m, COLUMNS), lambda i: (0, i)), pl.BlockSpec((m, 128), lambda i: (0, 0))],
        out_shape=[jax.ShapeDtypeStruct((m, d), BF16), jax.ShapeDtypeStruct((m, 128), F32)],
        compiler_params=params(),
        cost_estimate=cost(7),
        name="attn_grad_call",
    )(dqkv, h1)


def halve_kernel(keep_ref, recv_ref, keep_out, send_out):
    i = pl.program_id(0)
    total = (keep_ref[...].astype(F32) + recv_ref[...].astype(F32)).astype(BF16)

    @pl.when(i == 0)
    def _():
        keep_out[...] = total

    @pl.when(i == 1)
    def _():
        send_out[...] = total


def halve(keep, recv):
    size, n = keep.shape[0] // 2, keep.shape[1]
    block = pl.BlockSpec((size, n), lambda i: (i, 0))
    return pl.pallas_call(
        halve_kernel,
        grid=(2,),
        in_specs=[block, block],
        out_specs=[pl.BlockSpec((size, n), lambda i: (0, 0))] * 2,
        out_shape=[jax.ShapeDtypeStruct((size, n), BF16)] * 2,
        compiler_params=params(),
        cost_estimate=cost(2.5),
        name="halve",
    )(keep, recv)


def slot_of(i, order):
    return jnp.where(i & 1, order[2], 0) | jnp.where(i & 2, order[1], 0) | jnp.where(i & 4, order[0], 0)


def place_kernel(count, info, one, two, four, eight, *rest):
    i = pl.program_id(0)
    outs = rest[-count:]
    for ref, low, high in ((one, 0, 1), (two, 1, 2), (four, 2, 4), (eight, 4, 8)):

        @pl.when((i >= low) & (i < high))
        def _():
            size = ref.shape[0] // count
            for n, out in enumerate(outs):
                out[...] = ref[n * size : (n + 1) * size].astype(F32)


def place(parts, info, order, first, rows, carry, extra_rows):
    size, n = parts[0].shape
    count = 2 if extra_rows else 1
    half = size // count
    start = first // half
    near = lambda at, many: pl.BlockSpec((size, n), lambda i, s: (jnp.clip(i - at, 0, many - 1), 0))
    in_specs = [near(0, 1), near(1, 1), near(2, 2), near(4, 4)]
    args = list(parts)
    alias = {}
    if carry is not None:
        in_specs.append(pl.BlockSpec(memory_space=pl.ANY))
        args.append(carry)
        alias = {5: 0}
    out_specs = [pl.BlockSpec((half, n), lambda i, s: (start + (slot_of(i, order) ^ s[0]), 0))]
    out_shape = [jax.ShapeDtypeStruct((rows, n), F32)]
    if extra_rows:
        out_specs.append(pl.BlockSpec((half, n), lambda i, s: (slot_of(i, order) ^ s[0], 0)))
        out_shape.append(jax.ShapeDtypeStruct((8 * half, n), F32))
    spec = pltpu.PrefetchScalarGridSpec(num_scalar_prefetch=1, grid=(8,), in_specs=in_specs, out_specs=out_specs)
    out = pl.pallas_call(
        functools.partial(place_kernel, count),
        grid_spec=spec,
        out_shape=out_shape,
        input_output_aliases=alias,
        compiler_params=params(),
        cost_estimate=cost(6.5),
        name="place",
    )(info, *args)
    return (out[0], out[1][:extra_rows]) if extra_rows else out[0]


def swap_dp(v, k):
    return lax.ppermute(v, "dp", [(i, i ^ k) for i in range(8)])


class CellSum:
    def __init__(self, line, keep, send, info, order, rows, first=0, extra_rows=0):
        self.line, self.keep, self.info, self.order = line, keep, info, order
        self.rows, self.first, self.extra_rows = rows, first, extra_rows
        self.stage = 0
        self.known = lax.axis_size("dp") == 8
        if not self.known:
            both = lax.psum(jnp.stack([keep, send]), "dp")
            size = keep.shape[0] // 4
            self.parts = [both[0, :size], both[0, size : 2 * size], both[0, 2 * size :], both[1]]
            self.got = both[1]
            return
        self.got = swap_dp(send, order[0])

    def step(self):
        if not self.known:
            return
        self.stage += 1
        k1, k2, k3 = self.order
        if self.stage < 3:
            self.keep, send = self.line(halve, self.keep, self.got)
            self.got = swap_dp(send, k2 if self.stage == 1 else k3)
        elif self.stage == 3:
            self.parts = [self.line(lambda a, b: add(BF16, a, b), self.keep, self.got)]
            self.got = swap_dp(self.parts[0], k3)
        else:
            self.parts.append(self.got)
            self.got = swap_dp(self.line(stack, *self.parts), k2 if self.stage == 4 else k1)
            if self.stage == 5:
                self.parts.append(self.got)

    def finish(self, carry=None):
        return self.line(
            lambda p, *c: place(
                p, self.info, self.order, self.first, self.rows, c[0] if c else None, self.extra_rows
            ),
            self.parts,
            *([] if carry is None else [carry]),
        )


class Rounds:
    def __init__(self, line, v, over_tensor=False):
        self.line, self.v = line, v
        self.todo = [(swap_dp, 1), (swap_dp, 2), (swap_dp, 4)]
        if lax.axis_size("dp") != 8:
            self.v = lax.psum(v.astype(F32), "dp").astype(v.dtype)
            self.todo = []
        self.cells = self.v
        if over_tensor:
            self.todo += [(swap, 1), (swap, 2)]
        self.send()

    def send(self):
        self.got = None
        if self.todo:
            self.move, k = self.todo.pop(0)
            self.got = self.move(self.v, k)

    def step(self):
        if self.got is None:
            return
        self.v = self.line(lambda a, b: add(a.dtype, a, b), self.v, self.got)
        if self.move is swap_dp:
            self.cells = self.v
        self.send()


def out_grad_kernel(chunks, dev_at, info, *refs):
    atts, y1gs, outs = refs[: chunks * SLOTS], refs[chunks * SLOTS : -SLOTS], refs[-SLOTS:]
    dev = info[dev_at]
    totals = [None] * SLOTS
    for c in range(chunks):
        for s in range(SLOTS):
            at = pl.multiple_of((s ^ dev) * BLK, BLK)
            y1g = y1gs[s][:, c * BLK : (c + 1) * BLK]
            for n in range(SLOTS):
                part = dot(atts[c * SLOTS + n][:, pl.ds(at, BLK)], y1g, NT)
                totals[n] = part if totals[n] is None else totals[n] + part
    for n in range(SLOTS):
        outs[n][...] = totals[n].astype(BF16)


def out_grad_call(info, atts, y1gs):
    rows = atts[0][0].shape[0]
    d, wide = y1gs[0].shape
    heads = [a for chunk in atts for a in chunk]
    spec = pltpu.PrefetchScalarGridSpec(
        num_scalar_prefetch=1,
        grid=(-(-d // COLUMNS),),
        in_specs=[pl.BlockSpec(a.shape, lambda i, s: (0, 0), pipeline_mode=pl.Buffered(1)) for a in heads]
        + [pl.BlockSpec((COLUMNS, wide), lambda i, s: (i, 0))] * SLOTS,
        out_specs=[pl.BlockSpec((rows, COLUMNS), lambda i, s: (0, i))] * SLOTS,
    )
    return pl.pallas_call(
        functools.partial(out_grad_kernel, len(atts), 3 * wide * SLOTS // BLK),
        grid_spec=spec,
        out_shape=[jax.ShapeDtypeStruct((rows, d), BF16)] * SLOTS,
        compiler_params=params(),
        cost_estimate=cost(9),
        name="out_grad_call",
    )(info, *heads, *y1gs)


def h1_grad_kernel(w_ref, dqkv_ref, x_ref, sum_ref, *outs):
    s = pl.program_id(1)
    first = (s == 0) & (pl.program_id(0) == 0)
    hg_s = outs[-1]
    d = x_ref.shape[0]
    pieces = cuts(d, ROWS)
    total = 0.0
    for m in pieces:
        total = total + jnp.sum(x_ref[m].astype(F32), axis=0, keepdims=True)
    mean = total * (1.0 / d)
    total = 0.0
    for m in pieces:
        center = x_ref[m].astype(F32) - mean
        total = total + jnp.sum(center * center, axis=0, keepdims=True)
    root = lax.rsqrt(total * (1.0 / d) + EPS)
    dqkv = dqkv_ref[...]
    for m in pieces:
        hg = dot(w_ref[m], dqkv)
        n = (x_ref[m].astype(F32) - mean) * root
        hg_s[m] = hg.astype(BF16)
        add_to(first, sum_ref, 0, m, fold(hg * n))
        add_to(first, sum_ref, 1, m, fold(hg))
    to_slot(s, hg_s, outs[:SLOTS])


def h1_grad_call(w, dqkv, x):
    d, total = x.shape
    per = total // (BLK * SLOTS)
    m = w.shape[1]
    at = lambda p, s: (0, p * SLOTS + s)
    mine = pl.BlockSpec((d, BLK), lambda p, s: (0, p))
    return pl.pallas_call(
        h1_grad_kernel,
        grid=(per, SLOTS),
        in_specs=[
            pl.BlockSpec((d, m), lambda p, s: (0, 0), pipeline_mode=pl.Buffered(1)),
            pl.BlockSpec((m, BLK), at),
            pl.BlockSpec((d, BLK), at),
        ],
        out_specs=[pl.BlockSpec((2, d, 128), lambda p, s: (0, 0, 0))] + [mine] * SLOTS,
        out_shape=[jax.ShapeDtypeStruct((2, d, 128), F32)]
        + [jax.ShapeDtypeStruct((d, per * BLK), BF16)] * SLOTS,
        scratch_shapes=[pltpu.VMEM((d, BLK), BF16)],
        compiler_params=params(),
        cost_estimate=cost(13),
        name="h1_grad_call",
    )(w, dqkv, x)


def input_grad_kernel(x_ref, a_ref, b_ref, c_ref, d_ref, y1g_ref, gain_ref, out_ref):
    n, root = normal(x_ref[...].astype(F32))
    total = a_ref[...].astype(F32) + b_ref[...].astype(F32) + c_ref[...].astype(F32) + d_ref[...].astype(F32)
    e = total * gain_ref[:, GAIN1 : GAIN1 + 1]
    e = root * (e - jnp.mean(e, axis=0, keepdims=True) - n * jnp.mean(e * n, axis=0, keepdims=True))
    out_ref[...] = (y1g_ref[...] + e).astype(BF16)


def input_grad_call(x, a, b, c, d4, y1g, gain):
    d, rows = x.shape
    block = pl.BlockSpec((d, 128), lambda i: (0, i))
    return pl.pallas_call(
        input_grad_kernel,
        grid=(rows // 128,),
        in_specs=[block] * 6 + [pl.BlockSpec(gain.shape, lambda i: (0, 0))],
        out_specs=block,
        out_shape=jax.ShapeDtypeStruct((d, rows), BF16),
        compiler_params=params(),
        cost_estimate=cost(6),
        name="input_grad_call",
    )(x, a, b, c, d4, y1g, gain)


def layer_kernel(own_ref, a_ref, b_ref, c_ref, vec_ref, out_ref):
    total = a_ref[...].astype(F32) + b_ref[...].astype(F32) + c_ref[...].astype(F32)
    out_ref[...] = (own_ref[...] + total + vec_ref[:, DOWN_BIAS : DOWN_BIAS + 1]).astype(BF16)


def layer_call(own, a, b, c, vec):
    d, rows = own.shape
    block = pl.BlockSpec((d, 128), lambda i: (0, i))
    return pl.pallas_call(
        layer_kernel,
        grid=(rows // 128,),
        in_specs=[block] * 4 + [pl.BlockSpec(vec.shape, lambda i: (0, 0))],
        out_specs=block,
        out_shape=jax.ShapeDtypeStruct((d, rows), BF16),
        compiler_params=params(),
        cost_estimate=cost(3),
        name="layer_call",
    )(own, a, b, c, vec)


def small_kernel(chunks, width, sum1_ref, *refs):
    sums, ups, (qkv_ref, g_ref, out_ref) = refs[:chunks], refs[chunks : 2 * chunks], refs[2 * chunks :]
    across = lambda v: jnp.sum(v, axis=1, keepdims=True)
    columns = [across(sum1_ref[0]), across(sum1_ref[1])]
    columns += [across(sum(ref[n] for ref in sums)) for n in range(3)]
    columns += [across(g_ref[...].astype(F32)), across(sum(ref[0] for ref in ups))]
    d = g_ref.shape[0]
    qv = jnp.concatenate([qkv_ref[0:width], qkv_ref[2 * width : 3 * width]], 0)
    qv = jnp.concatenate([across(qv), jnp.zeros((d - 2 * width, 1), F32)], 0)
    out_ref[...] = jnp.concatenate([v.T for v in columns + [qv]], 0)


def small_sums(sum1, sums, up_sums, qkv_sum, g):
    return pl.pallas_call(
        functools.partial(small_kernel, len(sums), qkv_sum.shape[0] // 3),
        out_shape=jax.ShapeDtypeStruct((8, g.shape[0]), F32),
        compiler_params=params(),
        cost_estimate=cost(5),
        name="small_sums",
    )(sum1, *sums, *up_sums, qkv_sum, g)


def swap(v, k):
    return lax.ppermute(v, "tensor", [(i, i ^ k) for i in range(SLOTS)])


def after(v, *done):
    return lax.optimization_barrier((v, done))[0]


class Line:
    def __init__(self):
        self.last = []

    def __call__(self, step, *args):
        args, _ = lax.optimization_barrier((args, self.last))
        out = step(*args)
        self.last = jax.tree.leaves(out)
        return out

    def wait(self, *values):
        self.last = self.last + jax.tree.leaves(values)

    def pin(self, v, *also):
        return after(v, self.last, also)


class Gather:
    def __init__(self, v):
        self.own, self.side, self.across = v, swap(v, 1), swap(v, 2)

    def finish(self, line):
        self.corner = swap(line.pin(self.across), 1)
        return self

    def all(self):
        return self.own, self.side, self.across, self.corner


def plus(a, b):
    return a.astype(F32) + b.astype(F32)


def plus_low(a, b):
    return plus(a, b).astype(BF16)


def add_kernel(*refs):
    total = None
    for ref in refs[:-1]:
        v = (ref[0] if len(ref.shape) == 3 else ref[...]).astype(F32)
        total = v if total is None else total + v
    refs[-1][...] = total.astype(refs[-1].dtype)


def add(dtype, *terms):
    rows, columns = terms[0].shape
    size = rows // 2 if rows % 32 == 0 and rows * columns > 1 << 18 else rows
    in_specs, args = [], []
    for term in terms:
        if isinstance(term, tuple):
            in_specs.append(pl.BlockSpec((1, size, columns), functools.partial(lambda at, i: (at, i, 0), term[1])))
            args.append(term[0])
        else:
            in_specs.append(pl.BlockSpec((size, columns), lambda i: (i, 0)))
            args.append(term)
    return pl.pallas_call(
        add_kernel,
        grid=(rows // size,),
        in_specs=in_specs,
        out_specs=pl.BlockSpec((size, columns), lambda i: (i, 0)),
        out_shape=jax.ShapeDtypeStruct((rows, columns), dtype),
        compiler_params=params(),
        cost_estimate=cost(2.3),
        name="add",
    )(*args)


class GroupSum:
    def __init__(self, line, parts):
        self.line, self.parts = line, parts
        self.side = swap(line.pin(parts[3]), 1)

    def step(self, wait=True):
        self.far = swap(self.line(lambda a, b: add(BF16, a, b), self.parts[2], self.side), 2)
        self.near = swap(self.line.pin(self.parts[1]), 1)
        if wait:
            self.line.wait(self.near)

    def terms(self):
        return self.parts[0], self.near, self.far


def stack_kernel(*refs):
    at = 0
    for ref in refs[:-1]:
        refs[-1][at : at + ref.shape[0]] = ref[...]
        at += ref.shape[0]


def stack(*parts):
    return pl.pallas_call(
        stack_kernel,
        out_shape=jax.ShapeDtypeStruct((sum(p.shape[0] for p in parts), parts[0].shape[1]), parts[0].dtype),
        compiler_params=params(),
        cost_estimate=cost(2),
        name="stack",
    )(*parts)


def token_starts(lengths, offsets, total, dev):
    pos = jnp.arange(total, dtype=jnp.int32)[:, None]
    inside = (pos >= offsets[None]) & (pos < (offsets + lengths)[None])
    first = jnp.max(jnp.where(inside, offsets[None], -1), axis=1)
    start = jnp.where(first >= 0, first, pos[:, 0])
    nb = total // BLK
    per = nb // SLOTS
    b = jnp.arange(nb, dtype=jnp.int32)
    first_key = start.reshape(nb, BLK)[:, 0] // BLK
    place = (b % per) * SLOTS + ((b // per) ^ dev)
    last_query = jnp.max(jnp.where(first_key[None, :] <= b[:, None], b[None, :], 0), axis=1)
    info = jnp.concatenate([first_key, place, last_query, jnp.full((1,), dev)])
    return start[None], info.astype(jnp.int32)


def body(
    tokens,
    cotangent,
    ln1_gain,
    ln1_bias,
    attn_weight,
    qv_bias,
    out_weight,
    out_bias,
    ln2_gain,
    ln2_bias,
    up_weight,
    up_bias,
    down_weight,
    down_bias,
    cell_lengths,
    cell_offsets,
):
    rows, d = tokens.shape
    width = attn_weight.shape[2]
    heads = width // HEAD_DIM
    total = rows * SLOTS
    per = rows // BLK
    dev = lax.axis_index("tensor")
    start, info = token_starts(cell_lengths[0], cell_offsets[0], total, dev)

    whole_dp = lax.axis_size("dp") == 8
    dp_info = jnp.full((1,), lax.axis_index("dp") if whole_dp else 0, jnp.int32)

    line = Line()
    x_own = tokens.T
    g_own = cotangent.T
    x_go = Gather(x_own)

    w_in = attn_weight.transpose(1, 2, 0)
    zero = jnp.zeros_like(ln1_gain)
    rows8 = jnp.stack([ln1_gain, ln1_bias, out_bias, ln2_gain, ln2_bias, up_bias, down_bias, zero])
    bias8 = jnp.zeros((8, width), F32).at[0].set(qv_bias[0]).at[2].set(qv_bias[1])
    upt, wdt, w_back, vec, bias, *g_cuts = line(
        turn, g_own, up_weight, down_weight, w_in.reshape(3 * width, d), rows8, bias8
    )
    carry = line(lambda a, b: qkv_call(0, a, b, w_in, vec, bias, None), x_own, x_go.side)
    wo_go = Gather(line.pin(out_weight, x_go.across))
    g_go = [Gather(line.pin(g_cuts[0], x_go.across))]
    x_parts = x_go.finish(line).all()
    x_all, h1, qkv, kn, vn = line(lambda a, b, c: qkv_call(1, a, b, w_in, vec, bias, c), x_parts[2], x_parts[3], carry)
    chunks = range(per)
    fronts, att_go = [], []
    for c in chunks:
        fronts.append(line(functools.partial(attend, c), info, start, qkv, kn))
        if c == 0:
            line.wait(wo_go.across, g_go[0].across)
        att_go.append(Gather(line.pin(fronts[c][0]).reshape(width, SLOTS * BLK)))
        if c == 0:
            wo_parts = wo_go.finish(line).all()
    wot = line(turn_pieces, *wo_parts)
    g_parts = [g_go[0].finish(line).all()]
    atts, ahead = [], []
    for c in chunks:
        atts.append(att_go[c].finish(line).all())
        if c > 0:
            g_parts.append(g_go[c].finish(line).all())
        if c + 1 < per:
            g_go.append(Gather(line.pin(g_cuts[c + 1], atts[c][2])))
        ahead.append(
            line(
                functools.partial(forward, c),
                info,
                atts[c],
                x_all,
                g_parts[c],
                wot,
                upt,
                down_weight,
                wdt,
                vec,
                ahead[-1][7:] if c else None,
            )
        )
    h2s, acts, pgs, gs, ns, roots, up_sums = zip(*[m[:7] for m in ahead])
    own, *layer_parts = ahead[-1][7:]
    flat = lambda a, b: list(zip(a, b))
    down_order, up_order = (1, 2, 4), (2, 1, 4)
    f = down_weight.shape[0]
    layer_sum = GroupSum(line, layer_parts)
    down = CellSum(line, *line(lambda a, b: outer(flat(a, b), dp_info, down_order), acts, gs), dp_info, down_order, f)
    layer_sum.step(False)
    up = CellSum(line, *line(lambda a, b: outer(flat(a, b), dp_info, up_order), h2s, pgs), dp_info, up_order, d)

    back, attgs = [], []
    for c in chunks:
        carry = back[-1][1 + SLOTS :] if c else None
        back.append(
            line(functools.partial(backward, c), info, pgs[c], ns[c], roots[c], g_own, up_weight, wo_parts, vec, carry)
        )
        if c:
            line.wait(attgs[-1].far, down.got, up.got)
            up.step()
        else:
            line.wait(layer_sum.far, layer_sum.near, down.got)
        down.step()
        attgs.append(GroupSum(line, back[c][1 : 1 + SLOTS]))
        attgs[c].step()
    y1g_parts = back[-1][1 + SLOTS :]
    y1g = GroupSum(line, y1g_parts)
    out_parts = line(out_grad_call, info, atts, y1g_parts)
    line.wait(attgs[-1].far, down.got, up.got, y1g.side)
    out_terms = [out_parts[0]] + [swap(line.pin(out_parts[k]), k) for k in (1, 2, 3)]
    down.step()
    up.step()
    do, stat = line(join, [a.terms() + tuple(f) for a, f in zip(attgs, fronts)])
    dqkv = line(attend_back, info, start, qkv, kn, vn, do, stat).reshape(3 * width, total)
    line.wait(down.got, up.got, out_terms)
    down.step()
    up.step()
    attn_grad, qkv_sum = line(attn_grad_call, dqkv, h1)
    line.wait(down.got, up.got)
    out_grad = line(lambda *v: add(BF16, *v), *out_terms)
    late = lax.psum((attn_grad, out_grad), "dp")
    y1g.step(False)
    sum1, *h1_parts = line(h1_grad_call, w_back, dqkv, x_all)
    line.wait(y1g.near)
    up.step()
    down.step()
    small = line(small_sums, sum1, [b[0] for b in back], up_sums, qkv_sum, g_own)
    line.wait(up.got, y1g.far)
    h1g = [h1_parts[0]] + [swap(line.pin(h1_parts[k]), k) for k in (1, 2, 3)]
    up.step()
    layer = line(layer_call, own, *layer_sum.terms(), vec)
    y1_grad = line(lambda *v: add(F32, *v), *y1g.terms())
    line.wait(down.got)
    down_grad = down.finish()
    small = Rounds(line, line.pin(small), True)
    line.wait(h1g)
    input_grad = line(input_grad_call, x_own, *h1g, y1_grad, vec)
    small.step()
    small.step()
    line.wait(up.got)
    up_grad = up.finish()
    small.step()
    small.step()
    small.step()
    line.wait(late)
    attn_grad, out_grad = (v.astype(F32) for v in line(lambda a, b: (a, b), *late))
    small, own_small = small.v, small.cells[6:]
    return (
        layer.T,
        input_grad.T,
        small[0],
        small[1],
        attn_grad.reshape(3, width, d).transpose(2, 0, 1),
        own_small[1, : 2 * width].reshape(2, width),
        out_grad,
        small[4],
        small[2],
        small[3],
        up_grad,
        own_small[0],
        down_grad,
        small[5],
    )


def solution(mesh):
    rows = P(("dp", "tensor"), None)
    in_specs = (
        rows,
        rows,
        P(),
        P(),
        P(None, None, "tensor"),
        P(None, "tensor"),
        P("tensor", None),
        P(),
        P(),
        P(),
        P(None, "tensor"),
        P("tensor"),
        P("tensor", None),
        P(),
        P("dp", None),
        P("dp", None),
    )
    out_specs = (
        rows,
        rows,
        P(),
        P(),
        P(None, None, "tensor"),
        P(None, "tensor"),
        P("tensor", None),
        P(),
        P(),
        P(),
        P(None, "tensor"),
        P("tensor"),
        P("tensor", None),
        P(),
    )
    return jax.shard_map(body, mesh=mesh, in_specs=in_specs, out_specs=out_specs, check_vma=False)
```

```python
import functools
import math

import jax
import jax.numpy as jnp
from jax import lax
from jax.experimental import pallas as pl
from jax.experimental.pallas import tpu as pltpu
from jax.sharding import PartitionSpec as P


HEAD_DIM = 56
BLK = 256
SLOTS = 4
NEG = -1e30
EPS = 1e-05
SCALE = 1.0 / math.sqrt(HEAD_DIM)
SCALE2 = SCALE * math.log2(math.e)
GELU_C = math.sqrt(2.0 / math.pi)
GELU_A = 0.044715
F32 = jnp.float32
BF16 = jnp.bfloat16
NT = ((1,), (1,))
ROWS = 224
GAIN1, SHIFT1, OUT_BIAS, GAIN2, SHIFT2, UP_BIAS, DOWN_BIAS = range(7)
VEC8 = True
ATT_PIECES = True
VMEM = 60 << 20
PACE = 0.0


def dot(a, b, dims=((1,), (0,))):
    return lax.dot_general(a, b, (dims, ((), ())), preferred_element_type=F32)


def params():
    return pltpu.CompilerParams(vmem_limit_bytes=VMEM)


def cost(microseconds):
    return pl.CostEstimate(flops=max(1, int(microseconds * PACE)), bytes_accessed=1, transcendentals=0)


def fold(v):
    total = v[:, :128]
    for at in range(128, v.shape[1], 128):
        total = total + v[:, at : at + 128]
    return total


def normal(x):
    center = x - jnp.mean(x, axis=0, keepdims=True)
    root = lax.rsqrt(jnp.mean(center * center, axis=0, keepdims=True) + EPS)
    return center * root, root


def turn_kernel(count, parts, *refs):
    for n in range(count):
        refs[count + 1 + n][...] = refs[n][...].T
    for n in range(parts):
        refs[2 * count + 1 + n][...] = refs[count][:, n * BLK : (n + 1) * BLK]


def turn(cut, *arrays):
    wide = max(a.shape[1] for a in arrays)
    steps = -(-wide // 256)
    in_specs, out_specs, outs = [], [], []
    for a in arrays:
        rows, columns = a.shape
        if columns == wide:
            in_specs.append(pl.BlockSpec((rows, 256), lambda i: (0, i)))
            out_specs.append(pl.BlockSpec((256, rows), lambda i: (i, 0)))
        else:
            in_specs.append(pl.BlockSpec((rows, columns), lambda i: (0, 0)))
            out_specs.append(pl.BlockSpec((columns, rows), lambda i: (0, 0)))
        outs.append(jax.ShapeDtypeStruct((columns, rows), a.dtype))
    rows, columns = cut.shape
    parts = columns // BLK
    size = -(-rows // (16 * steps)) * 16
    in_specs.append(pl.BlockSpec((size, columns), lambda i: (i, 0)))
    out_specs += [pl.BlockSpec((size, BLK), lambda i: (i, 0))] * parts
    outs += [jax.ShapeDtypeStruct((rows, BLK), cut.dtype)] * parts
    return pl.pallas_call(
        functools.partial(turn_kernel, len(arrays), parts),
        grid=(steps,),
        in_specs=in_specs,
        out_specs=out_specs,
        out_shape=outs,
        compiler_params=params(),
        cost_estimate=cost(8),
        name="turn",
    )(*arrays, cut)


def turn_pieces_kernel(*refs):
    refs[-1][...] = jnp.concatenate([ref[...] for ref in refs[:-1]], 0).T


def turn_pieces(*pieces):
    rows, columns = pieces[0].shape
    return pl.pallas_call(
        turn_pieces_kernel,
        grid=(-(-columns // 256),),
        in_specs=[pl.BlockSpec((rows, 256), lambda i: (0, i))] * len(pieces),
        out_specs=pl.BlockSpec((256, rows * len(pieces)), lambda i: (i, 0)),
        out_shape=jax.ShapeDtypeStruct((columns, rows * len(pieces)), pieces[0].dtype),
        compiler_params=params(),
        cost_estimate=cost(5),
        name="turn_pieces",
    )(*pieces)


def col(ref, at, m):
    return ref[m, at : at + 1]


def cuts(total, size):
    return [slice(at, min(at + size, total)) for at in range(0, total, size)]


def qkv_kernel(heads, a_ref, b_ref, w_ref, vec_ref, bias_ref, *rest):
    x_out, h_out, q_out, kn_out, vn_out = rest[-5:]
    x_out[:, :BLK] = a_ref[...]
    x_out[:, BLK:] = b_ref[...]
    d = x_out.shape[0]
    pieces = cuts(d, ROWS)
    total = 0.0
    for m in pieces:
        total = total + jnp.sum(x_out[m].astype(F32), axis=0, keepdims=True)
    mean = total * (1.0 / d)
    total = 0.0
    for m in pieces:
        center = x_out[m].astype(F32) - mean
        total = total + jnp.sum(center * center, axis=0, keepdims=True)
    root = lax.rsqrt(total * (1.0 / d) + EPS)
    for m in pieces:
        n = (x_out[m].astype(F32) - mean) * root
        h_out[m] = (n * col(vec_ref, GAIN1, m) + col(vec_ref, SHIFT1, m)).astype(BF16)
    h = h_out[...]
    for part in range(3):
        r = (dot(w_ref[part], h) + bias_ref[:, part : part + 1]).astype(BF16)
        r = r.reshape(heads, HEAD_DIM, r.shape[1])
        q_out[part * heads : (part + 1) * heads] = r
        if part > 0:
            out = kn_out if part == 1 else vn_out
            for h_at in range(heads):
                out[h_at] = r[h_at].T


def qkv_call(pair, a, b, w, vec, bias, carry):
    d, rows = a.shape
    per = rows // BLK
    total = rows * SLOTS
    heads = w.shape[1] // HEAD_DIM
    wide = 2 * BLK
    outs = [
        jax.ShapeDtypeStruct((d, total), BF16),
        jax.ShapeDtypeStruct((d, total), BF16),
        jax.ShapeDtypeStruct((3 * heads, HEAD_DIM, total), BF16),
        jax.ShapeDtypeStruct((heads, total, HEAD_DIM), BF16),
        jax.ShapeDtypeStruct((heads, total, HEAD_DIM), BF16),
    ]
    at = lambda p: p * (SLOTS // 2) + pair
    in_specs = [
        pl.BlockSpec((d, BLK), lambda p: (0, p)),
        pl.BlockSpec((d, BLK), lambda p: (0, p)),
        pl.BlockSpec(w.shape, lambda p: (0, 0, 0)),
        pl.BlockSpec(vec.shape, lambda p: (0, 0)),
        pl.BlockSpec(bias.shape, lambda p: (0, 0)),
    ]
    args = [a, b, w, vec, bias]
    alias = {}
    if carry is not None:
        alias = {len(args) + n: n for n in range(len(outs))}
        in_specs += [pl.BlockSpec(memory_space=pl.ANY)] * len(outs)
        args += list(carry)
    return pl.pallas_call(
        functools.partial(qkv_kernel, heads),
        grid=(per,),
        in_specs=in_specs,
        out_specs=[
            pl.BlockSpec((d, wide), lambda p: (0, at(p))),
            pl.BlockSpec((d, wide), lambda p: (0, at(p))),
            pl.BlockSpec((3 * heads, HEAD_DIM, wide), lambda p: (0, 0, at(p))),
            pl.BlockSpec((heads, wide, HEAD_DIM), lambda p: (0, at(p), 0)),
            pl.BlockSpec((heads, wide, HEAD_DIM), lambda p: (0, at(p), 0)),
        ],
        out_shape=outs,
        input_output_aliases=alias,
        compiler_params=params(),
        cost_estimate=cost(8),
        name="qkv_call",
    )(*args)


def attend_kernel(heads, nb, per, chunk, info, start_ref, q_ref, kn_ref, v_ref, o_ref, lse_ref, acc, m_s, l_s):
    b = pl.program_id(0) * per + chunk

    def visit(kb, diag):
        at = pl.multiple_of(info[nb + kb] * BLK, BLK)
        kpos = lax.broadcasted_iota(jnp.int32, (BLK, BLK), 0)
        ok = kpos >= (start_ref[...] - kb * BLK)
        if diag:
            ok = ok & (kpos <= lax.broadcasted_iota(jnp.int32, (BLK, BLK), 1))
        scores = [dot(kn_ref[h, pl.ds(at, BLK), :], q_ref[h]) for h in range(heads)]
        scores = [jnp.where(ok, s, NEG) for s in scores]
        top = jnp.concatenate([jnp.max(s, axis=0, keepdims=True) for s in scores], 0)
        if not diag:
            old = m_s[0:heads, :]
            top = jnp.maximum(old, top)
            fade = jnp.exp2((old - top) * SCALE2)
        m_s[0:heads, :] = top
        expo = [jnp.exp2((scores[h] - top[h : h + 1]) * SCALE2) for h in range(heads)]
        sums = jnp.concatenate([jnp.sum(e, axis=0, keepdims=True) for e in expo], 0)
        l_s[0:heads, :] = sums if diag else l_s[0:heads, :] * fade + sums
        for h in range(heads):
            new = dot(v_ref[h, :, pl.ds(at, BLK)], expo[h].astype(BF16))
            acc[h] = new if diag else acc[h] * fade[h : h + 1] + new

    visit(b, True)

    def step(kb, _):
        visit(kb, False)
        return 0

    lax.fori_loop(info[b], b, step, 0)
    for h in range(heads):
        total = l_s[h : h + 1, :]
        o_ref[h] = (acc[h] * (1.0 / total)).astype(BF16)
        lse_ref[h : h + 1, :] = m_s[h : h + 1, :] * SCALE2 + jnp.log2(total)


def attend(chunk, info, start, qkv, kn):
    heads, total = qkv.shape[0] // 3, qkv.shape[2]
    nb = total // BLK
    per = nb // SLOTS
    spec = pltpu.PrefetchScalarGridSpec(
        num_scalar_prefetch=1,
        grid=(SLOTS,),
        in_specs=[
            pl.BlockSpec((1, BLK), lambda i, s: (0, i * per + chunk)),
            pl.BlockSpec((heads, HEAD_DIM, BLK), lambda i, s: (0, 0, s[nb + i * per + chunk])),
            pl.BlockSpec((heads, total, HEAD_DIM), lambda i, s: (0, 0, 0)),
            pl.BlockSpec((heads, HEAD_DIM, total), lambda i, s: (2, 0, 0)),
        ],
        out_specs=[
            pl.BlockSpec((heads, HEAD_DIM, BLK), lambda i, s: (0, 0, i)),
            pl.BlockSpec((8, BLK), lambda i, s: (0, i)),
        ],
        scratch_shapes=[
            pltpu.VMEM((heads, HEAD_DIM, BLK), F32),
            pltpu.VMEM((8, BLK), F32),
            pltpu.VMEM((8, BLK), F32),
        ],
    )
    return pl.pallas_call(
        functools.partial(attend_kernel, heads, nb, per, chunk),
        grid_spec=spec,
        out_shape=[
            jax.ShapeDtypeStruct((heads, HEAD_DIM, SLOTS * BLK), BF16),
            jax.ShapeDtypeStruct((8, SLOTS * BLK), F32),
        ],
        compiler_params=params(),
        cost_estimate=cost(9.5),
        name="attend",
    )(info, start, qkv, kn, qkv)


def attend_back_kernel(heads, nb, per, info, start_ref, q_ref, k_ref, kn_ref, vn_ref, do_ref, stat_ref, out_ref, dq_s, dk_s, dv_s):
    j = pl.program_id(0)

    def place(b):
        return pl.multiple_of(info[nb + b] * BLK, BLK)

    def ordered(b):
        return pl.multiple_of(((b % per) * SLOTS + b // per) * BLK, BLK)

    @pl.when(j == 0)
    def _():
        dq_s[...] = jnp.zeros_like(dq_s)

    def visit(b, diag):
        at = place(b)
        mine = ordered(b)
        kpos = lax.broadcasted_iota(jnp.int32, (BLK, BLK), 0)
        ok = kpos >= (start_ref[:, pl.ds(pl.multiple_of(b * BLK, BLK), BLK)] - j * BLK)
        if diag:
            ok = ok & (kpos <= lax.broadcasted_iota(jnp.int32, (BLK, BLK), 1))
        every = range(heads)
        query = [q_ref[h, :, pl.ds(at, BLK)] for h in every]
        grad = [do_ref[h, :, pl.ds(mine, BLK)] for h in every]
        scores = [dot(kn_ref[h], query[h]) for h in every]
        prob_grad = [dot(vn_ref[h], grad[h]) for h in every]
        probs = [
            jnp.where(ok, jnp.exp2(scores[h] * SCALE2 - stat_ref[h : h + 1, pl.ds(mine, BLK)]), 0.0) for h in every
        ]
        score_grad = [
            (probs[h] * (prob_grad[h] - stat_ref[8 + h : 9 + h, pl.ds(mine, BLK)])).astype(BF16) for h in every
        ]
        dv = [dot(grad[h], probs[h].astype(BF16), NT) for h in every]
        dk = [dot(query[h], score_grad[h], NT) for h in every]
        dq = [dot(k_ref[h], score_grad[h]) for h in every]
        for h in every:
            if diag:
                dv_s[h] = dv[h]
                dk_s[h] = dk[h]
            else:
                dv_s[h] += dv[h]
                dk_s[h] += dk[h]
            dq_s[h, :, pl.ds(at, BLK)] += dq[h]

    visit(j, True)

    def step(b, _):
        visit(b, False)
        return 0

    lax.fori_loop(j + 1, info[2 * nb + j] + 1, step, 0)
    at = place(j)
    for h in range(heads):
        out_ref[h] = (dq_s[h, :, pl.ds(at, BLK)] * SCALE).astype(BF16)
        out_ref[heads + h] = (dk_s[h] * SCALE).astype(BF16)
        out_ref[2 * heads + h] = dv_s[h].astype(BF16)


def attend_back(info, start, qkv, kn, vn, do, stat):
    heads, total = qkv.shape[0] // 3, qkv.shape[2]
    nb = total // BLK
    per = nb // SLOTS
    whole = pl.BlockSpec((heads, HEAD_DIM, total), lambda j, s: (0, 0, 0))
    block = lambda a: pl.BlockSpec((heads, HEAD_DIM, BLK), lambda j, s: (a, 0, s[nb + j]))
    tall = pl.BlockSpec((heads, BLK, HEAD_DIM), lambda j, s: (0, s[nb + j], 0))
    spec = pltpu.PrefetchScalarGridSpec(
        num_scalar_prefetch=1,
        grid=(nb,),
        in_specs=[
            pl.BlockSpec((1, total), lambda j, s: (0, 0)),
            whole,
            block(1),
            tall,
            tall,
            whole,
            pl.BlockSpec((16, total), lambda j, s: (0, 0)),
        ],
        out_specs=pl.BlockSpec((3 * heads, HEAD_DIM, BLK), lambda j, s: (0, 0, s[nb + j])),
        scratch_shapes=[
            pltpu.VMEM((heads, HEAD_DIM, total), F32),
            pltpu.VMEM((heads, HEAD_DIM, BLK), F32),
            pltpu.VMEM((heads, HEAD_DIM, BLK), F32),
        ],
    )
    return pl.pallas_call(
        functools.partial(attend_back_kernel, heads, nb, per),
        grid_spec=spec,
        out_shape=jax.ShapeDtypeStruct((3 * heads, HEAD_DIM, total), BF16),
        compiler_params=params(),
        cost_estimate=cost(20),
        name="attend_back",
    )(info, start, qkv, qkv, kn, vn, do, stat)


def join_kernel(chunks, *refs):
    do_out, stat_out = refs[-2:]
    h = pl.program_id(0)
    wide = SLOTS * BLK
    for c in range(chunks):
        a, near, far, o, lse = refs[5 * c : 5 * c + 5]
        cut = slice(c * wide, (c + 1) * wide)
        do = (a[0].astype(F32) + near[0].astype(F32) + far[0].astype(F32)).astype(BF16)
        do_out[0, :, cut] = do
        stat_out[pl.ds(h + 8, 1), cut] = jnp.sum(o[0].astype(F32) * do.astype(F32), axis=0, keepdims=True)

        @pl.when(h == 0)
        def _():
            stat_out[0:8, cut] = lse[...]


def join(parts):
    heads, _, wide = parts[0][3].shape
    total = wide * len(parts)
    in_specs, args = [], []
    block = pl.BlockSpec((1, HEAD_DIM, wide), lambda h: (h, 0, 0))
    for a, near, far, o, lse in parts:
        args += [
            a.reshape(heads, HEAD_DIM, wide),
            near.reshape(heads, HEAD_DIM, wide),
            far.reshape(heads, HEAD_DIM, wide),
            o,
            lse,
        ]
        in_specs += [
            block,
            block,
            block,
            block,
            pl.BlockSpec((8, wide), lambda h: (0, 0)),
        ]
    return pl.pallas_call(
        functools.partial(join_kernel, len(parts)),
        grid=(heads,),
        in_specs=in_specs,
        out_specs=[pl.BlockSpec((1, HEAD_DIM, total), lambda h: (h, 0, 0)), pl.BlockSpec((16, total), lambda h: (0, 0))],
        out_shape=[jax.ShapeDtypeStruct((heads, HEAD_DIM, total), BF16), jax.ShapeDtypeStruct((16, total), F32)],
        compiler_params=params(),
        cost_estimate=cost(5),
        name="join",
    )(*args)


def to_slot(s, value_ref, outs):
    for k in range(SLOTS):

        @pl.when(s == k)
        def _():
            outs[k][...] = value_ref[...]


def add_to(first, ref, at, m, part):
    ref[at, m] = jnp.where(first, part, ref[at, m] + part)


def forward_kernel(info, x_ref, *refs):
    att_refs, refs = refs[:SLOTS], refs[SLOTS:]
    g_refs = refs[:SLOTS]
    wot, vec_ref = refs[SLOTS : SLOTS + 2]
    far_weights = refs[SLOTS + 2 : SLOTS + 5]
    h_out, act_out, pg_out, g_out, n_out, root_out, sum_out, own_out = refs[-18:-10]
    layer_outs = refs[-10:-6]
    y1_s, layer_s, upt, wd, wdt, arrived = refs[-6:]
    s = pl.program_id(0)
    copies = [pltpu.make_async_copy(a, b, arrived.at[n]) for n, (a, b) in enumerate(zip(far_weights, (upt, wd, wdt)))]

    @pl.when(s == 0)
    def _():
        for copy in copies:
            copy.start()

    for k in range(SLOTS):

        @pl.when(s == k)
        def _():
            g_out[...] = g_refs[k][...]

    d = x_ref.shape[0]
    pieces = cuts(d, ROWS)
    att = jnp.concatenate([ref[...] for ref in att_refs], 0)
    total = 0.0
    for m in pieces:
        y1 = x_ref[m].astype(F32) + (dot(wot[m], att) + col(vec_ref, OUT_BIAS, m))
        y1_s[m] = y1
        total = total + jnp.sum(y1, axis=0, keepdims=True)
    mean = total * (1.0 / d)
    total = 0.0
    for m in pieces:
        center = y1_s[m] - mean
        total = total + jnp.sum(center * center, axis=0, keepdims=True)
    root = lax.rsqrt(total * (1.0 / d) + EPS)
    root_out[...] = jnp.broadcast_to(root, root_out.shape)
    for m in pieces:
        n = (y1_s[m] - mean) * root
        n_out[m] = n.astype(BF16)
        h_out[m] = (n * col(vec_ref, GAIN2, m) + col(vec_ref, SHIFT2, m)).astype(BF16)

    @pl.when(s == 0)
    def _():
        for copy in copies:
            copy.wait()

    h = h_out[...]
    g = g_out[...]
    for m in cuts(upt.shape[0], ROWS):
        pre = dot(upt[m], h) + col(vec_ref, UP_BIAS, m)
        act_grad = dot(wd[m], g)
        square = pre * pre
        t = jnp.tanh(pre * (GELU_C + (GELU_C * GELU_A) * square))
        half = 0.5 * (1.0 + t)
        act_out[m] = (pre * half).astype(BF16)
        slope = half + (0.5 * pre) * (1.0 - t * t) * (GELU_C + (3.0 * GELU_C * GELU_A) * square)
        pg = (act_grad * slope).astype(BF16)
        pg_out[m] = pg
        add_to(s == 0, sum_out, 0, m, fold(pg.astype(F32)))
    act = act_out[...]
    for m in pieces:
        layer_s[m] = dot(wdt[m], act).astype(BF16)
    to_slot(s, layer_s, layer_outs)

    @pl.when(s == 0)
    def _():
        own_out[...] = y1_s[...]


def forward(chunk, info, atts, x, gs, wot, upt, wd, wdt, vec, carry):
    d, total = x.shape
    f = upt.shape[0]
    wide = SLOTS * BLK
    dev = 3 * (total // BLK)
    keep = lambda a: pl.BlockSpec(a.shape, lambda s, i: (0,) * a.ndim, pipeline_mode=pl.Buffered(1))
    block = lambda r: pl.BlockSpec((r, BLK), lambda s, i: (0, s))
    mine = pl.BlockSpec((d, BLK), lambda s, i: (0, chunk))
    args = [info, x, *atts, *gs, wot, vec, upt, wd, wdt]
    in_specs = [pl.BlockSpec((d, BLK), lambda s, i: (0, chunk * SLOTS + s))]
    in_specs += [pl.BlockSpec((atts[0].shape[0], BLK), lambda s, i: (0, s ^ i[dev]))] * SLOTS
    in_specs += [pl.BlockSpec((d, BLK), lambda s, i: (0, 0))] * SLOTS + [keep(wot), keep(vec)]
    in_specs += [pl.BlockSpec(memory_space=pl.ANY)] * 3
    alias = {}
    if carry is not None:
        alias = {len(args) + n: 7 + n for n in range(len(carry))}
        in_specs += [pl.BlockSpec(memory_space=pl.ANY)] * len(carry)
        args += list(carry)
    spec = pltpu.PrefetchScalarGridSpec(
        num_scalar_prefetch=1,
        grid=(SLOTS,),
        in_specs=in_specs,
        out_specs=[
            block(d),
            block(f),
            block(f),
            block(d),
            block(d),
            block(8),
            pl.BlockSpec((1, f, 128), lambda s, i: (0, 0, 0)),
        ]
        + [mine] * 5,
        scratch_shapes=[pltpu.VMEM((d, BLK), F32), pltpu.VMEM((d, BLK), BF16)]
        + [pltpu.VMEM(a.shape, BF16) for a in (upt, wd, wdt)]
        + [pltpu.SemaphoreType.DMA((3,))],
    )
    shape = jax.ShapeDtypeStruct
    rows = total // SLOTS
    return pl.pallas_call(
        forward_kernel,
        grid_spec=spec,
        out_shape=[
            shape((d, wide), BF16),
            shape((f, wide), BF16),
            shape((f, wide), BF16),
            shape((d, wide), BF16),
            shape((d, wide), BF16),
            shape((8, wide), F32),
            shape((1, f, 128), F32),
            shape((d, rows), F32),
        ]
        + [shape((d, rows), BF16)] * SLOTS,
        input_output_aliases=alias,
        compiler_params=params(),
        cost_estimate=cost(26),
        name="forward",
    )(*args)


def backward_kernel(info, pg_ref, n_ref, root_ref, g_ref, up, *refs):
    vec_ref = refs[0]
    sum_out = refs[-16]
    attg_outs = refs[-15:-11]
    y1g_outs = refs[-11:-7]
    e_s, y1g_s = refs[-7:-5]
    wo, arrived = refs[-5:-1], refs[-1]
    s = pl.program_id(0)
    copies = [pltpu.make_async_copy(refs[1 + k], wo[k], arrived.at[k]) for k in range(SLOTS)]

    @pl.when(s == 0)
    def _():
        for copy in copies:
            copy.start()

    d = n_ref.shape[0]
    pieces = cuts(d, ROWS)
    pg = pg_ref[...]
    mean = 0.0
    tilt = 0.0
    for m in pieces:
        hg = dot(up[m], pg)
        n = n_ref[m].astype(F32)
        hn = hg * n
        gain = col(vec_ref, GAIN2, m)
        e = hg * gain
        e_s[m] = e
        mean = mean + jnp.sum(e, axis=0, keepdims=True)
        tilt = tilt + jnp.sum(hn * gain, axis=0, keepdims=True)
        add_to(s == 0, sum_out, 0, m, fold(hn))
        add_to(s == 0, sum_out, 1, m, fold(hg))
    mean = mean * (1.0 / d)
    tilt = tilt * (1.0 / d)
    root = root_ref[0:1]
    mine = jnp.where(s == 0, 1.0, 0.0)
    for m in pieces:
        y1g = root * (e_s[m] - mean - n_ref[m].astype(F32) * tilt) + g_ref[m].astype(F32) * mine
        y1g_s[m] = y1g.astype(BF16)
        add_to(s == 0, sum_out, 2, m, fold(y1g))

    @pl.when(s == 0)
    def _():
        for copy in copies:
            copy.wait()

    y1b = y1g_s[...]
    for k in range(SLOTS):
        attg_outs[k][...] = dot(wo[k][...], y1b).astype(BF16)
    to_slot(s, y1g_s, y1g_outs)


def backward(chunk, info, pg, n, root, g, up, wos, vec, carry):
    d, wide = n.shape
    f = up.shape[1]
    rows = wos[0].shape[0]
    dev = info.shape[0] - 1
    keep = lambda a: pl.BlockSpec(a.shape, lambda s, i: (0,) * a.ndim, pipeline_mode=pl.Buffered(1))
    block = lambda r: pl.BlockSpec((r, BLK), lambda s, i: (0, s))
    mine = pl.BlockSpec((d, BLK), lambda s, i: (0, chunk))
    ordered = pl.BlockSpec((rows, BLK), lambda s, i: (0, s ^ i[dev]))
    args = [info, pg, n, root, g, up, vec, *wos]
    in_specs = [block(f), block(d), block(8), mine, keep(up), keep(vec)] + [pl.BlockSpec(memory_space=pl.ANY)] * SLOTS
    alias = {}
    if carry is not None:
        alias = {len(args) + n: 5 + n for n in range(len(carry))}
        in_specs += [pl.BlockSpec(memory_space=pl.ANY)] * len(carry)
        args += list(carry)
    spec = pltpu.PrefetchScalarGridSpec(
        num_scalar_prefetch=1,
        grid=(SLOTS,),
        in_specs=in_specs,
        out_specs=[pl.BlockSpec((3, d, 128), lambda s, i: (0, 0, 0))] + [ordered] * SLOTS + [mine] * SLOTS,
        scratch_shapes=[pltpu.VMEM((d, BLK), F32), pltpu.VMEM((d, BLK), BF16)]
        + [pltpu.VMEM(a.shape, BF16) for a in wos]
        + [pltpu.SemaphoreType.DMA((SLOTS,))],
    )
    shape = jax.ShapeDtypeStruct
    return pl.pallas_call(
        backward_kernel,
        grid_spec=spec,
        out_shape=[shape((3, d, 128), F32)] + [shape((rows, wide), BF16)] * SLOTS + [shape(g.shape, BF16)] * SLOTS,
        input_output_aliases=alias,
        compiler_params=params(),
        cost_estimate=cost(17),
        name="backward",
    )(*args)


def shard_rows(m):
    return -(-m // (8 * 16)) * 16


COLUMNS = 256


def outer_kernel(count, order, info, *refs):
    dp = info[0]
    outs = refs[2 * count :]
    total = None
    for n in range(count):
        part = dot(refs[2 * n][...], refs[2 * n + 1][...], NT)
        total = part if total is None else total + part
    m = total.shape[0]
    size = shard_rows(m)
    for shard in range(8):
        low, high = min(shard * size, m), min((shard + 1) * size, m)
        if low == high:
            continue
        slot = shard ^ dp
        at = jnp.where((slot & order[2]) != 0, 1, 0) + jnp.where((slot & order[1]) != 0, 2, 0)
        value = total[low:high].astype(BF16)
        if high - low < size:
            value = jnp.concatenate([value, jnp.zeros((size - (high - low), value.shape[1]), BF16)], 0)
        goes = (slot & order[0]) != 0
        for k, out in enumerate(outs):

            @pl.when(goes if k else jnp.logical_not(goes))
            def _():
                out[pl.ds(pl.multiple_of(at * size, 16), size)] = value


def outer(pairs, info, order):
    m, depth = pairs[0][0].shape
    n = pairs[0][1].shape[0]
    size = shard_rows(m)
    in_specs, args = [], []
    for a, b in pairs:
        in_specs.append(pl.BlockSpec((m, depth), lambda i, s: (0, 0), pipeline_mode=pl.Buffered(1)))
        in_specs.append(pl.BlockSpec((COLUMNS, depth), lambda i, s: (i, 0)))
        args += [a, b]
    spec = pltpu.PrefetchScalarGridSpec(
        num_scalar_prefetch=1,
        grid=(-(-n // COLUMNS),),
        in_specs=in_specs,
        out_specs=[pl.BlockSpec((4 * size, COLUMNS), lambda i, s: (0, i))] * 2,
    )
    return pl.pallas_call(
        functools.partial(outer_kernel, len(pairs), order),
        grid_spec=spec,
        out_shape=[jax.ShapeDtypeStruct((4 * size, n), BF16)] * 2,
        compiler_params=params(),
        cost_estimate=cost(8),
        name="outer",
    )(info, *args)


def attn_grad_kernel(a_ref, b_ref, out_ref, sum_ref):
    a = a_ref[...]
    out_ref[...] = dot(a, b_ref[...], NT).astype(BF16)

    @pl.when(pl.program_id(0) == 0)
    def _():
        sum_ref[...] = fold(a.astype(F32))


def attn_grad_call(dqkv, h1):
    m, total = dqkv.shape
    d = h1.shape[0]
    return pl.pallas_call(
        attn_grad_kernel,
        grid=(-(-d // COLUMNS),),
        in_specs=[
            pl.BlockSpec((m, total), lambda i: (0, 0), pipeline_mode=pl.Buffered(1)),
            pl.BlockSpec((COLUMNS, total), lambda i: (i, 0)),
        ],
        out_specs=[pl.BlockSpec((m, COLUMNS), lambda i: (0, i)), pl.BlockSpec((m, 128), lambda i: (0, 0))],
        out_shape=[jax.ShapeDtypeStruct((m, d), BF16), jax.ShapeDtypeStruct((m, 128), F32)],
        compiler_params=params(),
        cost_estimate=cost(7),
        name="attn_grad_call",
    )(dqkv, h1)


def halve_kernel(keep_ref, recv_ref, keep_out, send_out):
    i = pl.program_id(0)
    total = (keep_ref[...].astype(F32) + recv_ref[...].astype(F32)).astype(BF16)

    @pl.when(i == 0)
    def _():
        keep_out[...] = total

    @pl.when(i == 1)
    def _():
        send_out[...] = total


def halve(keep, recv):
    size, n = keep.shape[0] // 2, keep.shape[1]
    block = pl.BlockSpec((size, n), lambda i: (i, 0))
    return pl.pallas_call(
        halve_kernel,
        grid=(2,),
        in_specs=[block, block],
        out_specs=[pl.BlockSpec((size, n), lambda i: (0, 0))] * 2,
        out_shape=[jax.ShapeDtypeStruct((size, n), BF16)] * 2,
        compiler_params=params(),
        cost_estimate=cost(2.5),
        name="halve",
    )(keep, recv)


def slot_of(i, order):
    return jnp.where(i & 1, order[2], 0) | jnp.where(i & 2, order[1], 0) | jnp.where(i & 4, order[0], 0)


def place_kernel(count, info, one, two, four, eight, *rest):
    i = pl.program_id(0)
    outs = rest[-count:]
    for ref, low, high in ((one, 0, 1), (two, 1, 2), (four, 2, 4), (eight, 4, 8)):

        @pl.when((i >= low) & (i < high))
        def _():
            size = ref.shape[0] // count
            for n, out in enumerate(outs):
                out[...] = ref[n * size : (n + 1) * size].astype(F32)


def place(parts, info, order, first, rows, carry, extra_rows):
    size, n = parts[0].shape
    count = 2 if extra_rows else 1
    half = size // count
    start = first // half
    near = lambda at, many: pl.BlockSpec((size, n), lambda i, s: (jnp.clip(i - at, 0, many - 1), 0))
    in_specs = [near(0, 1), near(1, 1), near(2, 2), near(4, 4)]
    args = list(parts)
    alias = {}
    if carry is not None:
        in_specs.append(pl.BlockSpec(memory_space=pl.ANY))
        args.append(carry)
        alias = {5: 0}
    out_specs = [pl.BlockSpec((half, n), lambda i, s: (start + (slot_of(i, order) ^ s[0]), 0))]
    out_shape = [jax.ShapeDtypeStruct((rows, n), F32)]
    if extra_rows:
        out_specs.append(pl.BlockSpec((half, n), lambda i, s: (slot_of(i, order) ^ s[0], 0)))
        out_shape.append(jax.ShapeDtypeStruct((8 * half, n), F32))
    spec = pltpu.PrefetchScalarGridSpec(num_scalar_prefetch=1, grid=(8,), in_specs=in_specs, out_specs=out_specs)
    out = pl.pallas_call(
        functools.partial(place_kernel, count),
        grid_spec=spec,
        out_shape=out_shape,
        input_output_aliases=alias,
        compiler_params=params(),
        cost_estimate=cost(6.5),
        name="place",
    )(info, *args)
    return (out[0], out[1][:extra_rows]) if extra_rows else out[0]


def swap_dp(v, k):
    return lax.ppermute(v, "dp", [(i, i ^ k) for i in range(8)])


class CellSum:
    def __init__(self, line, keep, send, info, order, rows, first=0, extra_rows=0):
        self.line, self.keep, self.info, self.order = line, keep, info, order
        self.rows, self.first, self.extra_rows = rows, first, extra_rows
        self.stage = 0
        self.known = lax.axis_size("dp") == 8
        if not self.known:
            both = lax.psum(jnp.stack([keep, send]), "dp")
            size = keep.shape[0] // 4
            self.parts = [both[0, :size], both[0, size : 2 * size], both[0, 2 * size :], both[1]]
            self.got = both[1]
            return
        self.got = swap_dp(send, order[0])

    def step(self):
        if not self.known:
            return
        self.stage += 1
        k1, k2, k3 = self.order
        if self.stage < 3:
            self.keep, send = self.line(halve, self.keep, self.got)
            self.got = swap_dp(send, k2 if self.stage == 1 else k3)
        elif self.stage == 3:
            self.parts = [self.line(lambda a, b: add(BF16, a, b), self.keep, self.got)]
            self.got = swap_dp(self.parts[0], k3)
        else:
            self.parts.append(self.got)
            self.got = swap_dp(self.line(stack, *self.parts), k2 if self.stage == 4 else k1)
            if self.stage == 5:
                self.parts.append(self.got)

    def finish(self, carry=None):
        return self.line(
            lambda p, *c: place(
                p, self.info, self.order, self.first, self.rows, c[0] if c else None, self.extra_rows
            ),
            self.parts,
            *([] if carry is None else [carry]),
        )


class Rounds:
    def __init__(self, line, v, over_tensor=False):
        self.line, self.v = line, v
        self.todo = [(swap_dp, 1), (swap_dp, 2), (swap_dp, 4)]
        if lax.axis_size("dp") != 8:
            self.v = lax.psum(v.astype(F32), "dp").astype(v.dtype)
            self.todo = []
        self.cells = self.v
        if over_tensor:
            self.todo += [(swap, 1), (swap, 2)]
        self.send()

    def send(self):
        self.got = None
        if self.todo:
            self.move, k = self.todo.pop(0)
            self.got = self.move(self.v, k)

    def step(self):
        if self.got is None:
            return
        self.v = self.line(lambda a, b: add(a.dtype, a, b), self.v, self.got)
        if self.move is swap_dp:
            self.cells = self.v
        self.send()


def out_grad_kernel(chunks, dev_at, info, *refs):
    atts, y1gs, outs = refs[: chunks * SLOTS], refs[chunks * SLOTS : -SLOTS], refs[-SLOTS:]
    dev = info[dev_at]
    totals = [None] * SLOTS
    for c in range(chunks):
        for s in range(SLOTS):
            at = pl.multiple_of((s ^ dev) * BLK, BLK)
            y1g = y1gs[s][:, c * BLK : (c + 1) * BLK]
            for n in range(SLOTS):
                part = dot(atts[c * SLOTS + n][:, pl.ds(at, BLK)], y1g, NT)
                totals[n] = part if totals[n] is None else totals[n] + part
    for n in range(SLOTS):
        outs[n][...] = totals[n].astype(BF16)


def out_grad_call(info, atts, y1gs):
    rows = atts[0][0].shape[0]
    d, wide = y1gs[0].shape
    heads = [a for chunk in atts for a in chunk]
    spec = pltpu.PrefetchScalarGridSpec(
        num_scalar_prefetch=1,
        grid=(-(-d // COLUMNS),),
        in_specs=[pl.BlockSpec(a.shape, lambda i, s: (0, 0), pipeline_mode=pl.Buffered(1)) for a in heads]
        + [pl.BlockSpec((COLUMNS, wide), lambda i, s: (i, 0))] * SLOTS,
        out_specs=[pl.BlockSpec((rows, COLUMNS), lambda i, s: (0, i))] * SLOTS,
    )
    return pl.pallas_call(
        functools.partial(out_grad_kernel, len(atts), 3 * wide * SLOTS // BLK),
        grid_spec=spec,
        out_shape=[jax.ShapeDtypeStruct((rows, d), BF16)] * SLOTS,
        compiler_params=params(),
        cost_estimate=cost(9),
        name="out_grad_call",
    )(info, *heads, *y1gs)


def h1_grad_kernel(w_ref, dqkv_ref, x_ref, sum_ref, *outs):
    s = pl.program_id(1)
    first = (s == 0) & (pl.program_id(0) == 0)
    hg_s = outs[-1]
    d = x_ref.shape[0]
    pieces = cuts(d, ROWS)
    total = 0.0
    for m in pieces:
        total = total + jnp.sum(x_ref[m].astype(F32), axis=0, keepdims=True)
    mean = total * (1.0 / d)
    total = 0.0
    for m in pieces:
        center = x_ref[m].astype(F32) - mean
        total = total + jnp.sum(center * center, axis=0, keepdims=True)
    root = lax.rsqrt(total * (1.0 / d) + EPS)
    dqkv = dqkv_ref[...]
    for m in pieces:
        hg = dot(w_ref[m], dqkv)
        n = (x_ref[m].astype(F32) - mean) * root
        hg_s[m] = hg.astype(BF16)
        add_to(first, sum_ref, 0, m, fold(hg * n))
        add_to(first, sum_ref, 1, m, fold(hg))
    to_slot(s, hg_s, outs[:SLOTS])


def h1_grad_call(w, dqkv, x):
    d, total = x.shape
    per = total // (BLK * SLOTS)
    m = w.shape[1]
    at = lambda p, s: (0, p * SLOTS + s)
    mine = pl.BlockSpec((d, BLK), lambda p, s: (0, p))
    return pl.pallas_call(
        h1_grad_kernel,
        grid=(per, SLOTS),
        in_specs=[
            pl.BlockSpec((d, m), lambda p, s: (0, 0), pipeline_mode=pl.Buffered(1)),
            pl.BlockSpec((m, BLK), at),
            pl.BlockSpec((d, BLK), at),
        ],
        out_specs=[pl.BlockSpec((2, d, 128), lambda p, s: (0, 0, 0))] + [mine] * SLOTS,
        out_shape=[jax.ShapeDtypeStruct((2, d, 128), F32)]
        + [jax.ShapeDtypeStruct((d, per * BLK), BF16)] * SLOTS,
        scratch_shapes=[pltpu.VMEM((d, BLK), BF16)],
        compiler_params=params(),
        cost_estimate=cost(13),
        name="h1_grad_call",
    )(w, dqkv, x)


def input_grad_kernel(x_ref, a_ref, b_ref, c_ref, d_ref, y1g_ref, gain_ref, out_ref):
    n, root = normal(x_ref[...].astype(F32))
    total = a_ref[...].astype(F32) + b_ref[...].astype(F32) + c_ref[...].astype(F32) + d_ref[...].astype(F32)
    e = total * gain_ref[:, GAIN1 : GAIN1 + 1]
    e = root * (e - jnp.mean(e, axis=0, keepdims=True) - n * jnp.mean(e * n, axis=0, keepdims=True))
    out_ref[...] = (y1g_ref[...] + e).astype(BF16)


def input_grad_call(x, a, b, c, d4, y1g, gain):
    d, rows = x.shape
    block = pl.BlockSpec((d, BLK), lambda i: (0, i))
    return pl.pallas_call(
        input_grad_kernel,
        grid=(rows // BLK,),
        in_specs=[block] * 6 + [pl.BlockSpec(gain.shape, lambda i: (0, 0))],
        out_specs=block,
        out_shape=jax.ShapeDtypeStruct((d, rows), BF16),
        compiler_params=params(),
        cost_estimate=cost(6),
        name="input_grad_call",
    )(x, a, b, c, d4, y1g, gain)


def layer_kernel(own_ref, a_ref, b_ref, c_ref, vec_ref, out_ref):
    total = a_ref[...].astype(F32) + b_ref[...].astype(F32) + c_ref[...].astype(F32)
    out_ref[...] = (own_ref[...] + total + vec_ref[:, DOWN_BIAS : DOWN_BIAS + 1]).astype(BF16)


def layer_call(own, a, b, c, vec):
    d, rows = own.shape
    block = pl.BlockSpec((d, BLK), lambda i: (0, i))
    return pl.pallas_call(
        layer_kernel,
        grid=(rows // BLK,),
        in_specs=[block] * 4 + [pl.BlockSpec(vec.shape, lambda i: (0, 0))],
        out_specs=block,
        out_shape=jax.ShapeDtypeStruct((d, rows), BF16),
        compiler_params=params(),
        cost_estimate=cost(3),
        name="layer_call",
    )(own, a, b, c, vec)


def small_kernel(chunks, width, sum1_ref, *refs):
    sums, ups, (qkv_ref, g_ref, out_ref) = refs[:chunks], refs[chunks : 2 * chunks], refs[2 * chunks :]
    across = lambda v: jnp.sum(v, axis=1, keepdims=True)
    columns = [across(sum1_ref[0]), across(sum1_ref[1])]
    columns += [across(sum(ref[n] for ref in sums)) for n in range(3)]
    columns += [across(g_ref[...].astype(F32)), across(sum(ref[0] for ref in ups))]
    d = g_ref.shape[0]
    qv = jnp.concatenate([qkv_ref[0:width], qkv_ref[2 * width : 3 * width]], 0)
    qv = jnp.concatenate([across(qv), jnp.zeros((d - 2 * width, 1), F32)], 0)
    out_ref[...] = jnp.concatenate([v.T for v in columns + [qv]], 0)


def small_sums(sum1, sums, up_sums, qkv_sum, g):
    return pl.pallas_call(
        functools.partial(small_kernel, len(sums), qkv_sum.shape[0] // 3),
        out_shape=jax.ShapeDtypeStruct((8, g.shape[0]), F32),
        compiler_params=params(),
        cost_estimate=cost(5),
        name="small_sums",
    )(sum1, *sums, *up_sums, qkv_sum, g)


def swap(v, k):
    return lax.ppermute(v, "tensor", [(i, i ^ k) for i in range(SLOTS)])


def after(v, *done):
    return lax.optimization_barrier((v, done))[0]


class Line:
    def __init__(self):
        self.last = []

    def __call__(self, step, *args):
        args, _ = lax.optimization_barrier((args, self.last))
        out = step(*args)
        self.last = jax.tree.leaves(out)
        return out

    def wait(self, *values):
        self.last = self.last + jax.tree.leaves(values)

    def pin(self, v, *also):
        return after(v, self.last, also)


class Gather:
    def __init__(self, v):
        self.own, self.side, self.across = v, swap(v, 1), swap(v, 2)

    def finish(self, line):
        self.corner = swap(line.pin(self.across), 1)
        return self

    def all(self):
        return self.own, self.side, self.across, self.corner


def plus(a, b):
    return a.astype(F32) + b.astype(F32)


def plus_low(a, b):
    return plus(a, b).astype(BF16)


def add_kernel(*refs):
    total = None
    for ref in refs[:-1]:
        v = (ref[0] if len(ref.shape) == 3 else ref[...]).astype(F32)
        total = v if total is None else total + v
    refs[-1][...] = total.astype(refs[-1].dtype)


def add(dtype, *terms):
    rows, columns = terms[0].shape
    size = rows // 2 if rows % 32 == 0 and rows * columns > 1 << 18 else rows
    in_specs, args = [], []
    for term in terms:
        if isinstance(term, tuple):
            in_specs.append(pl.BlockSpec((1, size, columns), functools.partial(lambda at, i: (at, i, 0), term[1])))
            args.append(term[0])
        else:
            in_specs.append(pl.BlockSpec((size, columns), lambda i: (i, 0)))
            args.append(term)
    return pl.pallas_call(
        add_kernel,
        grid=(rows // size,),
        in_specs=in_specs,
        out_specs=pl.BlockSpec((size, columns), lambda i: (i, 0)),
        out_shape=jax.ShapeDtypeStruct((rows, columns), dtype),
        compiler_params=params(),
        cost_estimate=cost(2.3),
        name="add",
    )(*args)


class GroupSum:
    def __init__(self, line, parts):
        self.line, self.parts = line, parts
        self.side = swap(line.pin(parts[3]), 1)

    def step(self, wait=True):
        self.far = swap(self.line(lambda a, b: add(BF16, a, b), self.parts[2], self.side), 2)
        self.near = swap(self.line.pin(self.parts[1]), 1)
        if wait:
            self.line.wait(self.near)

    def terms(self):
        return self.parts[0], self.near, self.far


def stack_kernel(*refs):
    at = 0
    for ref in refs[:-1]:
        refs[-1][at : at + ref.shape[0]] = ref[...]
        at += ref.shape[0]


def stack(*parts):
    return pl.pallas_call(
        stack_kernel,
        out_shape=jax.ShapeDtypeStruct((sum(p.shape[0] for p in parts), parts[0].shape[1]), parts[0].dtype),
        compiler_params=params(),
        cost_estimate=cost(2),
        name="stack",
    )(*parts)


def token_starts(lengths, offsets, total, dev):
    pos = jnp.arange(total, dtype=jnp.int32)[:, None]
    inside = (pos >= offsets[None]) & (pos < (offsets + lengths)[None])
    first = jnp.max(jnp.where(inside, offsets[None], -1), axis=1)
    start = jnp.where(first >= 0, first, pos[:, 0])
    nb = total // BLK
    per = nb // SLOTS
    b = jnp.arange(nb, dtype=jnp.int32)
    first_key = start.reshape(nb, BLK)[:, 0] // BLK
    place = (b % per) * SLOTS + ((b // per) ^ dev)
    last_query = jnp.max(jnp.where(first_key[None, :] <= b[:, None], b[None, :], 0), axis=1)
    info = jnp.concatenate([first_key, place, last_query, jnp.full((1,), dev)])
    return start[None], info.astype(jnp.int32)


def body(
    tokens,
    cotangent,
    ln1_gain,
    ln1_bias,
    attn_weight,
    qv_bias,
    out_weight,
    out_bias,
    ln2_gain,
    ln2_bias,
    up_weight,
    up_bias,
    down_weight,
    down_bias,
    cell_lengths,
    cell_offsets,
):
    rows, d = tokens.shape
    width = attn_weight.shape[2]
    heads = width // HEAD_DIM
    total = rows * SLOTS
    per = rows // BLK
    dev = lax.axis_index("tensor")
    start, info = token_starts(cell_lengths[0], cell_offsets[0], total, dev)

    whole_dp = lax.axis_size("dp") == 8
    dp_info = jnp.full((1,), lax.axis_index("dp") if whole_dp else 0, jnp.int32)

    line = Line()
    x_own = tokens.T
    g_own = cotangent.T
    x_go = Gather(x_own)

    w_in = attn_weight.transpose(1, 2, 0)
    zero = jnp.zeros_like(ln1_gain)
    rows8 = jnp.stack([ln1_gain, ln1_bias, out_bias, ln2_gain, ln2_bias, up_bias, down_bias, zero])
    bias8 = jnp.zeros((8, width), F32).at[0].set(qv_bias[0]).at[2].set(qv_bias[1])
    upt, wdt, w_back, vec, bias, *g_cuts = line(
        turn, g_own, up_weight, down_weight, w_in.reshape(3 * width, d), rows8, bias8
    )
    carry = line(lambda a, b: qkv_call(0, a, b, w_in, vec, bias, None), x_own, x_go.side)
    wo_go = Gather(line.pin(out_weight, x_go.across))
    g_go = [Gather(line.pin(g_cuts[0], x_go.across))]
    x_parts = x_go.finish(line).all()
    x_all, h1, qkv, kn, vn = line(lambda a, b, c: qkv_call(1, a, b, w_in, vec, bias, c), x_parts[2], x_parts[3], carry)
    chunks = range(per)
    fronts, att_go = [], []
    for c in chunks:
        fronts.append(line(functools.partial(attend, c), info, start, qkv, kn))
        if c == 0:
            line.wait(wo_go.across, g_go[0].across)
        att_go.append(Gather(line.pin(fronts[c][0]).reshape(width, SLOTS * BLK)))
        if c == 0:
            wo_parts = wo_go.finish(line).all()
    wot = line(turn_pieces, *wo_parts)
    g_parts = [g_go[0].finish(line).all()]
    atts, ahead = [], []
    for c in chunks:
        atts.append(att_go[c].finish(line).all())
        if c > 0:
            g_parts.append(g_go[c].finish(line).all())
        if c + 1 < per:
            g_go.append(Gather(line.pin(g_cuts[c + 1], atts[c][2])))
        ahead.append(
            line(
                functools.partial(forward, c),
                info,
                atts[c],
                x_all,
                g_parts[c],
                wot,
                upt,
                down_weight,
                wdt,
                vec,
                ahead[-1][7:] if c else None,
            )
        )
    h2s, acts, pgs, gs, ns, roots, up_sums = zip(*[m[:7] for m in ahead])
    own, *layer_parts = ahead[-1][7:]
    flat = lambda a, b: list(zip(a, b))
    down_order, up_order = (1, 2, 4), (2, 1, 4)
    f = down_weight.shape[0]
    layer_sum = GroupSum(line, layer_parts)
    down = CellSum(line, *line(lambda a, b: outer(flat(a, b), dp_info, down_order), acts, gs), dp_info, down_order, f)
    layer_sum.step(False)
    up = CellSum(line, *line(lambda a, b: outer(flat(a, b), dp_info, up_order), h2s, pgs), dp_info, up_order, d)

    back, attgs = [], []
    for c in chunks:
        carry = back[-1][1 + SLOTS :] if c else None
        back.append(
            line(functools.partial(backward, c), info, pgs[c], ns[c], roots[c], g_own, up_weight, wo_parts, vec, carry)
        )
        if c:
            line.wait(attgs[-1].far, down.got, up.got)
            up.step()
        else:
            line.wait(layer_sum.far, layer_sum.near, down.got)
        down.step()
        attgs.append(GroupSum(line, back[c][1 : 1 + SLOTS]))
        attgs[c].step()
    y1g_parts = back[-1][1 + SLOTS :]
    y1g = GroupSum(line, y1g_parts)
    out_parts = line(out_grad_call, info, atts, y1g_parts)
    line.wait(attgs[-1].far, down.got, up.got, y1g.side)
    out_terms = [out_parts[0]] + [swap(line.pin(out_parts[k]), k) for k in (1, 2, 3)]
    down.step()
    up.step()
    do, stat = line(join, [a.terms() + tuple(f) for a, f in zip(attgs, fronts)])
    dqkv = line(attend_back, info, start, qkv, kn, vn, do, stat).reshape(3 * width, total)
    line.wait(down.got, up.got, out_terms)
    down.step()
    up.step()
    attn_grad, qkv_sum = line(attn_grad_call, dqkv, h1)
    line.wait(down.got, up.got)
    out_grad = line(lambda *v: add(BF16, *v), *out_terms)
    late = lax.psum((attn_grad, out_grad), "dp")
    y1g.step(False)
    sum1, *h1_parts = line(h1_grad_call, w_back, dqkv, x_all)
    line.wait(y1g.near)
    up.step()
    down.step()
    small = line(small_sums, sum1, [b[0] for b in back], up_sums, qkv_sum, g_own)
    line.wait(up.got, y1g.far)
    h1g = [h1_parts[0]] + [swap(line.pin(h1_parts[k]), k) for k in (1, 2, 3)]
    up.step()
    layer = line(layer_call, own, *layer_sum.terms(), vec)
    y1_grad = line(lambda *v: add(F32, *v), *y1g.terms())
    line.wait(down.got)
    down_grad = down.finish()
    small = Rounds(line, line.pin(small), True)
    line.wait(h1g)
    input_grad = line(input_grad_call, x_own, *h1g, y1_grad, vec)
    small.step()
    small.step()
    line.wait(up.got)
    up_grad = up.finish()
    small.step()
    small.step()
    small.step()
    line.wait(late)
    attn_grad, out_grad = (v.astype(F32) for v in line(lambda a, b: (a, b), *late))
    small, own_small = small.v, small.cells[6:]
    return (
        layer.T,
        input_grad.T,
        small[0],
        small[1],
        attn_grad.reshape(3, width, d).transpose(2, 0, 1),
        own_small[1, : 2 * width].reshape(2, width),
        out_grad,
        small[4],
        small[2],
        small[3],
        up_grad,
        own_small[0],
        down_grad,
        small[5],
    )


def solution(mesh):
    rows = P(("dp", "tensor"), None)
    in_specs = (
        rows,
        rows,
        P(),
        P(),
        P(None, None, "tensor"),
        P(None, "tensor"),
        P("tensor", None),
        P(),
        P(),
        P(),
        P(None, "tensor"),
        P("tensor"),
        P("tensor", None),
        P(),
        P("dp", None),
        P("dp", None),
    )
    out_specs = (
        rows,
        rows,
        P(),
        P(),
        P(None, None, "tensor"),
        P(None, "tensor"),
        P("tensor", None),
        P(),
        P(),
        P(),
        P(None, "tensor"),
        P("tensor"),
        P("tensor", None),
        P(),
    )
    return jax.shard_map(body, mesh=mesh, in_specs=in_specs, out_specs=out_specs, check_vma=False)
```
